32 devices in a mesh: rng: 8 (over y, x, core), xr: 4 (over z).
Axes of the slice: x: 2, y: 2, z: 4, core: 2. Of those that a mesh axis runs over, the one named last changes fastest.
Arguments:
- incident: float32 [4, 128, 512], P(None, 'rng', 'xr'), may hold values from -6 to 6
- inverse_diag: float32 [4, 128, 512], P(None, 'rng', 'xr'), may hold values from -4 to 4
- previous: float32 [4, 128, 512], P(None, 'rng', 'xr'), may hold values from -4 to 4
- heights: float32 [128, 512], P('rng', 'xr'), may hold values from -3 to 3
- neighbours: int32 [24, 128, 512], P(None, 'rng', 'xr'), may hold values from 0 to 47, as said below
- counts: int32 [128, 512], P('rng', 'xr'), may hold values from 1 to 24
- transmit: float32 [8, 2, 64], P('rng'), may hold values from 0.02 to 1
- angle_weights: float32 [2, 2, 64], replicated, may hold values from -0.15 to 0.15
Outputs:
- forward_currents: float32 [4, 128, 512], P(None, 'rng', 'xr')
- currents: float32 [4, 128, 512], P(None, 'rng', 'xr')
The draws below stay inside these ranges and needn't reach their ends.
Inputs may be any that keep to these rules, and one draw needn't show every extreme that they name: `neighbours`: the entries of one patch's list are distinct; slots at or beyond the patch's count hold entries that are not used.
All inputs are finite; a program needn't handle non-finite values.
Results may differ from the reference program's by a relative error of at most 0.0003.
Values sent between devices are 32-bit elements; how exact they have to be, the bound alone decides.
No kernel may reach another device: no remote copies, remote signals or barrier semaphores. Data moves between devices by JAX's collectives and lax.ppermute only.
A program may use at most 128 MiB of HBM per device.

```python
import math
import jax
import jax.numpy as jnp
from jax import lax

F = 2
Q = 64
H = 3
LMAX = 24
RD = 16
XD = 128
OFFSETS = 48
RANGE_BLOCKS = 8
NR = 128
NC = 512


def neighbour_tables(key):
    key = jax.random.fold_in(key, 311)
    score_key, steep_key, count_key = jax.random.split(key, 3)
    scores = jax.random.randint(score_key, (NR, NC, OFFSETS), 0, 2 ** 20) * 64 + jnp.arange(OFFSETS, dtype=jnp.int32)
    scores = scores.at[0, 0, OFFSETS - 1].set(2 ** 26 + 1).at[0, 0, 0].set(2 ** 26)
    _, picked = lax.top_k(scores, LMAX)
    offset_codes = jnp.moveaxis(picked, 2, 0)
    steep_blocks = jax.random.randint(steep_key, (NR // RD, NC // XD), 0, 8) == 0
    steep_blocks = steep_blocks.at[0, 0].set(True)
    cap_blocks = jnp.where(steep_blocks, LMAX, LMAX // 4)
    cap_cells = jnp.repeat(jnp.repeat(cap_blocks, RD, axis=0), XD, axis=1)
    slot_counts = jax.random.randint(count_key, (NR, NC), 1, cap_cells + 1).at[0, 0].set(LMAX)
    return (offset_codes.astype(jnp.int32), slot_counts.astype(jnp.int32))


def draw_neighbours(key, part):
    return neighbour_tables(key)[0]


def draw_counts(key, part):
    return neighbour_tables(key)[1]


def draw_heights(key, part):
    key = jax.random.fold_in(key, 701)
    level_key = jax.random.fold_in(key, 1)
    terrain = jax.random.uniform(level_key, (NR, NC), minval=-3.0, maxval=3.0)
    return terrain.astype(jnp.float32)


def draw_transmit(key, part):
    key = jax.random.fold_in(key, 523)
    selection_key, gradual_random_key, quick_random_key, spike_random_key, depth_random_key = jax.random.split(key, 5)
    slow_share = 0.5
    lasting = jax.random.uniform(selection_key, (1, F, Q)) < slow_share
    spreads = jax.random.uniform(gradual_random_key, (RANGE_BLOCKS, F, Q), minval=0.5, maxval=1.5)
    slow_rates = jnp.power(0.1, spreads / (2.0 * RANGE_BLOCKS))
    fast_rates = jax.random.uniform(quick_random_key, (RANGE_BLOCKS, F, Q), minval=0.02, maxval=0.1)
    spike_rows = jax.random.randint(spike_random_key, (3,), 0, RANGE_BLOCKS)
    spiking_active = jnp.any(jnp.arange(RANGE_BLOCKS)[:, None] == spike_rows[None, :], axis=1)[:, None, None]
    depths = jax.random.uniform(depth_random_key, (RANGE_BLOCKS, F, Q), minval=0.5, maxval=0.8)
    slow_rates = jnp.where(spiking_active, slow_rates * depths, slow_rates)
    return jnp.where(lasting, slow_rates, fast_rates).astype(jnp.float32)


def steps_of(stream_key, extent, cuts, low, largest):
    loudness, own = 1.0, jax.random.fold_in(stream_key, 6)
    for axis_at, shards_of in cuts:
        steps = jnp.exp(jax.random.uniform(jax.random.fold_in(own, axis_at), (shards_of,), jnp.float32, low / len(cuts), largest / len(cuts)))
        loudness = loudness * jnp.repeat(steps, extent[axis_at] // shards_of).reshape([-1 if axis == axis_at else 1 for axis in range(len(extent))])
    return loudness


def bell_draw(own_key, dims, scale, most, shards=(), kind=jnp.bfloat16):
    values = jax.random.normal(own_key, dims, jnp.float32) * scale
    if len(shards) > 0:
        values = steps_of(own_key, dims, shards, -0.22, 0.18) * values
    return jnp.clip(values, min=-most, max=most).astype(kind)


def setup_inputs(seed: int = 0) -> dict:
    splits = jax.random.split(jax.random.key(seed), 9)
    incident = bell_draw(splits[0], (2 * F, NR, NC), 1.0, 6.0, ((1, 8), (2, 4)), jnp.float32)
    inverse_diag = bell_draw(splits[1], (2 * F, NR, NC), 0.7, 4.0, ((1, 8), (2, 4)), jnp.float32)
    previous = bell_draw(splits[2], (2 * F, NR, NC), 0.5, 4.0, ((1, 8), (2, 4)), jnp.float32)
    heights = draw_heights(jax.random.fold_in(splits[8], 71), 0)
    neighbours = draw_neighbours(jax.random.fold_in(splits[8], 71), 0)
    counts = draw_counts(jax.random.fold_in(splits[8], 71), 0)
    transmit = draw_transmit(jax.random.fold_in(splits[8], 71), 0)
    angle_weights = bell_draw(splits[7], (F, 2, Q), 0.03, 0.15, (), jnp.float32)
    return dict(incident=incident, inverse_diag=inverse_diag, previous=previous, heights=heights, neighbours=neighbours, counts=counts, transmit=transmit, angle_weights=angle_weights)


green_scale = 0.25
phase_period = 64
highest_precision = lax.Precision.HIGHEST

def wave_tables(frequency, direction, row_ids, col_ids, block_heights):
    angle_ids = jnp.arange(Q, dtype=jnp.int32)
    range_step = direction * (1 + angle_ids // 8 + 2 * frequency)
    cross_step = angle_ids % 8 - 4 + frequency
    height_lift = 0.3 + 0.2 * frequency + 0.03 * angle_ids.astype(jnp.float32)
    phase_turns = (range_step[:, None, None] * row_ids[None, :, None] + cross_step[:, None, None] * col_ids[None, None, :]) % phase_period
    phase_angle = phase_turns.astype(jnp.float32) * (2.0 * math.pi / phase_period) + height_lift[:, None, None] * block_heights[None]
    return (jnp.cos(phase_angle), jnp.sin(phase_angle))

def decode_offsets(offset_codes):
    full_code = offset_codes + (offset_codes >= OFFSETS // 2).astype(jnp.int32)
    return (full_code // (2 * H + 1) - H, full_code % (2 * H + 1) - H)

def green_terms(distance, weight_live):
    pieces = []
    for frequency in range(F):
        wavenum = 0.5 * math.pi * (1.0 + 0.25 * frequency)
        magnitude = weight_live * green_scale / distance
        pieces.append(magnitude * jnp.cos(wavenum * distance))
        pieces.append(magnitude * jnp.sin(wavenum * distance))
    return jnp.stack(pieces)

def complex_apply(coupling, values):
    pieces = []
    for frequency in range(F):
        real_c = coupling[2 * frequency]
        imag_c = coupling[2 * frequency + 1]
        real_v = values[2 * frequency]
        imag_v = values[2 * frequency + 1]
        pieces.append(real_c * real_v - imag_c * imag_v)
        pieces.append(real_c * imag_v + imag_c * real_v)
    return jnp.stack(pieces)

def near_field(field, heights, neighbours, counts):
    width_pad = NC + 2 * H
    padded_field = jnp.pad(field, ((0, 0), (H, H), (H, H))).reshape(2 * F, -1)
    padded_heights = jnp.pad(heights, H).reshape(-1)
    anchor = ((jnp.arange(NR, dtype=jnp.int32)[:, None] + H) * width_pad + jnp.arange(NC, dtype=jnp.int32)[None, :] + H).astype(jnp.int32)

    def add_slot(running, slot_data):
        slot_codes, slot_index = slot_data
        shift_rows, shift_cols = decode_offsets(slot_codes)
        source_ids = (anchor + shift_rows * width_pad + shift_cols).astype(jnp.int32)
        other_heights = jnp.take(padded_heights, source_ids)
        distance = jnp.sqrt((shift_rows * shift_rows + shift_cols * shift_cols).astype(jnp.float32) + (other_heights - heights) ** 2)
        live_slot = (slot_index < counts).astype(jnp.float32)
        coupling = green_terms(distance, live_slot)
        gathered = jnp.take(padded_field, source_ids, axis=1)
        return (running + complex_apply(coupling, gathered), None)
    start_total = jnp.zeros((2 * F, NR, NC), jnp.float32)
    slot_indices = jnp.arange(LMAX, dtype=jnp.int32)
    total_field, _ = lax.scan(add_slot, start_total, (neighbours, slot_indices))
    return total_field

def reference(incident, inverse_diag, previous, heights, neighbours, counts, transmit, angle_weights):
    spread = 1.0 / math.sqrt(RD * NC)
    col_ids = jnp.arange(NC, dtype=jnp.int32)
    block_ids = jnp.arange(RANGE_BLOCKS, dtype=jnp.int32)

    def by_block(array):
        return jnp.moveaxis(array.reshape(array.shape[0], RANGE_BLOCKS, RD, NC), 1, 0)

    def unblock(array):
        return jnp.moveaxis(array, 0, 1).reshape(2 * F, NR, NC)
    height_blocks = heights.reshape(RANGE_BLOCKS, RD, NC)

    def weak_field(frequency, direction, row_ids, block_heights, carried):
        cos_wave, sin_wave = wave_tables(frequency, direction, row_ids, col_ids, block_heights)
        real_w = angle_weights[frequency, 0]
        imag_w = angle_weights[frequency, 1]
        real_s = carried[frequency, 0]
        imag_s = carried[frequency, 1]
        amp_real = real_w * real_s - imag_w * imag_s
        amp_imag = real_w * imag_s + imag_w * real_s
        field_real = spread * (jnp.einsum('a,arc->rc', amp_real, cos_wave, precision=highest_precision) - jnp.einsum('a,arc->rc', amp_imag, sin_wave, precision=highest_precision))
        field_imag = spread * (jnp.einsum('a,arc->rc', amp_real, sin_wave, precision=highest_precision) + jnp.einsum('a,arc->rc', amp_imag, cos_wave, precision=highest_precision))
        return (cos_wave, sin_wave, field_real, field_imag)

    def gather_back(cos_wave, sin_wave, flow_real, flow_imag):
        gain_real = jnp.einsum('arc,rc->a', cos_wave, flow_real, precision=highest_precision) + jnp.einsum('arc,rc->a', sin_wave, flow_imag, precision=highest_precision)
        gain_imag = jnp.einsum('arc,rc->a', cos_wave, flow_imag, precision=highest_precision) - jnp.einsum('arc,rc->a', sin_wave, flow_real, precision=highest_precision)
        return jnp.stack([gain_real, gain_imag])
    near_old = near_field(previous, heights, neighbours, counts)

    def forward_step(carried, block_data):
        block_id, fed_block, inverse_block, near_block, block_heights, decay = block_data
        row_ids = (block_id * RD + jnp.arange(RD, dtype=jnp.int32)).astype(jnp.int32)
        flows = []
        weak_parts = []
        renewed = []
        for frequency in range(F):
            cos_wave, sin_wave, field_real, field_imag = weak_field(frequency, 1, row_ids, block_heights, carried)
            rest_real = fed_block[2 * frequency] - near_block[2 * frequency] - field_real
            rest_imag = fed_block[2 * frequency + 1] - near_block[2 * frequency + 1] - field_imag
            inv_real = inverse_block[2 * frequency]
            inv_imag = inverse_block[2 * frequency + 1]
            flow_real = inv_real * rest_real - inv_imag * rest_imag
            flow_imag = inv_real * rest_imag + inv_imag * rest_real
            gained = gather_back(cos_wave, sin_wave, flow_real, flow_imag)
            renewed.append(decay[frequency] * (carried[frequency] + gained))
            flows += [flow_real, flow_imag]
            weak_parts += [field_real, field_imag]
        return (jnp.stack(renewed), (jnp.stack(flows), jnp.stack(weak_parts)))
    start_carry = jnp.zeros((F, 2, Q), jnp.float32)
    _, (forward_blocks, weak_blocks) = lax.scan(forward_step, start_carry, (block_ids, by_block(incident), by_block(inverse_diag), by_block(near_old), height_blocks, transmit))
    forward_currents = unblock(forward_blocks)
    near_new = near_field(forward_currents, heights, neighbours, counts)

    def backward_step(carried, block_data):
        block_id, fed_block, inverse_block, near_block, block_heights, decay, weak_block = block_data
        row_ids = (block_id * RD + jnp.arange(RD, dtype=jnp.int32)).astype(jnp.int32)
        flows = []
        renewed = []
        for frequency in range(F):
            inv_real = inverse_block[2 * frequency]
            inv_imag = inverse_block[2 * frequency + 1]
            rest_real = fed_block[2 * frequency] - near_block[2 * frequency] - weak_block[2 * frequency]
            rest_imag = fed_block[2 * frequency + 1] - near_block[2 * frequency + 1] - weak_block[2 * frequency + 1]
            driven_real = inv_real * rest_real - inv_imag * rest_imag
            driven_imag = inv_real * rest_imag + inv_imag * rest_real
            cos_wave, sin_wave, field_real, field_imag = weak_field(frequency, -1, row_ids, block_heights, carried)
            flow_real = driven_real - (inv_real * field_real - inv_imag * field_imag)
            flow_imag = driven_imag - (inv_real * field_imag + inv_imag * field_real)
            gained = gather_back(cos_wave, sin_wave, flow_real, flow_imag)
            renewed.append(decay[frequency] * (carried[frequency] + gained))
            flows += [flow_real, flow_imag]
        return (jnp.stack(renewed), jnp.stack(flows))
    _, backward_blocks = lax.scan(backward_step, start_carry, (block_ids, by_block(incident), by_block(inverse_diag), by_block(near_new), height_blocks, transmit, weak_blocks), reverse=True)
    currents = unblock(backward_blocks)
    return (forward_currents, currents)
```

```python
import functools
import math

import jax
import jax.numpy as jnp
from jax import lax
from jax.experimental import pallas as pl
from jax.experimental.pallas import tpu as pltpu
from jax.sharding import PartitionSpec as P

F = 2
Q = 64
H = 3
LMAX = 24
OFFSETS = 48
SUB = 8
LANES = 128
PERIOD = 64
TOP = SUB
GREEN = 0.25
TURN = 2.0 * math.pi
SLOT = 24
HIGHEST = lax.Precision.HIGHEST
BOTH = ("rng", "xr")
f32 = jnp.float32


def iota(shape, dim):
    return lax.broadcasted_iota(jnp.int32, shape, dim)


def roll(x, shift, axis=1):
    shift = shift % x.shape[axis]
    return x if shift == 0 else pltpu.roll(x, shift, axis)


def cos_sin(turns):
    quarter = jnp.floor(4.0 * turns + 0.5)
    rest = turns - 0.25 * quarter
    which = quarter.astype(jnp.int32)
    sq = rest * rest
    s = rest * (TURN + sq * (-(TURN**3) / 6 + sq * (TURN**5 / 120 + sq * (-(TURN**7) / 5040 + sq * (TURN**9 / 362880)))))
    c = 1.0 + sq * (-(TURN**2) / 2 + sq * (TURN**4 / 24 + sq * (-(TURN**6) / 720 + sq * (TURN**8 / 40320))))
    odd = (which & 1) == 1
    cos = jnp.where(odd, s, c)
    sin = jnp.where(odd, c, s)
    cos = jnp.where(((which + 1) & 2) == 2, -cos, cos)
    sin = jnp.where((which & 2) == 2, -sin, sin)
    return cos, sin


def times(a, b):
    return a[0] * b[0] - a[1] * b[1], a[0] * b[1] + a[1] * b[0]


def conj_times(a, b):
    return a[0] * b[0] + a[1] * b[1], a[0] * b[1] - a[1] * b[0]


def wave(step_x, x, step_y, y, lift, heights):
    phase = (step_x * x + step_y * y) & (PERIOD - 1)
    return cos_sin(phase.astype(f32) * (1.0 / PERIOD) + (lift / TURN) * heights)


def offset_of(code):
    full = code + (1 if code >= OFFSETS // 2 else 0)
    return full // (2 * H + 1) - H, full % (2 * H + 1) - H


def vmem():
    return pl.BlockSpec(memory_space=pltpu.VMEM)


def smem():
    return pl.BlockSpec(memory_space=pltpu.SMEM)


def call(body, out, n_in, scratch=(), flops=2_000_000):
    return pl.pallas_call(
        body,
        out_shape=tuple(jax.ShapeDtypeStruct(s, f32) for s in out),
        in_specs=[smem()] + [vmem()] * n_in,
        out_specs=tuple(vmem() for _ in out),
        scratch_shapes=list(scratch),
        compiler_params=pltpu.CompilerParams(vmem_limit_bytes=48 * 1024 * 1024),
        cost_estimate=pl.CostEstimate(flops=flops, bytes_accessed=1 << 20, transcendentals=0),
    )


def pack_columns(fields, right):
    rows = fields[0].shape[0]
    lane = iota((rows, LANES), 1)
    packed = jnp.zeros((rows, LANES), f32)
    for k, field in enumerate(fields):
        moved = roll(field, H * k - (LANES - H) if right else H * k)
        packed = jnp.where((lane >= H * k) & (lane < H * (k + 1)), moved, packed)
    return packed


def unpack_columns(from_left, from_right, k):
    lane = iota(from_left.shape, 1)
    left = jnp.where(lane >= LANES - H, roll(from_left, LANES - H - H * k), 0.0)
    return jnp.where(lane < H, roll(from_right, -H * k), left)


def shifted(inner, edge, dy):
    if dy == 0:
        return inner
    lane = iota(inner.shape, 1)
    outside = lane >= LANES - dy if dy > 0 else lane < -dy
    return jnp.where(outside, roll(edge, -dy), roll(inner, -dy))


def columns_body(place, prev, heights, inverse, send_a, send_b):
    fields = [prev[k] for k in range(2 * F)] + [heights[...]] + [inverse[k] for k in range(2 * F)]
    right = pack_columns(fields, True)
    left = pack_columns(fields, False)
    even = (place[1] & 1) == 0
    send_a[...] = jnp.where(even, right, left)
    send_b[...] = jnp.where(even, left, right)


N_FIELDS = 4 * F + 1
ROWS_SENT = 40


def rows_body(place, prev, heights, inverse, recv_a, recv_b, send_a, send_b):
    even_c = (place[1] & 1) == 0
    even_r = (place[0] & 1) == 0
    rows = heights.shape[0]
    fields = [prev[k] for k in range(2 * F)] + [heights[...]] + [inverse[k] for k in range(2 * F)]
    fields.append(jnp.where(even_c, recv_b[...], recv_a[...]))
    fields.append(jnp.where(even_c, recv_a[...], recv_b[...]))
    for k, field in enumerate(fields):
        last, first = field[rows - H :], field[:H]
        send_a[H * k : H * (k + 1)] = jnp.where(even_r, last, first)
        send_b[H * k : H * (k + 1)] = jnp.where(even_r, first, last)
    used = H * len(fields)
    send_a[used:] = jnp.zeros((ROWS_SENT - used, LANES), f32)
    send_b[used:] = jnp.zeros((ROWS_SENT - used, LANES), f32)


def tables_body(place, heights, inverse, weights_unused, tables, gens, left_mat, right_mat):
    rows = heights.shape[0]
    x0 = place[0] * rows
    y0 = place[1] * LANES
    angle = iota((2 * SUB, LANES), 0) - SUB
    y = iota((2 * SUB, LANES), 1) + y0
    for i in range(rows):
        h = heights[i : i + 1, :]
        x = jnp.full((2 * SUB, LANES), x0 + i, jnp.int32)
        lanes = pl.ds(i * LANES, LANES)
        h2 = jnp.broadcast_to(h, (2 * SUB, LANES)) * angle.astype(f32)
        c2, s2 = wave(0, x, angle, y, 0.03, h2)
        tables[4, i] = c2[SUB:]
        tables[5, i] = s2[SUB:]
        right_mat[0 : 2 * SUB, lanes] = c2
        right_mat[2 * SUB : 4 * SUB, lanes] = s2
        for direction in range(2):
            c1, s1 = wave(angle * (1 - 2 * direction), x, 0, y, 0.24, h2)
            tables[2 * direction, i] = c1[SUB:]
            tables[2 * direction + 1, i] = s1[SUB:]
            for f in range(F):
                zr = inverse[2 * f, i : i + 1, :]
                zi = inverse[2 * f + 1, i : i + 1, :]
                base = (direction * F + f) * 4 * SUB
                left_mat[base : base + 2 * SUB, lanes] = zr * c1 - zi * s1
                left_mat[base + 2 * SUB : base + 4 * SUB, lanes] = zr * s1 + zi * c1
    both = lax.dot_general(
        left_mat[...], right_mat[...], (((1,), (1,)), ((), ())), precision=HIGHEST, preferred_element_type=f32
    )
    lane = iota((SUB, LANES), 1)
    for direction in range(2):
        for f in range(F):
            base = (direction * F + f) * 4 * SUB
            for half in range(2):
                p = both[base + half * SUB : base + (half + 1) * SUB]
                q = both[base + (2 + half) * SUB : base + (3 + half) * SUB]
                for part in range(2):
                    if part == 0:
                        g = p - roll(q, -2 * SUB)
                    else:
                        g = roll(p, -2 * SUB) + q
                    g = jnp.where(lane < 2 * SUB, g, 0.0)
                    g = pltpu.roll(g, 0, 1, stride=2 * SUB, stride_axis=0)
                    row = jnp.sum(g, axis=0, keepdims=True)
                    at = direction * SUB + f * 4 + part * 2 + (1 - half)
                    gens[at : at + 1] = row


def project(left_mat, right_mat, tables, first, cs, rows, f_out):
    for i in range(rows):
        lanes = pl.ds(i * LANES, LANES)
        right_mat[0:SUB, lanes] = tables[4, i]
        right_mat[SUB : 2 * SUB, lanes] = tables[5, i]
        c1, s1 = tables[first, i], tables[first + 1, i]
        for f in range(F):
            re, im = conj_times((c1, s1), (cs[2 * f, i : i + 1, :], cs[2 * f + 1, i : i + 1, :]))
            left_mat[2 * f * SUB : (2 * f + 1) * SUB, lanes] = re
            left_mat[(2 * f + 1) * SUB : (2 * f + 2) * SUB, lanes] = im
    sums = lax.dot_general(
        left_mat[0 : 4 * SUB], right_mat[...], (((1,), (1,)), ((), ())), precision=HIGHEST, preferred_element_type=f32
    )
    lane = iota((SUB, LANES), 1)
    for f in range(F):
        gr = sums[2 * f * SUB : (2 * f + 1) * SUB]
        gi = sums[(2 * f + 1) * SUB : (2 * f + 2) * SUB]
        re = gr + roll(gi, -SUB)
        im = gi - roll(gr, -SUB)
        packed = jnp.where(lane < SUB, re, jnp.where(lane < 2 * SUB, roll(im, SUB), 0.0))
        packed = pltpu.roll(packed, 0, 1, stride=2 * SUB, stride_axis=0)
        f_out(f, jnp.sum(packed, axis=0, keepdims=True))


def carrier(f, direction, x, y, heights):
    sign = 1 - 2 * direction
    return wave(sign * (1 + 2 * f), x, f - 4, y, 0.3 + 0.2 * f, heights)


def place_ids(place, rows, cols, first_row, first_col, own_rows):
    x = place[0] * own_rows + first_row + iota((rows, cols), 0)
    y = place[1] * LANES + first_col + iota((rows, cols), 1)
    return x, y


def near_body(
    n_r, n_c, place, prev, heights, inverse, incident, neighbours, counts, transmit, cols_a, cols_b, rows_a, rows_b,
    gens, tables, payload, green, source, ext, inner, edge, edge_l, edge_r, moved, cs, left_mat, right_mat, common,
):
    rows = heights.shape[0]
    d, c = place[0], place[1]
    even_c = (c & 1) == 0
    even_r = (d & 1) == 0
    below = jnp.where(even_r, rows_a[...], rows_b[...])
    above = jnp.where(even_r, rows_b[...], rows_a[...])
    edge_l[...] = jnp.zeros(edge_l.shape, f32)
    edge_r[...] = jnp.zeros(edge_r.shape, f32)
    edge_l[TOP : TOP + rows] = jnp.where(even_c, cols_b[...], cols_a[...])
    edge_r[TOP : TOP + rows] = jnp.where(even_c, cols_a[...], cols_b[...])
    at = H * N_FIELDS
    edge_l[TOP - H : TOP] = above[at : at + H]
    edge_l[TOP + rows : TOP + rows + H] = below[at : at + H]
    edge_r[TOP - H : TOP] = above[at + H : at + 2 * H]
    edge_r[TOP + rows : TOP + rows + H] = below[at + H : at + 2 * H]
    fields = [prev[k] for k in range(2 * F)] + [heights[...]] + [inverse[k] for k in range(2 * F)]
    from_left, from_right = edge_l[...], edge_r[...]
    for k, field in enumerate(fields):
        inner[k] = jnp.zeros(inner.shape[1:], f32)
        inner[k, TOP : TOP + rows] = field
        inner[k, TOP - H : TOP] = above[H * k : H * (k + 1)]
        inner[k, TOP + rows : TOP + rows + H] = below[H * k : H * (k + 1)]
        side = unpack_columns(from_left, from_right, k)
        if k >= 2 * F:
            ext[2 * (k - 2 * F)] = inner[k]
            ext[2 * (k - 2 * F) + 1] = side
        if k <= 2 * F:
            middle = inner[k]
            for dy in range(-H, H + 1):
                moved[k * (2 * H + 1) + dy + H] = shifted(middle, side, dy)
    h = heights[...]
    count = counts[...]
    low = jnp.zeros(count.shape, jnp.int32)
    high = jnp.zeros(count.shape, jnp.int32)
    half = OFFSETS // 2
    one = jnp.ones(count.shape, jnp.int32)
    for slot in range(LMAX):
        code = neighbours[slot]
        live = count > slot
        is_low = code < half
        bit = lax.shift_left(one, jnp.where(is_low, code, code - half))
        low = low | jnp.where(live & is_low, bit, 0)
        high = high | jnp.where(live & (code >= half), bit, 0)
    near = [jnp.zeros((rows, LANES), f32) for _ in range(2 * F)]
    for code in range(OFFSETS):
        dx, dy = offset_of(code)
        window = lambda k: moved[k * (2 * H + 1) + dy + H, TOP + dx : TOP + dx + rows]
        lift = window(2 * F) - h
        squared = float(dx * dx + dy * dy) + lift * lift
        inverse_r = lax.rsqrt(squared)
        r = squared * inverse_r
        bits = low if code < half else high
        there = (bits & (1 << (code % half))) != 0
        size = jnp.where(there, GREEN * inverse_r, 0.0)
        for f in range(F):
            cos, sin = cos_sin(r * (0.25 * (1.0 + 0.25 * f)))
            g = (size * cos, size * sin)
            green[4 * code + 2 * f] = g[0]
            green[4 * code + 2 * f + 1] = g[1]
            got = times(g, (window(2 * f), window(2 * f + 1)))
            near[2 * f] += got[0]
            near[2 * f + 1] += got[1]
    x, y = place_ids(place, rows, LANES, 0, 0, rows)
    sources = []
    for f in range(F):
        z = (inverse[2 * f], inverse[2 * f + 1])
        s = times(z, (incident[2 * f] - near[2 * f], incident[2 * f + 1] - near[2 * f + 1]))
        sources += s
        source[2 * f] = s[0]
        source[2 * f + 1] = s[1]
        got = conj_times(carrier(f, 0, x, y, h), s)
        cs[2 * f] = got[0]
        cs[2 * f + 1] = got[1]

    def keep(f, row):
        common[2 * SUB + f : 2 * SUB + f + 1] = row

    right_mat[2 * SUB :] = jnp.zeros((right_mat.shape[0] - 2 * SUB, right_mat.shape[1]), f32)
    project(left_mat, right_mat, tables, 0, cs, rows, keep)
    common[0 : 2 * SUB] = gens[...]
    common[2 * SUB + 2 : 2 * SUB + 3] = transmit[...]
    tail = common[2 * SUB : 3 * SUB]
    for direction in range(2):
        part = common[direction * SUB : (direction + 1) * SUB]

        def fill(s, _, part=part, tail=tail):
            payload[s, 0:SUB] = part
            payload[s, SUB : 2 * SUB] = tail
            return 0

        if direction == 0:
            lax.fori_loop(d * n_c, n_r * n_c, fill, 0)
        else:
            lax.fori_loop(0, d * n_c, fill, 0)
    lasts = pack_columns(sources, True)
    firsts = pack_columns(sources, False)
    at = 2 * SUB - 4

    def send(dr, dc, put):
        dst = (d + dr) * n_c + c + dc
        ok = (d + dr >= 0) & (d + dr < n_r) & (c + dc >= 0) & (c + dc < n_c)

        @pl.when(ok)
        def _():
            put(dst)

    def rows_to(dr):
        def put(dst):
            for k in range(2 * F):
                s = sources[k]
                payload[dst, at + H * k : at + H * (k + 1)] = s[rows - H :] if dr > 0 else s[:H]

        return put

    def cols_to(dc):
        packed = lasts if dc > 0 else firsts

        def put(dst):
            payload[dst, at : at + SUB] = packed[:SUB] + roll(packed[SUB:], LANES // 2)

        return put

    def corner_to(dr, dc):
        packed = lasts if dc > 0 else firsts

        def put(dst):
            payload[dst, at : at + H] = packed[rows - H :] if dr > 0 else packed[:H]

        return put

    for dr in (-1, 1):
        send(dr, 0, rows_to(dr))
        send(0, dr, cols_to(dr))
        for dc in (-1, 1):
            send(dr, dc, corner_to(dr, dc))


def toeplitz(gen, sub, lane):
    first = jnp.broadcast_to(gen[0:1], (SUB, LANES))
    second = jnp.broadcast_to(gen[1:2], (SUB, LANES))
    tiles = []
    for a1 in range(Q // SUB):
        by = 2 * SUB * a1 - SUB
        inside = (lane >= by + sub) & (lane < by + sub + LANES)
        one = pltpu.roll(first, by % LANES, 1, stride=1, stride_axis=0)
        two = pltpu.roll(second, by % LANES, 1, stride=1, stride_axis=0)
        tiles.append(jnp.where(inside, one, two))
    return tiles


def to_column(row, sub, lane):
    return [
        jnp.sum(jnp.where(lane == 2 * SUB * a1 + sub, row, 0.0), axis=1, keepdims=True) for a1 in range(Q // SUB)
    ]


def to_row(columns, sub, lane):
    total = jnp.zeros((SUB, LANES), f32)
    for a1, column in enumerate(columns):
        total = jnp.where(lane == 2 * SUB * a1 + sub, column, total)
    return jnp.broadcast_to(jnp.sum(total, axis=0, keepdims=True), (SUB, LANES))


def sweep_step(gens, feeds, share, weights, carry, spread):
    sub = iota((SUB, LANES), 0)
    lane = iota((SUB, LANES), 1)
    wide = lambda row: jnp.broadcast_to(row, (SUB, LANES))
    low = (lane & SUB) == 0
    out = []
    for f in range(F):
        amp = times((wide(weights[2 * f]), wide(weights[2 * f + 1])), carry[f])
        re = toeplitz(gens[4 * f : 4 * f + 2], sub, lane)
        im = toeplitz(gens[4 * f + 2 : 4 * f + 4], sub, lane)
        col_r, col_i = [], []
        for kr, ki in zip(re, im, strict=True):
            got = times((kr, ki), amp)
            col_r.append(jnp.sum(got[0], axis=1, keepdims=True))
            col_i.append(jnp.sum(got[1], axis=1, keepdims=True))
        feed = wide(feeds[f : f + 1])
        t = wide(share)
        if f == 1:
            t = roll(t, -SUB)
        t = jnp.where(low, t, 0.0)
        out.append(
            (
                t * (carry[f][0] + feed - spread * to_row(col_r, sub, lane)),
                t * (carry[f][1] + roll(feed, -SUB) - spread * to_row(col_i, sub, lane)),
            )
        )
    return out


def amplitudes(weights, carry, spread):
    sub = iota((SUB, LANES), 0)
    lane = iota((SUB, LANES), 1)
    out = []
    for f in range(F):
        amp = times((weights[2 * f], weights[2 * f + 1]), carry[f])
        out.append([to_column(spread * part, sub, lane) for part in amp])
    return out


def powers(base, count):
    out = [None, base]
    for _ in range(2, count):
        out.append(times(out[-1], base))
    return out


def radiate(amp, f, splat, direction, x, y, heights):
    u1 = powers(wave(1 - 2 * direction, x, 0, y, 0.24, heights), Q // SUB)
    u2 = powers(wave(0, x, 1, y, 0.03, heights), SUB)
    return u1, u2


def radiated(f, splat, u1, u2, carried):
    total = None
    for a1 in range(Q // SUB):
        ar, ai = splat(f, 0, SUB * a1), splat(f, 1, SUB * a1)
        inner = (ar, ai)
        for a2 in range(1, SUB):
            got = times((splat(f, 0, SUB * a1 + a2), splat(f, 1, SUB * a1 + a2)), u2[a2])
            inner = (inner[0] + got[0], inner[1] + got[1])
        if a1 == 0:
            total = inner
        else:
            got = times(u1[a1], inner)
            total = (total[0] + got[0], total[1] + got[1])
    return times(carried, total)


def sums_of(recv, at, n_c):
    total = recv[at, 0 : 2 * SUB]
    for k in range(1, n_c):
        total = total + recv[at + k, 0 : 2 * SUB]
    return total


def new_body(
    n_r, n_c, spread, place, recv, green, source, ext, heights, inverse, incident, tables, weights,
    forward, driven, payload, carries, amps, inner, moved, edge_l, edge_r, cs, left_mat, right_mat, common,
):
    rows = heights.shape[0]
    d, c = place[0], place[1]
    wts = [weights[k : k + 1] for k in range(2 * F)]
    zero = jnp.zeros((SUB, LANES), f32)
    for k in range(2 * F):
        carries[0, k] = zero

    def lap(j, carry):
        sums = sums_of(recv, j * n_c, n_c)
        share = recv[j * n_c, SUB + 2 : SUB + 3]
        new = sweep_step(sums[:SUB], sums[SUB : SUB + 2], share, wts, [(carry[0], carry[1]), (carry[2], carry[3])], spread)
        flat = (new[0][0], new[0][1], new[1][0], new[1][1])
        for k in range(2 * F):
            carries[j + 1, k] = flat[k]
        return flat

    lax.fori_loop(0, jnp.minimum(d + 1, n_r - 1), lap, (zero,) * (2 * F))
    for which in range(3):
        at = jnp.clip(d + which - 1, 0, n_r - 1)
        carry = [(carries[at, 2 * f], carries[at, 2 * f + 1]) for f in range(F)]
        for f, parts in enumerate(amplitudes(wts, carry, spread)):
            for part, columns in enumerate(parts):
                for a1, column in enumerate(columns):
                    amps[which, 2 * f + part, SUB * a1 : SUB * (a1 + 1)] = jnp.broadcast_to(column, (SUB, LANES))

    at = 2 * SUB - 4

    def got(dr, dc, start, size):
        src = jnp.clip(d + dr, 0, n_r - 1) * n_c + jnp.clip(c + dc, 0, n_c - 1)
        ok = (d + dr >= 0) & (d + dr < n_r) & (c + dc >= 0) & (c + dc < n_c)
        return jnp.where(ok, recv[src, start : start + size], 0.0)

    edge_l[...] = jnp.zeros(edge_l.shape, f32)
    edge_r[...] = jnp.zeros(edge_r.shape, f32)
    for edge, dc in ((edge_l, -1), (edge_r, 1)):
        side = got(0, dc, at, SUB)
        edge[TOP : TOP + SUB] = side
        edge[TOP + SUB : TOP + rows] = roll(side, -(LANES // 2))
        edge[TOP - H : TOP] = got(-1, dc, at, H)
        edge[TOP + rows : TOP + rows + H] = got(1, dc, at, H)
    from_left, from_right = edge_l[...], edge_r[...]
    for k in range(2 * F):
        inner[k] = jnp.zeros(inner.shape[1:], f32)
        inner[k, TOP : TOP + rows] = source[k]
        inner[k, TOP - H : TOP] = got(-1, 0, at + H * k, H)
        inner[k, TOP + rows : TOP + rows + H] = got(1, 0, at + H * k, H)
    sides = [unpack_columns(from_left, from_right, k) for k in range(2 * F)]

    weak = {}
    tiles = (rows + 2 * SUB) // SUB
    for tile in range(tiles):
        which = 0 if tile == 0 else 2 if tile == tiles - 1 else 1
        splat = lambda f, part, a, which=which: amps[which, 2 * f + part, a : a + 1]
        rows_at = slice(SUB * tile, SUB * (tile + 1))
        for side in range(2):
            x, y = place_ids(place, SUB, LANES, SUB * tile - TOP, 0, rows)
            if side == 1:
                lane = iota((SUB, LANES), 1)
                y = y + jnp.where(lane < LANES // 2, LANES, -LANES)
            h = ext[side, rows_at]
            u1, u2 = radiate(None, 0, None, 0, x, y, h)
            for f in range(F):
                w = radiated(f, splat, u1, u2, carrier(f, 0, x, y, h))
                z = (ext[2 * (1 + 2 * f) + side, rows_at], ext[2 * (2 + 2 * f) + side, rows_at])
                lost = times(z, w)
                for part in range(2):
                    k = 2 * f + part
                    if side == 0:
                        inner[k, rows_at] = inner[k, rows_at] - lost[part]
                        weak[tile, k] = w[part]
                    else:
                        sides[k] = (sides[k] if isinstance(sides[k], list) else [sides[k]]) + [
                            sides_tile(sides[k], rows_at) - lost[part]
                        ]
    for k in range(2 * F):
        side = jnp.concatenate(sides[k][1:], axis=0)
        middle = inner[k]
        forward[k] = middle[TOP : TOP + rows]
        for dy in range(-H, H + 1):
            moved[k * (2 * H + 1) + dy + H] = shifted(middle, side, dy)
    near = [jnp.zeros((rows, LANES), f32) for _ in range(2 * F)]
    for code in range(OFFSETS):
        dx, dy = offset_of(code)
        window = lambda k: moved[k * (2 * H + 1) + dy + H, TOP + dx : TOP + dx + rows]
        for f in range(F):
            g = (green[4 * code + 2 * f], green[4 * code + 2 * f + 1])
            add = times(g, (window(2 * f), window(2 * f + 1)))
            near[2 * f] += add[0]
            near[2 * f + 1] += add[1]
    x, y = place_ids(place, rows, LANES, 0, 0, rows)
    h = heights[...]
    for f in range(F):
        rest = []
        for part in range(2):
            k = 2 * f + part
            w = jnp.concatenate([weak[tile, k] for tile in range(1, tiles - 1)], axis=0)
            rest.append(incident[k] - near[k] - w)
        s = times((inverse[2 * f], inverse[2 * f + 1]), rest)
        driven[2 * f] = s[0]
        driven[2 * f + 1] = s[1]
        add = conj_times(carrier(f, 1, x, y, h), s)
        cs[2 * f] = add[0]
        cs[2 * f + 1] = add[1]

    def keep(f, row):
        common[f : f + 1] = row

    right_mat[2 * SUB :] = jnp.zeros((right_mat.shape[0] - 2 * SUB, right_mat.shape[1]), f32)
    project(left_mat, right_mat, tables, 2, cs, rows, keep)
    pair = common[0:2]

    def fill(s, _):
        payload[s] = pair
        return 0

    lax.fori_loop(0, n_r * n_c, fill, 0)


def sides_tile(side, rows_at):
    return side[0][rows_at] if isinstance(side, list) else side[rows_at]


def last_body(n_r, n_c, spread, place, recv, feeds, driven, heights, inverse, weights, currents, amps):
    rows = heights.shape[0]
    d = place[0]
    wts = [weights[k : k + 1] for k in range(2 * F)]
    zero = jnp.zeros((SUB, LANES), f32)

    def lap(k, carry):
        j = n_r - 1 - k
        gens = sums_of(recv, j * n_c, n_c)[:SUB]
        share = recv[j * n_c, SUB + 2 : SUB + 3]
        feed = feeds[j * n_c]
        for i in range(1, n_c):
            feed = feed + feeds[j * n_c + i]
        new = sweep_step(gens, feed, share, wts, [(carry[0], carry[1]), (carry[2], carry[3])], spread)
        return (new[0][0], new[0][1], new[1][0], new[1][1])

    carry = lax.fori_loop(0, n_r - 1 - d, lap, (zero,) * (2 * F))
    carry = [(carry[0], carry[1]), (carry[2], carry[3])]
    for f, parts in enumerate(amplitudes(wts, carry, spread)):
        for part, columns in enumerate(parts):
            for a1, column in enumerate(columns):
                amps[2 * f + part, SUB * a1 : SUB * (a1 + 1)] = jnp.broadcast_to(column, (SUB, LANES))
    splat = lambda f, part, a: amps[2 * f + part, a : a + 1]
    for tile in range(rows // SUB):
        rows_at = slice(SUB * tile, SUB * (tile + 1))
        x, y = place_ids(place, SUB, LANES, SUB * tile, 0, rows)
        h = heights[rows_at]
        u1, u2 = radiate(None, 0, None, 1, x, y, h)
        for f in range(F):
            w = radiated(f, splat, u1, u2, carrier(f, 1, x, y, h))
            lost = times((inverse[2 * f, rows_at], inverse[2 * f + 1, rows_at]), w)
            currents[2 * f, rows_at] = driven[2 * f, rows_at] - lost[0]
            currents[2 * f + 1, rows_at] = driven[2 * f + 1, rows_at] - lost[1]


def swaps(n):
    first = [(i, i ^ 1) for i in range(n) if i ^ 1 < n]
    second = [(i, i + 1) for i in range(1, n - 1, 2)] + [(i + 1, i) for i in range(1, n - 1, 2)]
    return first, second


def swap(axis, n, a, b):
    first, second = swaps(n)
    return lax.ppermute(a, axis, first), lax.ppermute(b, axis, second)


def lanes_of(values):
    lead = values.shape[:-1]
    split = values.reshape(lead + (Q // SUB, SUB))
    return jnp.concatenate([split, jnp.zeros_like(split)], -1).reshape(lead + (2 * Q,))


def per_device(n_r, n_c, incident, inverse_diag, previous, heights, neighbours, counts, transmit, angle_weights):
    rows, cols = heights.shape
    patches = rows * cols
    spread = 1.0 / math.sqrt(rows * cols * n_c)
    slots = n_r * n_c
    place = jnp.stack([lax.axis_index("rng"), lax.axis_index("xr")]).astype(jnp.int32)
    weights = lanes_of(angle_weights.reshape(2 * F, Q))
    share = transmit.reshape(F, Q // SUB, SUB)
    share = jnp.concatenate([share[0], share[1]], -1).reshape(1, 2 * Q)
    tall = rows + 2 * SUB
    cols_a, cols_b = call(columns_body, [(rows, LANES)] * 2, 3)(place, previous, heights, inverse_diag)
    tables, gens = call(
        tables_body,
        [(6, rows, SUB, LANES), (2 * SUB, LANES)],
        3,
        [pltpu.VMEM((16 * SUB, patches), f32), pltpu.VMEM((16 * SUB, patches), f32)],
    )(place, heights, inverse_diag, weights)
    cols_a, cols_b = swap("xr", n_c, cols_a, cols_b)
    rows_a, rows_b = call(rows_body, [(ROWS_SENT, LANES)] * 2, 5)(
        place, previous, heights, inverse_diag, cols_a, cols_b
    )
    rows_a, rows_b = swap("rng", n_r, rows_a, rows_b)
    payload, green, source, ext = call(
        functools.partial(near_body, n_r, n_c),
        [(slots, SLOT, LANES), (4 * OFFSETS, rows, LANES), (2 * F, rows, LANES), (4 * F + 2, tall, LANES)],
        13,
        [
            pltpu.VMEM((N_FIELDS, tall, LANES), f32),
            pltpu.VMEM((SUB, LANES), f32),
            pltpu.VMEM((tall, LANES), f32),
            pltpu.VMEM((tall, LANES), f32),
            pltpu.VMEM(((2 * F + 1) * (2 * H + 1), tall, LANES), f32),
            pltpu.VMEM((2 * F, rows, LANES), f32),
            pltpu.VMEM((4 * SUB, patches), f32),
            pltpu.VMEM((16 * SUB, patches), f32),
            pltpu.VMEM((3 * SUB, LANES), f32),
        ],
    )(
        place, previous, heights, inverse_diag, incident, neighbours, counts, share,
        cols_a, cols_b, rows_a, rows_b, gens, tables,
    )
    recv = lax.all_to_all(payload, BOTH, 0, 0)
    forward, driven, payload = call(
        functools.partial(new_body, n_r, n_c, spread),
        [(2 * F, rows, LANES), (2 * F, rows, LANES), (slots, 2, LANES)],
        9,
        [
            pltpu.VMEM((n_r + 1, 2 * F, SUB, LANES), f32),
            pltpu.VMEM((3, 2 * F, Q, LANES), f32),
            pltpu.VMEM((2 * F, tall, LANES), f32),
            pltpu.VMEM((2 * F * (2 * H + 1), tall, LANES), f32),
            pltpu.VMEM((tall, LANES), f32),
            pltpu.VMEM((tall, LANES), f32),
            pltpu.VMEM((2 * F, rows, LANES), f32),
            pltpu.VMEM((4 * SUB, patches), f32),
            pltpu.VMEM((16 * SUB, patches), f32),
            pltpu.VMEM((SUB, LANES), f32),
        ],
    )(place, recv, green, source, ext, heights, inverse_diag, incident, tables, weights)
    feeds = lax.all_to_all(payload, BOTH, 0, 0)
    (currents,) = call(
        functools.partial(last_body, n_r, n_c, spread),
        [(2 * F, rows, LANES)],
        6,
        [pltpu.VMEM((2 * F, Q, LANES), f32)],
    )(place, recv, feeds, driven, heights, inverse_diag, weights)
    return forward, currents


def solution(mesh):
    body = functools.partial(per_device, mesh.shape["rng"], mesh.shape["xr"])
    field = P(None, "rng", "xr")
    return jax.shard_map(
        body,
        mesh=mesh,
        in_specs=(field, field, field, P("rng", "xr"), field, P("rng", "xr"), P("rng", None, None), P()),
        out_specs=(field, field),
        check_vma=False,
    )
```

```python
import functools
import math

import jax
import jax.numpy as jnp
from jax import lax
from jax.experimental import pallas as pl
from jax.experimental.pallas import tpu as pltpu
from jax.sharding import PartitionSpec as P

F = 2
Q = 64
H = 3
LMAX = 24
OFFSETS = 48
SUB = 8
LANES = 128
PERIOD = 64
TOP = SUB
GREEN = 0.25
TURN = 2.0 * math.pi
SLOT = 16
HALO_AT = SUB + 3
HIGHEST = lax.Precision.HIGHEST
BOTH = ("rng", "xr")
f32 = jnp.float32


def iota(shape, dim):
    return lax.broadcasted_iota(jnp.int32, shape, dim)


def roll(x, shift, axis=1):
    shift = shift % x.shape[axis]
    return x if shift == 0 else pltpu.roll(x, shift, axis)


def cos_sin(turns):
    quarter = jnp.floor(4.0 * turns + 0.5)
    rest = turns - 0.25 * quarter
    which = quarter.astype(jnp.int32)
    sq = rest * rest
    s = rest * (TURN + sq * (-(TURN**3) / 6 + sq * (TURN**5 / 120 + sq * (-(TURN**7) / 5040 + sq * (TURN**9 / 362880)))))
    c = 1.0 + sq * (-(TURN**2) / 2 + sq * (TURN**4 / 24 + sq * (-(TURN**6) / 720 + sq * (TURN**8 / 40320))))
    odd = (which & 1) == 1
    cos = jnp.where(odd, s, c)
    sin = jnp.where(odd, c, s)
    cos = jnp.where(((which + 1) & 2) == 2, -cos, cos)
    sin = jnp.where((which & 2) == 2, -sin, sin)
    return cos, sin


def times(a, b):
    return a[0] * b[0] - a[1] * b[1], a[0] * b[1] + a[1] * b[0]


def conj_times(a, b):
    return a[0] * b[0] + a[1] * b[1], a[0] * b[1] - a[1] * b[0]


def wave(step_x, x, step_y, y, lift, heights):
    phase = (step_x * x + step_y * y) & (PERIOD - 1)
    return cos_sin(phase.astype(f32) * (1.0 / PERIOD) + (lift / TURN) * heights)


def offset_of(code):
    full = code + (1 if code >= OFFSETS // 2 else 0)
    return full // (2 * H + 1) - H, full % (2 * H + 1) - H


VMEM = pl.BlockSpec(memory_space=pltpu.VMEM)
PLAIN = pl.BlockSpec()


def call(body, out, ins, scratch=(), flops=2_000_000):
    return pl.pallas_call(
        body,
        out_shape=tuple(jax.ShapeDtypeStruct(s, f32) if isinstance(s, tuple) else s for s in out),
        in_specs=list(ins),
        out_specs=tuple(VMEM for _ in out),
        scratch_shapes=list(scratch),
        compiler_params=pltpu.CompilerParams(vmem_limit_bytes=48 * 1024 * 1024),
        cost_estimate=pl.CostEstimate(flops=flops, bytes_accessed=1 << 20, transcendentals=0),
    )


def place_of():
    return lax.axis_index("rng"), lax.axis_index("xr")


def pack_columns(fields, right):
    rows = fields[0].shape[0]
    lane = iota((rows, LANES), 1)
    packed = jnp.zeros((rows, LANES), f32)
    for k, field in enumerate(fields):
        moved = roll(field, H * k - (LANES - H) if right else H * k)
        packed = jnp.where((lane >= H * k) & (lane < H * (k + 1)), moved, packed)
    return packed


def unpack_columns(from_left, from_right, k):
    lane = iota(from_left.shape, 1)
    left = jnp.where(lane >= LANES - H, roll(from_left, LANES - H - H * k), 0.0)
    return jnp.where(lane < H, roll(from_right, -H * k), left)


def shifted(inner, edge, dy):
    if dy == 0:
        return inner
    lane = iota(inner.shape, 1)
    outside = lane >= LANES - dy if dy > 0 else lane < -dy
    return jnp.where(outside, roll(edge, -dy), roll(inner, -dy))


N_FIELDS = 4 * F + 1
ROWS_SENT = 48
GENS_AT = 40


def columns_body(fields, send_a, send_b):
    values = [fields[k] for k in range(N_FIELDS)]
    right = pack_columns(values, True)
    left = pack_columns(values, False)
    even = (lax.axis_index("xr") & 1) == 0
    send_a[...] = jnp.where(even, right, left)
    send_b[...] = jnp.where(even, left, right)


def rows_body(fields, gens, recv_a, recv_b, send_a, send_b):
    d, c = place_of()
    even_c = (c & 1) == 0
    even_r = (d & 1) == 0
    rows = fields.shape[1]
    values = [fields[k] for k in range(N_FIELDS)]
    values.append(jnp.where(even_c, recv_b[...], recv_a[...]))
    values.append(jnp.where(even_c, recv_a[...], recv_b[...]))
    for k, field in enumerate(values):
        last, first = field[rows - H :], field[:H]
        send_a[H * k : H * (k + 1)] = jnp.where(even_r, last, first)
        send_b[H * k : H * (k + 1)] = jnp.where(even_r, first, last)
    used = H * len(values)
    send_a[used:GENS_AT] = jnp.zeros((GENS_AT - used, LANES), f32)
    send_b[used:GENS_AT] = jnp.zeros((GENS_AT - used, LANES), f32)
    down, up = gens[0:SUB], gens[SUB : 2 * SUB]
    send_a[GENS_AT:] = jnp.where(even_r, down, up)
    send_b[GENS_AT:] = jnp.where(even_r, up, down)


def tables_body(fields, tables, gens, left_mat, right_mat):
    d, c = place_of()
    rows = fields.shape[1]
    x0 = d * rows
    y0 = c * LANES
    angle = iota((2 * SUB, LANES), 0) - SUB
    y = iota((2 * SUB, LANES), 1) + y0
    for i in range(rows):
        x = jnp.full((2 * SUB, LANES), x0 + i, jnp.int32)
        lanes = pl.ds(i * LANES, LANES)
        h2 = jnp.broadcast_to(fields[2 * F, i : i + 1, :], (2 * SUB, LANES)) * angle.astype(f32)
        c2, s2 = wave(0, x, angle, y, 0.03, h2)
        tables[4, i] = c2[SUB:]
        tables[5, i] = s2[SUB:]
        right_mat[0 : 2 * SUB, lanes] = c2
        right_mat[2 * SUB : 4 * SUB, lanes] = s2
        for direction in range(2):
            c1, s1 = wave(angle * (1 - 2 * direction), x, 0, y, 0.24, h2)
            tables[2 * direction, i] = c1[SUB:]
            tables[2 * direction + 1, i] = s1[SUB:]
            for f in range(F):
                zr = fields[2 * F + 1 + 2 * f, i : i + 1, :]
                zi = fields[2 * F + 2 + 2 * f, i : i + 1, :]
                base = (direction * F + f) * 4 * SUB
                left_mat[base : base + 2 * SUB, lanes] = zr * c1 - zi * s1
                left_mat[base + 2 * SUB : base + 4 * SUB, lanes] = zr * s1 + zi * c1
    right_mat[4 * SUB :] = jnp.zeros((right_mat.shape[0] - 4 * SUB, right_mat.shape[1]), f32)
    both = lax.dot_general(
        left_mat[...], right_mat[...], (((1,), (1,)), ((), ())), precision=HIGHEST, preferred_element_type=f32
    )
    lane = iota((SUB, LANES), 1)
    for direction in range(2):
        for f in range(F):
            base = (direction * F + f) * 4 * SUB
            for half in range(2):
                p = both[base + half * SUB : base + (half + 1) * SUB]
                q = both[base + (2 + half) * SUB : base + (3 + half) * SUB]
                for part in range(2):
                    if part == 0:
                        g = p - roll(q, -2 * SUB)
                    else:
                        g = roll(p, -2 * SUB) + q
                    g = jnp.where(lane < 2 * SUB, g, 0.0)
                    g = pltpu.roll(g, 0, 1, stride=2 * SUB, stride_axis=0)
                    row = jnp.sum(g, axis=0, keepdims=True)
                    at = direction * SUB + f * 4 + part * 2 + (1 - half)
                    gens[at : at + 1] = row


def lists_body(lists, params, bits, weights, share):
    count = lists[LMAX]
    low = jnp.zeros(count.shape, jnp.int32)
    high = jnp.zeros(count.shape, jnp.int32)
    half = OFFSETS // 2
    one = jnp.ones(count.shape, jnp.int32)
    for slot in range(LMAX):
        code = lists[slot]
        live = count > slot
        is_low = code < half
        bit = lax.shift_left(one, jnp.where(is_low, code, code - half))
        low = low | jnp.where(live & is_low, bit, 0)
        high = high | jnp.where(live & (code >= half), bit, 0)
    bits[0] = low
    bits[1] = high
    spot = iota((Q, LANES), 0)
    spot = 2 * SUB * (spot // SUB) + (spot & (SUB - 1))
    values = params[...]
    placed = [
        lax.dot_general(
            values,
            (iota((Q, LANES), 1) == spot + SUB * k).astype(f32),
            (((1,), (0,)), ((), ())),
            precision=HIGHEST,
            preferred_element_type=f32,
        )
        for k in range(2)
    ]
    weights[...] = placed[0][: 2 * F] + placed[1][: 2 * F]
    share[...] = placed[0][2 * F : 2 * F + 1] + placed[1][2 * F + 1 : 2 * F + 2]


def project(left_mat, right_mat, tables, first, cs, rows, f_out):
    for i in range(rows):
        lanes = pl.ds(i * LANES, LANES)
        right_mat[0:SUB, lanes] = tables[4, i]
        right_mat[SUB : 2 * SUB, lanes] = tables[5, i]
        c1, s1 = tables[first, i], tables[first + 1, i]
        for f in range(F):
            re, im = conj_times((c1, s1), (cs[2 * f, i : i + 1, :], cs[2 * f + 1, i : i + 1, :]))
            left_mat[2 * f * SUB : (2 * f + 1) * SUB, lanes] = re
            left_mat[(2 * f + 1) * SUB : (2 * f + 2) * SUB, lanes] = im
    sums = lax.dot_general(
        left_mat[0 : 4 * SUB], right_mat[...], (((1,), (1,)), ((), ())), precision=HIGHEST, preferred_element_type=f32
    )
    lane = iota((SUB, LANES), 1)
    for f in range(F):
        gr = sums[2 * f * SUB : (2 * f + 1) * SUB]
        gi = sums[(2 * f + 1) * SUB : (2 * f + 2) * SUB]
        re = gr + roll(gi, -SUB)
        im = gi - roll(gr, -SUB)
        packed = jnp.where(lane < SUB, re, jnp.where(lane < 2 * SUB, roll(im, SUB), 0.0))
        packed = pltpu.roll(packed, 0, 1, stride=2 * SUB, stride_axis=0)
        f_out(f, jnp.sum(packed, axis=0, keepdims=True))


def carrier(f, direction, x, y, heights):
    sign = 1 - 2 * direction
    return wave(sign * (1 + 2 * f), x, f - 4, y, 0.3 + 0.2 * f, heights)


def place_ids(rows, cols, first_row, first_col, own_rows):
    d, c = place_of()
    x = d * own_rows + first_row + iota((rows, cols), 0)
    y = c * LANES + first_col + iota((rows, cols), 1)
    return x, y


def near_body(
    n_r, n_c, fields, fed, bits, share, cols_a, cols_b, rows_a, rows_b, gens, tables,
    payload, green, source, ext, near_gens, inner, edge_l, edge_r, moved, cs, left_mat, right_mat, common, halo,
):
    rows = fields.shape[1]
    d, c = place_of()
    even_c = (c & 1) == 0
    even_r = (d & 1) == 0
    below = jnp.where(even_r, rows_a[...], rows_b[...])
    above = jnp.where(even_r, rows_b[...], rows_a[...])
    near_gens[0] = above[GENS_AT:]
    near_gens[1] = below[GENS_AT:]
    edge_l[...] = jnp.zeros(edge_l.shape, f32)
    edge_r[...] = jnp.zeros(edge_r.shape, f32)
    edge_l[TOP : TOP + rows] = jnp.where(even_c, cols_b[...], cols_a[...])
    edge_r[TOP : TOP + rows] = jnp.where(even_c, cols_a[...], cols_b[...])
    at = H * N_FIELDS
    edge_l[TOP - H : TOP] = above[at : at + H]
    edge_l[TOP + rows : TOP + rows + H] = below[at : at + H]
    edge_r[TOP - H : TOP] = above[at + H : at + 2 * H]
    edge_r[TOP + rows : TOP + rows + H] = below[at + H : at + 2 * H]
    from_left, from_right = edge_l[...], edge_r[...]
    for k in range(N_FIELDS):
        inner[k] = jnp.zeros(inner.shape[1:], f32)
        inner[k, TOP : TOP + rows] = fields[k]
        inner[k, TOP - H : TOP] = above[H * k : H * (k + 1)]
        inner[k, TOP + rows : TOP + rows + H] = below[H * k : H * (k + 1)]
        side = unpack_columns(from_left, from_right, k)
        if k >= 2 * F:
            ext[2 * (k - 2 * F)] = inner[k]
            ext[2 * (k - 2 * F) + 1] = side
        if k <= 2 * F:
            middle = inner[k]
            for dy in range(-H, H + 1):
                moved[k * (2 * H + 1) + dy + H] = shifted(middle, side, dy)
    h = fields[2 * F]
    inverse = [fields[2 * F + 1 + k] for k in range(2 * F)]
    incident = [fed[k] for k in range(2 * F)]
    low, high = bits[0], bits[1]
    half = OFFSETS // 2
    near = [jnp.zeros((rows, LANES), f32) for _ in range(2 * F)]
    for code in range(OFFSETS):
        dx, dy = offset_of(code)
        window = lambda k: moved[k * (2 * H + 1) + dy + H, TOP + dx : TOP + dx + rows]
        lift = window(2 * F) - h
        squared = float(dx * dx + dy * dy) + lift * lift
        inverse_r = lax.rsqrt(squared)
        r = squared * inverse_r
        bits = low if code < half else high
        there = (bits & (1 << (code % half))) != 0
        size = jnp.where(there, GREEN * inverse_r, 0.0)
        for f in range(F):
            cos, sin = cos_sin(r * (0.25 * (1.0 + 0.25 * f)))
            g = (size * cos, size * sin)
            green[4 * code + 2 * f] = g[0]
            green[4 * code + 2 * f + 1] = g[1]
            got = times(g, (window(2 * f), window(2 * f + 1)))
            near[2 * f] += got[0]
            near[2 * f + 1] += got[1]
    x, y = place_ids(rows, LANES, 0, 0, rows)
    sources = []
    for f in range(F):
        z = (inverse[2 * f], inverse[2 * f + 1])
        s = times(z, (incident[2 * f] - near[2 * f], incident[2 * f + 1] - near[2 * f + 1]))
        sources += s
        source[2 * f] = s[0]
        source[2 * f + 1] = s[1]
        got = conj_times(carrier(f, 0, x, y, h), s)
        cs[2 * f] = got[0]
        cs[2 * f + 1] = got[1]

    def keep(f, row):
        common[2 * SUB + f : 2 * SUB + f + 1] = row

    right_mat[2 * SUB :] = jnp.zeros((right_mat.shape[0] - 2 * SUB, right_mat.shape[1]), f32)
    common[2 * SUB :] = jnp.zeros((SUB, LANES), f32)
    project(left_mat, right_mat, tables, 0, cs, rows, keep)
    common[0 : 2 * SUB] = gens[...]
    common[2 * SUB + 2 : 2 * SUB + 3] = share[...]
    tail = common[2 * SUB : 3 * SUB]
    for direction in range(2):
        part = common[direction * SUB : (direction + 1) * SUB]

        def fill(s, _, part=part, tail=tail):
            payload[s, 0:SUB] = part
            payload[s, SUB : 2 * SUB] = tail
            return 0

        if direction == 0:
            lax.fori_loop(d * n_c, n_r * n_c, fill, 0)
        else:
            lax.fori_loop(0, d * n_c, fill, 0)
    lasts = pack_columns(sources, True)
    firsts = pack_columns(sources, False)
    at = HALO_AT

    def send(dr, dc, put):
        dst = (d + dr) * n_c + c + dc
        ok = (d + dr >= 0) & (d + dr < n_r) & (c + dc >= 0) & (c + dc < n_c)

        @pl.when(ok)
        def _():
            put(dst)

    def rows_to(dr):
        for k in range(2 * F):
            s = sources[k]
            halo[H * k : H * (k + 1)] = s[rows - H :] if dr > 0 else s[:H]
        first, rest = halo[0:SUB], halo[SUB : 2 * F * H]

        def put(dst):
            payload[dst, 0:SUB] = first
            payload[dst, at : at + 2 * F * H - SUB] = rest

        return put

    def cols_to(dc):
        packed = lasts if dc > 0 else firsts
        quarter = rows // 4
        parts = [roll(packed, 4 * SUB * i)[quarter * i : quarter * (i + 1)] for i in range(4)]
        packed = parts[0] + parts[1] + parts[2] + parts[3]

        def put(dst):
            payload[dst, at : at + quarter] = packed

        return put

    def corner_to(dr, dc):
        packed = lasts if dc > 0 else firsts

        def put(dst):
            payload[dst, at : at + H] = packed[rows - H :] if dr > 0 else packed[:H]

        return put

    for dr in (-1, 1):
        send(dr, 0, rows_to(dr))
        send(0, dr, cols_to(dr))
        for dc in (-1, 1):
            send(dr, dc, corner_to(dr, dc))


def toeplitz(gens, sub, lane):
    wide = [jnp.broadcast_to(gens[k : k + 1], (SUB, LANES)) for k in range(4)]
    low = (lane & SUB) == 0

    def tile(part, by):
        inside = (lane >= by + sub) & (lane < by + sub + LANES)
        one = pltpu.roll(wide[2 * part], by % LANES, 1, stride=1, stride_axis=0)
        two = pltpu.roll(wide[2 * part + 1], by % LANES, 1, stride=1, stride_axis=0)
        return jnp.where(inside, one, two)

    out = []
    for a1 in range(Q // SUB):
        by = 2 * SUB * a1 - SUB
        out.append(jnp.where(low, tile(0, by), -tile(1, by + SUB)))
    for a1 in range(Q // SUB):
        by = 2 * SUB * a1 - SUB
        out.append(jnp.where(low, tile(1, by), tile(0, by + SUB)))
    return out


def to_columns(row, sub, lane):
    return [
        jnp.sum(jnp.where(lane == 2 * SUB * a1 + SUB * part + sub, row, 0.0), axis=1, keepdims=True)
        for part in range(2)
        for a1 in range(Q // SUB)
    ]


def to_row(columns, sub, lane):
    total = jnp.zeros((SUB, LANES), f32)
    for k, column in enumerate(columns):
        part, a1 = k // (Q // SUB), k % (Q // SUB)
        total = jnp.where(lane == 2 * SUB * a1 + SUB * part + sub, column, total)
    return jnp.broadcast_to(jnp.sum(total, axis=0, keepdims=True), (SUB, LANES))


def wide(row):
    return jnp.broadcast_to(row, (SUB, LANES))


def packed_times(wr, wi, row, low):
    turned = jnp.where(low, -roll(row, -SUB), roll(row, SUB))
    return wr * row + wi * turned


def sweep_step(maps, feeds, shares, weights, carry, spread):
    sub = iota((SUB, LANES), 0)
    lane = iota((SUB, LANES), 1)
    low = (lane & SUB) == 0
    out = []
    for f in range(F):
        amp = packed_times(weights[2 * f], weights[2 * f + 1], carry[f], low)
        columns = [jnp.sum(maps(f, k) * amp, axis=1, keepdims=True) for k in range(2 * Q // SUB)]
        out.append(shares[f] * (carry[f] + feeds[f] - spread * to_row(columns, sub, lane)))
    return out


def shares_of(row):
    lane = iota((SUB, LANES), 1)
    low = (lane & SUB) == 0
    row = wide(row)
    return jnp.where(low, row, roll(row, SUB)), jnp.where(low, roll(row, -SUB), row)


def put_amplitudes(put, weights, carry, spread):
    sub = iota((SUB, LANES), 0)
    lane = iota((SUB, LANES), 1)
    low = (lane & SUB) == 0
    for f in range(F):
        amp = spread * packed_times(weights[2 * f], weights[2 * f + 1], carry[f], low)
        for k, column in enumerate(to_columns(amp, sub, lane)):
            put(f, slice(SUB * k, SUB * (k + 1)), jnp.broadcast_to(column, (SUB, LANES)))


def laps(n, body):
    if n <= SUB:
        for j in range(n):
            body(j)
    else:
        lax.fori_loop(0, n, lambda j, _: (body(j), 0)[1], 0)


def gens_sum(recv, j, n_c, d, c, step, own):
    total = None
    for k in range(n_c):
        part = recv[j * n_c + k, 0:SUB]
        part = jnp.where((j == d + step) & (k == c), own, part)
        total = part if total is None else total + part
    return total


def store_maps(maps, j, gens):
    sub = iota((SUB, LANES), 0)
    lane = iota((SUB, LANES), 1)
    for f in range(F):
        for k, tile in enumerate(toeplitz(gens[4 * f : 4 * f + 4], sub, lane)):
            maps[j, f, SUB * k : SUB * (k + 1)] = tile


def powers(base, count):
    out = [None, base]
    for _ in range(2, count):
        out.append(times(out[-1], base))
    return out


def wave_powers(direction, x, y, heights):
    u1 = powers(wave(1 - 2 * direction, x, 0, y, 0.24, heights), Q // SUB)
    u2 = powers(wave(0, x, 1, y, 0.03, heights), SUB)
    return u1, u2


def radiated(f, splat, u1, u2, carried):
    total = None
    for a1 in range(Q // SUB):
        ar, ai = splat(f, SUB * a1), splat(f, Q + SUB * a1)
        inner = (ar, ai)
        for a2 in range(1, SUB):
            got = times((splat(f, SUB * a1 + a2), splat(f, Q + SUB * a1 + a2)), u2[a2])
            inner = (inner[0] + got[0], inner[1] + got[1])
        if a1 == 0:
            total = inner
        else:
            got = times(u1[a1], inner)
            total = (total[0] + got[0], total[1] + got[1])
    return times(carried, total)


def back_body(n_r, n_c, recv, near_gens, maps):
    d, c = place_of()
    below = near_gens[1]

    def body(j):
        store_maps(maps, j, gens_sum(recv, j + 1, n_c, d, c, 1, below))

    laps(n_r - 1, body)


def new_body(
    n_r, n_c, spread, recv, green, source, ext, fields, fed, near_gens, tables, weights,
    forward, driven, payload, maps, feeds, carries, amps, inner, moved, edge_l, edge_r, cs, left_mat, right_mat, common, halo,
):
    rows = fields.shape[1]
    d, c = place_of()
    wts = [wide(weights[k : k + 1]) for k in range(2 * F)]
    zero = jnp.zeros((SUB, LANES), f32)
    above = near_gens[0]

    def prepare(j):
        store_maps(maps, j, gens_sum(recv, j, n_c, d, c, -1, above))
        feed = recv[j * n_c, SUB : 2 * SUB]
        for k in range(1, n_c):
            feed = feed + recv[j * n_c + k, SUB : 2 * SUB]
        feeds[j] = feed

    laps(n_r - 1, prepare)
    for f in range(F):
        carries[0, f] = zero

    def lap(j, carry):
        new = sweep_step(
            lambda f, k: maps[j, f, SUB * k : SUB * (k + 1)],
            [wide(feeds[j, f : f + 1]) for f in range(F)],
            shares_of(recv[j * n_c, SUB + 2 : SUB + 3]),
            wts,
            carry,
            spread,
        )
        for f in range(F):
            carries[j + 1, f] = new[f]
        return tuple(new)

    lax.fori_loop(0, jnp.minimum(d + 1, n_r - 1), lap, (zero,) * F)
    for which in range(3):
        at = jnp.clip(d + which - 1, 0, n_r - 1)

        def put(f, at_rows, tile, which=which):
            amps[which, f, at_rows] = tile

        put_amplitudes(put, wts, [carries[at, f] for f in range(F)], spread)

    at = HALO_AT

    def got(dr, dc, start, size):
        src = jnp.clip(d + dr, 0, n_r - 1) * n_c + jnp.clip(c + dc, 0, n_c - 1)
        ok = (d + dr >= 0) & (d + dr < n_r) & (c + dc >= 0) & (c + dc < n_c)
        return jnp.where(ok, recv[src, start : start + size], 0.0)

    edge_l[...] = jnp.zeros(edge_l.shape, f32)
    edge_r[...] = jnp.zeros(edge_r.shape, f32)
    quarter = rows // 4
    for edge, dc in ((edge_l, -1), (edge_r, 1)):
        side = got(0, dc, at, quarter)
        for i in range(4):
            edge[TOP + quarter * i : TOP + quarter * (i + 1)] = roll(side, -4 * SUB * i)
        edge[TOP - H : TOP] = got(-1, dc, at, H)
        edge[TOP + rows : TOP + rows + H] = got(1, dc, at, H)
    from_left, from_right = edge_l[...], edge_r[...]
    for i, dr in enumerate((-1, 1)):
        halo[i, 0:SUB] = got(dr, 0, 0, SUB)
        halo[i, SUB : 2 * F * H] = got(dr, 0, at, 2 * F * H - SUB)
    for k in range(2 * F):
        inner[k] = jnp.zeros(inner.shape[1:], f32)
        inner[k, TOP : TOP + rows] = source[k]
        inner[k, TOP - H : TOP] = halo[0, H * k : H * (k + 1)]
        inner[k, TOP + rows : TOP + rows + H] = halo[1, H * k : H * (k + 1)]
    sides = [unpack_columns(from_left, from_right, k) for k in range(2 * F)]

    weak = {}
    tiles = (rows + 2 * SUB) // SUB
    for tile in range(tiles):
        which = 0 if tile == 0 else 2 if tile == tiles - 1 else 1
        splat = lambda f, a, which=which: amps[which, f, a : a + 1]
        rows_at = slice(SUB * tile, SUB * (tile + 1))
        for side in range(2):
            x, y = place_ids(SUB, LANES, SUB * tile - TOP, 0, rows)
            if side == 1:
                lane = iota((SUB, LANES), 1)
                y = y + jnp.where(lane < LANES // 2, LANES, -LANES)
            h = ext[side, rows_at]
            u1, u2 = wave_powers(0, x, y, h)
            for f in range(F):
                w = radiated(f, splat, u1, u2, carrier(f, 0, x, y, h))
                z = (ext[2 * (1 + 2 * f) + side, rows_at], ext[2 * (2 + 2 * f) + side, rows_at])
                lost = times(z, w)
                for part in range(2):
                    k = 2 * f + part
                    if side == 0:
                        inner[k, rows_at] = inner[k, rows_at] - lost[part]
                        weak[tile, k] = w[part]
                    else:
                        sides[k] = (sides[k] if isinstance(sides[k], list) else [sides[k]]) + [
                            sides_tile(sides[k], rows_at) - lost[part]
                        ]
    for k in range(2 * F):
        side = jnp.concatenate(sides[k][1:], axis=0)
        middle = inner[k]
        forward[k] = middle[TOP : TOP + rows]
        for dy in range(-H, H + 1):
            moved[k * (2 * H + 1) + dy + H] = shifted(middle, side, dy)
    near = [jnp.zeros((rows, LANES), f32) for _ in range(2 * F)]
    for code in range(OFFSETS):
        dx, dy = offset_of(code)
        window = lambda k: moved[k * (2 * H + 1) + dy + H, TOP + dx : TOP + dx + rows]
        for f in range(F):
            g = (green[4 * code + 2 * f], green[4 * code + 2 * f + 1])
            add = times(g, (window(2 * f), window(2 * f + 1)))
            near[2 * f] += add[0]
            near[2 * f + 1] += add[1]
    x, y = place_ids(rows, LANES, 0, 0, rows)
    h = fields[2 * F]
    for f in range(F):
        rest = []
        for part in range(2):
            k = 2 * f + part
            w = jnp.concatenate([weak[tile, k] for tile in range(1, tiles - 1)], axis=0)
            rest.append(fed[k] - near[k] - w)
        s = times((fields[2 * F + 1 + 2 * f], fields[2 * F + 2 + 2 * f]), rest)
        driven[2 * f] = s[0]
        driven[2 * f + 1] = s[1]
        add = conj_times(carrier(f, 1, x, y, h), s)
        cs[2 * f] = add[0]
        cs[2 * f + 1] = add[1]

    def keep(f, row):
        common[f : f + 1] = row

    right_mat[2 * SUB :] = jnp.zeros((right_mat.shape[0] - 2 * SUB, right_mat.shape[1]), f32)
    project(left_mat, right_mat, tables, 2, cs, rows, keep)
    pair = common[0:2]

    def fill(s, _):
        payload[s] = pair
        return 0

    lax.fori_loop(0, n_r * n_c, fill, 0)


def sides_tile(side, rows_at):
    return side[0][rows_at] if isinstance(side, list) else side[rows_at]


def last_body(n_r, n_c, spread, recv, maps, feeds, driven, fields, weights, currents, amps):
    rows = fields.shape[1]
    d, _ = place_of()
    wts = [wide(weights[k : k + 1]) for k in range(2 * F)]
    zero = jnp.zeros((SUB, LANES), f32)

    def lap(k, carry):
        j = n_r - 1 - k
        feed = feeds[j * n_c]
        for i in range(1, n_c):
            feed = feed + feeds[j * n_c + i]
        new = sweep_step(
            lambda f, k: maps[j - 1, f, SUB * k : SUB * (k + 1)],
            [wide(feed[f : f + 1]) for f in range(F)],
            shares_of(recv[j * n_c, SUB + 2 : SUB + 3]),
            wts,
            carry,
            spread,
        )
        return tuple(new)

    carry = lax.fori_loop(0, n_r - 1 - d, lap, (zero,) * F)

    def put(f, at_rows, tile):
        amps[f, at_rows] = tile

    put_amplitudes(put, wts, carry, spread)
    splat = lambda f, a: amps[f, a : a + 1]
    for tile in range(rows // SUB):
        rows_at = slice(SUB * tile, SUB * (tile + 1))
        x, y = place_ids(SUB, LANES, SUB * tile, 0, rows)
        h = fields[2 * F, rows_at]
        u1, u2 = wave_powers(1, x, y, h)
        for f in range(F):
            w = radiated(f, splat, u1, u2, carrier(f, 1, x, y, h))
            lost = times((fields[2 * F + 1 + 2 * f, rows_at], fields[2 * F + 2 + 2 * f, rows_at]), w)
            currents[2 * f, rows_at] = driven[2 * f, rows_at] - lost[0]
            currents[2 * f + 1, rows_at] = driven[2 * f + 1, rows_at] - lost[1]


def swaps(n):
    first = [(i, i ^ 1) for i in range(n) if i ^ 1 < n]
    second = [(i, i + 1) for i in range(1, n - 1, 2)] + [(i + 1, i) for i in range(1, n - 1, 2)]
    return first, second


def swap(axis, n, a, b):
    first, second = swaps(n)
    b = lax.ppermute(b, axis, second)
    return lax.ppermute(a, axis, first), b


def per_device(n_r, n_c, incident, inverse_diag, previous, heights, neighbours, counts, transmit, angle_weights):
    rows, cols = heights.shape
    patches = rows * cols
    spread = 1.0 / math.sqrt(rows * cols * n_c)
    slots = n_r * n_c
    tall = rows + 2 * SUB
    fields = jnp.concatenate([previous, heights[None], inverse_diag])
    cols_a, cols_b = call(columns_body, [(rows, LANES)] * 2, [VMEM], flops=500_000)(fields)
    cols_a, cols_b = swap("xr", n_c, cols_a, cols_b)
    tables, gens = call(
        tables_body,
        [(6, rows, SUB, LANES), (2 * SUB, LANES)],
        [VMEM],
        [pltpu.VMEM((16 * SUB, patches), f32), pltpu.VMEM((16 * SUB, patches), f32)],
    )(fields)
    rows_a, rows_b = call(rows_body, [(ROWS_SENT, LANES)] * 2, [VMEM] * 4, flops=500_000)(fields, gens, cols_a, cols_b)
    rows_a, rows_b, neighbours, counts, transmit, angle_weights = lax.optimization_barrier(
        (rows_a, rows_b, neighbours, counts, transmit, angle_weights)
    )
    rows_a, rows_b = swap("rng", n_r, rows_a, rows_b)
    lists = jnp.concatenate([neighbours, counts[None]])
    params = jnp.concatenate([angle_weights.reshape(2 * F, Q), transmit.reshape(F, Q)])
    bits, weights, share = call(
        lists_body, [jax.ShapeDtypeStruct((2, rows, LANES), jnp.int32), (2 * F, LANES), (1, LANES)], [VMEM] * 2
    )(lists, params)
    payload, green, source, ext, near_gens = call(
        functools.partial(near_body, n_r, n_c),
        [
            (slots, SLOT, LANES),
            (4 * OFFSETS, rows, LANES),
            (2 * F, rows, LANES),
            (4 * F + 2, tall, LANES),
            (2, SUB, LANES),
        ],
        [VMEM] * 10,
        [
            pltpu.VMEM((N_FIELDS, tall, LANES), f32),
            pltpu.VMEM((tall, LANES), f32),
            pltpu.VMEM((tall, LANES), f32),
            pltpu.VMEM(((2 * F + 1) * (2 * H + 1), tall, LANES), f32),
            pltpu.VMEM((2 * F, rows, LANES), f32),
            pltpu.VMEM((4 * SUB, patches), f32),
            pltpu.VMEM((16 * SUB, patches), f32),
            pltpu.VMEM((3 * SUB, LANES), f32),
            pltpu.VMEM((2 * SUB, LANES), f32),
        ],
    )(fields, incident, bits, share, cols_a, cols_b, rows_a, rows_b, gens, tables)
    recv = lax.all_to_all(payload, BOTH, 0, 0)
    forward, driven, payload = call(
        functools.partial(new_body, n_r, n_c, spread),
        [(2 * F, rows, LANES), (2 * F, rows, LANES), (slots, 2, LANES)],
        [VMEM] * 9,
        [
            pltpu.VMEM((n_r - 1, F, 2 * Q, LANES), f32),
            pltpu.VMEM((n_r - 1, SUB, LANES), f32),
            pltpu.VMEM((n_r, F, SUB, LANES), f32),
            pltpu.VMEM((3, F, 2 * Q, LANES), f32),
            pltpu.VMEM((2 * F, tall, LANES), f32),
            pltpu.VMEM((2 * F * (2 * H + 1), tall, LANES), f32),
            pltpu.VMEM((tall, LANES), f32),
            pltpu.VMEM((tall, LANES), f32),
            pltpu.VMEM((2 * F, rows, LANES), f32),
            pltpu.VMEM((4 * SUB, patches), f32),
            pltpu.VMEM((16 * SUB, patches), f32),
            pltpu.VMEM((SUB, LANES), f32),
            pltpu.VMEM((2, 2 * SUB, LANES), f32),
        ],
    )(recv, green, source, ext, fields, incident, near_gens, tables, weights)
    feeds = lax.all_to_all(payload, BOTH, 0, 0)
    (maps,) = call(functools.partial(back_body, n_r, n_c), [(n_r - 1, F, 2 * Q, LANES)], [VMEM] * 2)(recv, near_gens)
    (currents,) = call(
        functools.partial(last_body, n_r, n_c, spread),
        [(2 * F, rows, LANES)],
        [VMEM] * 6,
        [pltpu.VMEM((F, 2 * Q, LANES), f32)],
    )(recv, maps, feeds, driven, fields, weights)
    return forward, currents


def solution(mesh):
    body = functools.partial(per_device, mesh.shape["rng"], mesh.shape["xr"])
    field = P(None, "rng", "xr")
    return jax.shard_map(
        body,
        mesh=mesh,
        in_specs=(field, field, field, P("rng", "xr"), field, P("rng", "xr"), P("rng", None, None), P()),
        out_specs=(field, field),
        check_vma=False,
    )
```

```python
import functools
import math

import jax
import jax.numpy as jnp
from jax import lax
from jax.experimental import pallas as pl
from jax.experimental.pallas import tpu as pltpu
from jax.sharding import PartitionSpec as P

F = 2
Q = 64
H = 3
LMAX = 24
OFFSETS = 48
SUB = 8
LANES = 128
PERIOD = 64
TOP = SUB
GREEN = 0.25
TURN = 2.0 * math.pi
SLOT = 16
HALO_AT = SUB + 3
HIGHEST = lax.Precision.HIGHEST
BOTH = ("rng", "xr")
f32 = jnp.float32


def iota(shape, dim):
    return lax.broadcasted_iota(jnp.int32, shape, dim)


def roll(x, shift, axis=1):
    shift = shift % x.shape[axis]
    return x if shift == 0 else pltpu.roll(x, shift, axis)


def cos_sin(turns):
    quarter = jnp.floor(4.0 * turns + 0.5)
    rest = turns - 0.25 * quarter
    which = quarter.astype(jnp.int32)
    sq = rest * rest
    s = rest * (TURN + sq * (-(TURN**3) / 6 + sq * (TURN**5 / 120 + sq * (-(TURN**7) / 5040 + sq * (TURN**9 / 362880)))))
    c = 1.0 + sq * (-(TURN**2) / 2 + sq * (TURN**4 / 24 + sq * (-(TURN**6) / 720 + sq * (TURN**8 / 40320))))
    odd = (which & 1) == 1
    cos = jnp.where(odd, s, c)
    sin = jnp.where(odd, c, s)
    cos = jnp.where(((which + 1) & 2) == 2, -cos, cos)
    sin = jnp.where((which & 2) == 2, -sin, sin)
    return cos, sin


def times(a, b):
    return a[0] * b[0] - a[1] * b[1], a[0] * b[1] + a[1] * b[0]


def conj_times(a, b):
    return a[0] * b[0] + a[1] * b[1], a[0] * b[1] - a[1] * b[0]


def wave(step_x, x, step_y, y, lift, heights):
    phase = (step_x * x + step_y * y) & (PERIOD - 1)
    return cos_sin(phase.astype(f32) * (1.0 / PERIOD) + (lift / TURN) * heights)


def offset_of(code):
    full = code + (1 if code >= OFFSETS // 2 else 0)
    return full // (2 * H + 1) - H, full % (2 * H + 1) - H


VMEM = pl.BlockSpec(memory_space=pltpu.VMEM)
PLAIN = pl.BlockSpec()


def call(body, out, ins, scratch=(), flops=2_000_000):
    return pl.pallas_call(
        body,
        out_shape=tuple(jax.ShapeDtypeStruct(s, f32) if isinstance(s, tuple) else s for s in out),
        in_specs=list(ins),
        out_specs=tuple(VMEM for _ in out),
        scratch_shapes=list(scratch),
        compiler_params=pltpu.CompilerParams(vmem_limit_bytes=48 * 1024 * 1024),
        cost_estimate=pl.CostEstimate(flops=flops, bytes_accessed=1 << 20, transcendentals=0),
    )


def place_of():
    return lax.axis_index("rng"), lax.axis_index("xr")


def pack_columns(fields, right):
    rows = fields[0].shape[0]
    lane = iota((rows, LANES), 1)
    packed = jnp.zeros((rows, LANES), f32)
    for k, field in enumerate(fields):
        moved = roll(field, H * k - (LANES - H) if right else H * k)
        packed = jnp.where((lane >= H * k) & (lane < H * (k + 1)), moved, packed)
    return packed


def unpack_columns(from_left, from_right, k):
    lane = iota(from_left.shape, 1)
    left = jnp.where(lane >= LANES - H, roll(from_left, LANES - H - H * k), 0.0)
    return jnp.where(lane < H, roll(from_right, -H * k), left)


def shifted(inner, edge, dy):
    if dy == 0:
        return inner
    lane = iota(inner.shape, 1)
    outside = lane >= LANES - dy if dy > 0 else lane < -dy
    return jnp.where(outside, roll(edge, -dy), roll(inner, -dy))


N_FIELDS = 4 * F + 1
ROWS_SENT = 48
GENS_AT = 40


def columns_body(fields, send_b, send_a):
    values = [fields[k] for k in range(N_FIELDS)]
    right = pack_columns(values, True)
    left = pack_columns(values, False)
    even = (lax.axis_index("xr") & 1) == 0
    send_a[...] = jnp.where(even, right, left)
    send_b[...] = jnp.where(even, left, right)


def rows_body(fields, gens, recv_b, recv_a, send_b, send_a):
    d, c = place_of()
    even_c = (c & 1) == 0
    even_r = (d & 1) == 0
    rows = fields.shape[1]
    values = [fields[k] for k in range(N_FIELDS)]
    values.append(jnp.where(even_c, recv_b[...], recv_a[...]))
    values.append(jnp.where(even_c, recv_a[...], recv_b[...]))
    for k, field in enumerate(values):
        last, first = field[rows - H :], field[:H]
        send_a[H * k : H * (k + 1)] = jnp.where(even_r, last, first)
        send_b[H * k : H * (k + 1)] = jnp.where(even_r, first, last)
    used = H * len(values)
    send_a[used:GENS_AT] = jnp.zeros((GENS_AT - used, LANES), f32)
    send_b[used:GENS_AT] = jnp.zeros((GENS_AT - used, LANES), f32)
    down, up = gens[0:SUB], gens[SUB : 2 * SUB]
    send_a[GENS_AT:] = jnp.where(even_r, down, up)
    send_b[GENS_AT:] = jnp.where(even_r, up, down)


def tables_body(n_r, fields, tables, gens, left_mat, right_mat):
    d, c = place_of()
    turned = [d & 1, (n_r - 1 - d) & 1]
    signs = [jnp.where(t == 1, -1.0, 1.0) for t in turned]
    rows = fields.shape[1]
    x0 = d * rows
    y0 = c * LANES
    angle = iota((2 * SUB, LANES), 0) - SUB
    y = iota((2 * SUB, LANES), 1) + y0
    for i in range(rows):
        x = jnp.full((2 * SUB, LANES), x0 + i, jnp.int32)
        lanes = pl.ds(i * LANES, LANES)
        h2 = jnp.broadcast_to(fields[2 * F, i : i + 1, :], (2 * SUB, LANES)) * angle.astype(f32)
        c2, s2 = wave(0, x, angle, y, 0.03, h2)
        tables[4, i] = c2[SUB:]
        tables[5, i] = s2[SUB:]
        right_mat[0 : 2 * SUB, lanes] = c2
        right_mat[2 * SUB : 4 * SUB, lanes] = s2
        for direction in range(2):
            c1, s1 = wave(angle * (1 - 2 * direction), x, 0, y, 0.24, h2)
            tables[2 * direction, i] = c1[SUB:]
            tables[2 * direction + 1, i] = s1[SUB:]
            s1 = signs[direction] * s1
            for f in range(F):
                zr = fields[2 * F + 1 + 2 * f, i : i + 1, :]
                zi = fields[2 * F + 2 + 2 * f, i : i + 1, :]
                base = (direction * F + f) * 4 * SUB
                left_mat[base : base + 2 * SUB, lanes] = zr * c1 - zi * s1
                left_mat[base + 2 * SUB : base + 4 * SUB, lanes] = zr * s1 + zi * c1
    right_mat[4 * SUB :] = jnp.zeros((right_mat.shape[0] - 4 * SUB, right_mat.shape[1]), f32)
    both = lax.dot_general(
        left_mat[...], right_mat[...], (((1,), (1,)), ((), ())), precision=HIGHEST, preferred_element_type=f32
    )
    lane = iota((SUB, LANES), 1)
    for direction in range(2):
        for f in range(F):
            base = (direction * F + f) * 4 * SUB
            for half in range(2):
                p = both[base + half * SUB : base + (half + 1) * SUB]
                q = both[base + (2 + half) * SUB : base + (3 + half) * SUB]
                for part in range(2):
                    sign = signs[direction]
                    if part == 0:
                        g = p - sign * roll(q, -2 * SUB)
                    else:
                        g = roll(p, -2 * SUB) + sign * q
                    g = jnp.where(lane < 2 * SUB, g, 0.0)
                    g = pltpu.roll(g, 0, 1, stride=2 * SUB, stride_axis=0)
                    row = jnp.sum(g, axis=0, keepdims=True)
                    at = direction * SUB + f * 4 + part * 2 + (1 - half)
                    gens[at : at + 1] = row


def lists_body(lists, bits):
    count = lists[LMAX]
    low = jnp.zeros(count.shape, jnp.int32)
    high = jnp.zeros(count.shape, jnp.int32)
    half = OFFSETS // 2
    one = jnp.ones(count.shape, jnp.int32)
    for slot in range(LMAX):
        code = lists[slot]
        live = count > slot
        is_low = code < half
        bit = lax.shift_left(one, jnp.where(is_low, code, code - half))
        low = low | jnp.where(live & is_low, bit, 0)
        high = high | jnp.where(live & (code >= half), bit, 0)
    bits[0] = low
    bits[1] = high


def params_body(params, weights, share, columns):
    spot = iota((Q, LANES), 0)
    spot = 2 * SUB * (spot // SUB) + (spot & (SUB - 1))
    values = params[...]
    placed = [
        lax.dot_general(
            values,
            (iota((Q, LANES), 1) == spot + SUB * k).astype(f32),
            (((1,), (0,)), ((), ())),
            precision=HIGHEST,
            preferred_element_type=f32,
        )
        for k in range(2)
    ]
    weights[...] = placed[0][: 2 * F] + placed[1][: 2 * F]
    share[...] = placed[0][2 * F : 2 * F + 1] + placed[1][2 * F + 1 : 2 * F + 2]
    for k in range(2 * F):
        for a1, column in enumerate(to_columns(wide(placed[0][k : k + 1]))[::2]):
            columns[k, SUB * a1 : SUB * (a1 + 1)] = wide(column)


def project(left_mat, right_mat, tables, first, cs, rows, f_out):
    for i in range(rows):
        lanes = pl.ds(i * LANES, LANES)
        right_mat[0:SUB, lanes] = tables[4, i]
        right_mat[SUB : 2 * SUB, lanes] = tables[5, i]
        c1, s1 = tables[first, i], tables[first + 1, i]
        for f in range(F):
            re, im = conj_times((c1, s1), (cs[2 * f, i : i + 1, :], cs[2 * f + 1, i : i + 1, :]))
            left_mat[2 * f * SUB : (2 * f + 1) * SUB, lanes] = re
            left_mat[(2 * f + 1) * SUB : (2 * f + 2) * SUB, lanes] = im
    sums = lax.dot_general(
        left_mat[0 : 4 * SUB], right_mat[...], (((1,), (1,)), ((), ())), precision=HIGHEST, preferred_element_type=f32
    )
    lane = iota((SUB, LANES), 1)
    for f in range(F):
        gr = sums[2 * f * SUB : (2 * f + 1) * SUB]
        gi = sums[(2 * f + 1) * SUB : (2 * f + 2) * SUB]
        re = gr + roll(gi, -SUB)
        im = gi - roll(gr, -SUB)
        packed = jnp.where(lane < SUB, re, jnp.where(lane < 2 * SUB, roll(im, SUB), 0.0))
        packed = pltpu.roll(packed, 0, 1, stride=2 * SUB, stride_axis=0)
        f_out(f, jnp.sum(packed, axis=0, keepdims=True))


def carrier(f, direction, x, y, heights):
    sign = 1 - 2 * direction
    return wave(sign * (1 + 2 * f), x, f - 4, y, 0.3 + 0.2 * f, heights)


def place_ids(rows, cols, first_row, first_col, own_rows):
    d, c = place_of()
    x = d * own_rows + first_row + iota((rows, cols), 0)
    y = c * LANES + first_col + iota((rows, cols), 1)
    return x, y


def halo_rows(rows_a, rows_b):
    even = (lax.axis_index("rng") & 1) == 0
    return jnp.where(even, rows_b[...], rows_a[...]), jnp.where(even, rows_a[...], rows_b[...])


def with_halo(ks, fields, cols_a, cols_b, above, below, inner, edge_l, edge_r):
    rows = fields.shape[1]
    even = (lax.axis_index("xr") & 1) == 0
    edge_l[...] = jnp.zeros(edge_l.shape, f32)
    edge_r[...] = jnp.zeros(edge_r.shape, f32)
    edge_l[TOP : TOP + rows] = jnp.where(even, cols_b[...], cols_a[...])
    edge_r[TOP : TOP + rows] = jnp.where(even, cols_a[...], cols_b[...])
    at = H * N_FIELDS
    edge_l[TOP - H : TOP] = above[at : at + H]
    edge_l[TOP + rows : TOP + rows + H] = below[at : at + H]
    edge_r[TOP - H : TOP] = above[at + H : at + 2 * H]
    edge_r[TOP + rows : TOP + rows + H] = below[at + H : at + 2 * H]
    from_left, from_right = edge_l[...], edge_r[...]
    sides = []
    for i, k in enumerate(ks):
        inner[i] = jnp.zeros(inner.shape[1:], f32)
        inner[i, TOP : TOP + rows] = fields[k]
        inner[i, TOP - H : TOP] = above[H * k : H * (k + 1)]
        inner[i, TOP + rows : TOP + rows + H] = below[H * k : H * (k + 1)]
        sides.append(unpack_columns(from_left, from_right, k))
    return sides


def near_body(
    n_r, n_c, fields, bits, share, cols_b, cols_a, rows_b, rows_a, gens, tables,
    payload, green, source, inner, edge_l, edge_r, moved, cs, left_mat, right_mat, common, halo,
):
    rows = fields.shape[1]
    d, c = place_of()
    above, below = halo_rows(rows_a, rows_b)
    sides = with_halo(range(2 * F + 1), fields, cols_a, cols_b, above, below, inner, edge_l, edge_r)
    for k, side in enumerate(sides):
        middle = inner[k]
        for dy in range(-H, H + 1):
            moved[k * (2 * H + 1) + dy + H] = shifted(middle, side, dy)
    h = fields[2 * F]
    inverse = [fields[2 * F + 1 + k] for k in range(2 * F)]
    incident = [fields[N_FIELDS + k] for k in range(2 * F)]
    low, high = bits[0], bits[1]
    half = OFFSETS // 2
    near = [jnp.zeros((rows, LANES), f32) for _ in range(2 * F)]
    for code in range(OFFSETS):
        dx, dy = offset_of(code)
        window = lambda k: moved[k * (2 * H + 1) + dy + H, TOP + dx : TOP + dx + rows]
        lift = window(2 * F) - h
        squared = float(dx * dx + dy * dy) + lift * lift
        inverse_r = lax.rsqrt(squared)
        r = squared * inverse_r
        bits = low if code < half else high
        there = (bits & (1 << (code % half))) != 0
        size = jnp.where(there, GREEN * inverse_r, 0.0)
        for f in range(F):
            cos, sin = cos_sin(r * (0.25 * (1.0 + 0.25 * f)))
            g = (size * cos, size * sin)
            green[4 * code + 2 * f] = g[0]
            green[4 * code + 2 * f + 1] = g[1]
            got = times(g, (window(2 * f), window(2 * f + 1)))
            near[2 * f] += got[0]
            near[2 * f + 1] += got[1]
    x, y = place_ids(rows, LANES, 0, 0, rows)
    sources = []
    for f in range(F):
        z = (inverse[2 * f], inverse[2 * f + 1])
        s = times(z, (incident[2 * f] - near[2 * f], incident[2 * f + 1] - near[2 * f + 1]))
        sources += s
        source[2 * f] = s[0]
        source[2 * f + 1] = s[1]
        got = conj_times(carrier(f, 0, x, y, h), s)
        cs[2 * f] = got[0]
        cs[2 * f + 1] = got[1]

    def keep(f, row):
        common[2 * SUB + f : 2 * SUB + f + 1] = row

    right_mat[2 * SUB :] = jnp.zeros((right_mat.shape[0] - 2 * SUB, right_mat.shape[1]), f32)
    common[2 * SUB :] = jnp.zeros((SUB, LANES), f32)
    project(left_mat, right_mat, tables, 0, cs, rows, keep)
    common[0 : 2 * SUB] = gens[...]
    common[2 * SUB + 2 : 2 * SUB + 3] = share[...]
    tail = common[2 * SUB : 3 * SUB]
    for direction in range(2):
        part = common[direction * SUB : (direction + 1) * SUB]

        def fill(s, _, part=part, tail=tail):
            payload[s, 0:SUB] = part
            payload[s, SUB : 2 * SUB] = tail
            return 0

        if direction == 0:
            lax.fori_loop(d * n_c, n_r * n_c, fill, 0)
        else:
            lax.fori_loop(0, d * n_c, fill, 0)
    lasts = pack_columns(sources, True)
    firsts = pack_columns(sources, False)
    at = HALO_AT

    def send(dr, dc, put):
        dst = (d + dr) * n_c + c + dc
        ok = (d + dr >= 0) & (d + dr < n_r) & (c + dc >= 0) & (c + dc < n_c)

        @pl.when(ok)
        def _():
            put(dst)

    def rows_to(dr):
        for k in range(2 * F):
            s = sources[k]
            halo[H * k : H * (k + 1)] = s[rows - H :] if dr > 0 else s[:H]
        first, rest = halo[0:SUB], halo[SUB : 2 * F * H]

        def put(dst):
            payload[dst, 0:SUB] = first
            payload[dst, at : at + 2 * F * H - SUB] = rest

        return put

    def cols_to(dc):
        packed = lasts if dc > 0 else firsts
        quarter = rows // 4
        parts = [roll(packed, 4 * SUB * i)[quarter * i : quarter * (i + 1)] for i in range(4)]
        packed = parts[0] + parts[1] + parts[2] + parts[3]

        def put(dst):
            payload[dst, at : at + quarter] = packed

        return put

    def corner_to(dr, dc):
        packed = lasts if dc > 0 else firsts

        def put(dst):
            payload[dst, at : at + H] = packed[rows - H :] if dr > 0 else packed[:H]

        return put

    for dr in (-1, 1):
        send(dr, 0, rows_to(dr))
        send(0, dr, cols_to(dr))
        for dc in (-1, 1):
            send(dr, dc, corner_to(dr, dc))


def toeplitz(gens, late):
    lane = iota((SUB, LANES), 1)
    low = (lane & SUB) == 0
    slid = [slide(wide(gens[k : k + 1])) for k in range(4)]
    re, im = slid[0:2], slid[2:4]
    bases = [
        [jnp.where(low, re[half], -roll(im[half], SUB)) for half in range(2)],
        [jnp.where(low, im[half], roll(re[half], SUB)) for half in range(2)],
    ]
    out = []
    for a1 in range(Q // SUB):
        for first, second in bases:
            tile = jnp.where(lane < LANES - 2 * SUB * a1, first, second)
            out.append(tile if late else roll(tile, 2 * SUB * a1))
    return out


def slide(row):
    return pltpu.roll(row, LANES - SUB, 1, stride=1, stride_axis=0)


TILES = 2 * Q // SUB


def diagonal(k):
    return iota((SUB, LANES), 1) == SUB * k + iota((SUB, LANES), 0)


def to_columns(row):
    return [jnp.sum(jnp.where(diagonal(k), row, 0.0), axis=1, keepdims=True) for k in range(TILES)]


def wide(row):
    return jnp.broadcast_to(row, (SUB, LANES))


def tree_sum(parts):
    while len(parts) > 1:
        parts = [sum(parts[i : i + 2]) for i in range(0, len(parts), 2)]
    return parts[0]


def packed_times(wr, wi, row):
    low = (iota((SUB, LANES), 1) & SUB) == 0
    turned = jnp.where(low, -roll(row, -SUB), roll(row, SUB))
    return wr * row + wi * turned


def column_times(weights, columns, f):
    out = []
    for a1 in range(Q // SUB):
        at = slice(SUB * a1, SUB * (a1 + 1))
        out += times((weights[2 * f, at], weights[2 * f + 1, at]), (columns[2 * a1], columns[2 * a1 + 1]))
    return out


def shares_of(row):
    low = (iota((SUB, LANES), 1) & SUB) == 0
    row = wide(row)
    return jnp.where(low, row, roll(row, SUB)), jnp.where(low, roll(row, -SUB), row)


def row_step(maps, feeds, shares, weights, carry, spread, put, late):
    out = []
    for f in range(F):
        full = feeds[f] if carry is None else carry[f] + feeds[f]
        full = [jnp.where(diagonal(k), full, 0.0) for k in range(TILES)]
        if carry is None:
            put(f, [jnp.zeros((SUB, LANES), f32)] * TILES)
        else:
            amp = spread * packed_times(weights[2 * f], weights[2 * f + 1], carry[f])
            put(f, to_columns(amp))
            turns = [roll(amp, -2 * SUB * a1) if late else amp for a1 in range(Q // SUB)]
            full = [part - tile * turns[k // 2] for k, (part, tile) in enumerate(zip(full, maps(f), strict=True))]
        share = [jnp.sum(jnp.where(diagonal(k), shares[f], 0.0), axis=1, keepdims=True) for k in range(0, TILES, 2)]
        out.append([share[k // 2] * jnp.sum(full[k], axis=1, keepdims=True) for k in range(TILES)])
    return out


def column_step(maps, feeds, shares, columns, carry, spread, put, late):
    out = []
    for f in range(F):
        amp = [spread * part for part in column_times(columns, carry[f], f)]
        put(f, amp)
        tiles = maps(f)
        pairs = [tiles[k] * amp[k] + tiles[k + 1] * amp[k + 1] for k in range(0, TILES, 2)]
        parts = [roll(pair, 2 * SUB * a1) if late else pair for a1, pair in enumerate(pairs)]
        kept = [jnp.where(diagonal(k), carry[f][k], 0.0) for k in range(TILES)]
        total = wide(jnp.sum(tree_sum(kept) - tree_sum(parts), axis=0, keepdims=True))
        out.append(shares[f] * (total + feeds[f]))
    return out


def sweep(n_r, maps, feeds, share, weights, columns, spread, put, late):
    rows = [wide(weights[k : k + 1]) for k in range(2 * F)]

    def pair(j, carry):
        between = row_step(
            lambda f: maps(j, f), feeds(j), shares_of(share(j)), rows, carry, spread, lambda f, v: put(j, f, v),
            late,
        )
        return column_step(
            lambda f: maps(j + 1, f), feeds(j + 1), shares_of(share(j + 1)), columns, between, spread,
            lambda f, v: put(j + 1, f, v), late,
        )

    carry = None
    pairs = (n_r - 1) // 2
    if pairs > 0:
        carry = pair(0, carry)
    if n_r <= SUB:
        for i in range(1, pairs):
            carry = pair(2 * i, carry)
    else:
        carry = lax.fori_loop(1, pairs, lambda i, now: tuple(pair(2 * i, now)), tuple(carry))
    if (n_r - 1) % 2:
        j = n_r - 2
        last = row_step(
            lambda f: maps(j, f), feeds(j), shares_of(share(j)), rows, carry, spread, lambda f, v: put(j, f, v),
            late,
        )
        for f in range(F):
            put(n_r - 1, f, [spread * part for part in column_times(columns, last[f], f)])
    elif carry is not None:
        for f in range(F):
            put(n_r - 1, f, to_columns(spread * packed_times(rows[2 * f], rows[2 * f + 1], carry[f])))


def putter(amps):
    def put(j, f, columns):
        for k, column in enumerate(columns):
            amps[j, f, SUB * k : SUB * (k + 1)] = jnp.broadcast_to(column, (SUB, LANES))

    return put


def laps(n, body):
    if n <= SUB:
        for j in range(n):
            body(j)
    else:
        lax.fori_loop(0, n, lambda j, _: (body(j), 0)[1], 0)


def gens_sum(recv, j, n_c, d, c, step, own):
    total = None
    for k in range(n_c):
        part = recv[j * n_c + k, 0:SUB]
        part = jnp.where((j == d + step) & (k == c), own, part)
        total = part if total is None else total + part
    return total


def powers(base, count):
    out = [None, base]
    for _ in range(2, count):
        out.append(times(out[-1], base))
    return out


MERGED = 5


def merged(middle, side):
    sub = iota((SUB, LANES), 0)
    return [
        jnp.where(sub < H, roll(side[0:SUB], H, 0), middle[0:SUB]),
        middle[SUB : 2 * SUB],
        middle[2 * SUB : 3 * SUB],
        jnp.where(sub >= SUB - H, roll(side[3 * SUB :], -H, 0), middle[3 * SUB :]),
        side[SUB : 2 * SUB] + roll(side[2 * SUB : 3 * SUB], LANES // 2),
    ]


def apart(tiles):
    return [roll(tiles[0], -H, 0), tiles[4], roll(tiles[4], LANES // 2), roll(tiles[3], H, 0)]


def merged_places(rows):
    d, c = place_of()
    sub = iota((SUB, LANES), 0)
    lane = iota((SUB, LANES), 1)
    x0 = d * rows + sub
    y0 = c * LANES + lane
    side = y0 + jnp.where(lane < LANES // 2, LANES, -LANES)
    turned = (lane + LANES // 2) & (LANES - 1)
    side_turned = c * LANES + turned + jnp.where(turned < LANES // 2, LANES, -LANES)
    second = (lane >= LANES // 4) & (lane < 3 * LANES // 4)
    return [
        (jnp.where(sub < H, x0 - H, x0 - SUB), jnp.where(sub < H, side, y0)),
        (x0, y0),
        (x0 + SUB, y0),
        (jnp.where(sub >= SUB - H, x0 + rows - (SUB - H), x0 + rows), jnp.where(sub >= SUB - H, side, y0)),
        (jnp.where(second, x0 + SUB, x0), jnp.where(second, side_turned, side)),
    ]


def store_waves(
    fields, cols_a, cols_b, above, below, loss, first, second, carriers, back_first, back_carriers, inner, edge_l, edge_r
):
    rows = fields.shape[1]
    ks = range(2 * F, N_FIELDS)
    sides = with_halo(ks, fields, cols_a, cols_b, above, below, inner, edge_l, edge_r)
    tiles = [merged(inner[i], side) for i, side in enumerate(sides)]
    for k in range(2 * F):
        for t in range(MERGED):
            loss[t, k] = tiles[1 + k][t]

    def keep(out, t, values):
        for k, value in enumerate(values):
            for part in range(2):
                out[t, k, part] = value[part]

    for t, (x, y) in enumerate(merged_places(rows)):
        h = tiles[0][t]
        keep(first, t, powers(wave(1, x, 0, y, 0.24, h), Q // SUB)[1:])
        keep(second, t, powers(wave(0, x, 1, y, 0.03, h), SUB)[1:])
        keep(carriers, t, [carrier(f, 0, x, y, h) for f in range(F)])
        if t in (1, 2):
            keep(back_first, t - 1, powers(wave(-1, x, 0, y, 0.24, h), Q // SUB)[1:])
            keep(back_carriers, t - 1, [carrier(f, 1, x, y, h) for f in range(F)])


def radiated(amps, at, f, first, second, carriers, t, t_second):
    splat = lambda a: wide(amps[at, f, a : a + 1])
    total = None
    for a1 in range(Q // SUB):
        base = 2 * SUB * a1
        inner = (splat(base), splat(base + SUB))
        for a2 in range(1, SUB):
            u2 = (second[t_second, a2 - 1, 0], second[t_second, a2 - 1, 1])
            got = times((splat(base + a2), splat(base + SUB + a2)), u2)
            inner = (inner[0] + got[0], inner[1] + got[1])
        if a1 == 0:
            total = inner
        else:
            got = times((first[t, a1 - 1, 0], first[t, a1 - 1, 1]), inner)
            total = (total[0] + got[0], total[1] + got[1])
    return times((carriers[t, f, 0], carriers[t, f, 1]), total)


def new_body(
    n_r, n_c, spread, recv, green, source, fields, cols_b, cols_a, rows_b, rows_a, tables, weights, columns,
    forward, driven, payload, second, back_first, back_carriers, below_gens,
    loss, first, carriers, amps, held, inner, moved, edge_l, edge_r, cs, left_mat, right_mat, common, halo,
):
    rows = fields.shape[1]
    d, c = place_of()
    above_rows, below_rows = halo_rows(rows_a, rows_b)
    above = above_rows[GENS_AT:]
    below_gens[...] = below_rows[GENS_AT:]
    store_waves(
        fields, cols_a, cols_b, above_rows, below_rows,
        loss, first, second, carriers, back_first, back_carriers, held, edge_l, edge_r,
    )

    if n_r <= SUB:
        sums = [gens_sum(recv, j, n_c, d, c, -1, above) for j in range(n_r - 1)]

    def maps(j, f):
        gens = sums[j] if n_r <= SUB else gens_sum(recv, j, n_c, d, c, -1, above)
        return toeplitz(gens[4 * f : 4 * f + 4], False)

    def feeds(j):
        feed = recv[j * n_c, SUB : 2 * SUB]
        for k in range(1, n_c):
            feed = feed + recv[j * n_c + k, SUB : 2 * SUB]
        return [wide(feed[f : f + 1]) for f in range(F)]

    sweep(n_r, maps, feeds, lambda j: recv[j * n_c, SUB + 2 : SUB + 3], weights, columns, spread, putter(amps), False)

    at = HALO_AT

    def got(dr, dc, start, size):
        src = jnp.clip(d + dr, 0, n_r - 1) * n_c + jnp.clip(c + dc, 0, n_c - 1)
        ok = (d + dr >= 0) & (d + dr < n_r) & (c + dc >= 0) & (c + dc < n_c)
        return jnp.where(ok, recv[src, start : start + size], 0.0)

    edge_l[...] = jnp.zeros(edge_l.shape, f32)
    edge_r[...] = jnp.zeros(edge_r.shape, f32)
    quarter = rows // 4
    for edge, dc in ((edge_l, -1), (edge_r, 1)):
        side = got(0, dc, at, quarter)
        for i in range(4):
            edge[TOP + quarter * i : TOP + quarter * (i + 1)] = roll(side, -4 * SUB * i)
        edge[TOP - H : TOP] = got(-1, dc, at, H)
        edge[TOP + rows : TOP + rows + H] = got(1, dc, at, H)
    from_left, from_right = edge_l[...], edge_r[...]
    for i, dr in enumerate((-1, 1)):
        halo[i, 0:SUB] = got(dr, 0, 0, SUB)
        halo[i, SUB : 2 * F * H] = got(dr, 0, at, 2 * F * H - SUB)
    for k in range(2 * F):
        inner[k] = jnp.zeros(inner.shape[1:], f32)
        inner[k, TOP : TOP + rows] = source[k]
        inner[k, TOP - H : TOP] = halo[0, H * k : H * (k + 1)]
        inner[k, TOP + rows : TOP + rows + H] = halo[1, H * k : H * (k + 1)]
    sides = [unpack_columns(from_left, from_right, k) for k in range(2 * F)]

    weak = {}
    lost = {}
    for t, step in enumerate((-1, 0, 0, 1, 0)):
        at = jnp.clip(d + step, 0, n_r - 1)
        for f in range(F):
            w = radiated(amps, at, f, first, second, carriers, t, t)
            got = times((loss[t, 2 * f], loss[t, 2 * f + 1]), w)
            for part in range(2):
                weak[t, 2 * f + part] = w[part]
                lost[t, 2 * f + part] = got[part]
    for k in range(2 * F):
        tiles = [lost[t, k] for t in range(MERGED)]
        side = sides[k] - jnp.concatenate(apart(tiles), axis=0)
        middle = inner[k] - jnp.concatenate(tiles[:4], axis=0)
        forward[k] = middle[TOP : TOP + rows]
        for dy in range(-H, H + 1):
            moved[k * (2 * H + 1) + dy + H] = shifted(middle, side, dy)
    near = [jnp.zeros((rows, LANES), f32) for _ in range(2 * F)]
    for code in range(OFFSETS):
        dx, dy = offset_of(code)
        window = lambda k: moved[k * (2 * H + 1) + dy + H, TOP + dx : TOP + dx + rows]
        for f in range(F):
            g = (green[4 * code + 2 * f], green[4 * code + 2 * f + 1])
            add = times(g, (window(2 * f), window(2 * f + 1)))
            near[2 * f] += add[0]
            near[2 * f + 1] += add[1]
    for f in range(F):
        rest = []
        for part in range(2):
            k = 2 * f + part
            w = jnp.concatenate([weak[1, k], weak[2, k]], axis=0)
            rest.append(fields[N_FIELDS + k] - near[k] - w)
        s = times((fields[2 * F + 1 + 2 * f], fields[2 * F + 2 + 2 * f]), rest)
        driven[2 * f] = s[0]
        driven[2 * f + 1] = s[1]
        base = [jnp.concatenate([back_carriers[t, f, part] for t in range(2)], axis=0) for part in range(2)]
        add = conj_times(base, s)
        cs[2 * f] = add[0]
        cs[2 * f + 1] = add[1]

    def keep(f, row):
        common[f : f + 1] = row

    right_mat[2 * SUB :] = jnp.zeros((right_mat.shape[0] - 2 * SUB, right_mat.shape[1]), f32)
    project(left_mat, right_mat, tables, 2, cs, rows, keep)
    pair = common[0:2]

    def fill(s, _):
        payload[s] = pair
        return 0

    lax.fori_loop(0, n_r * n_c, fill, 0)


def last_body(
    n_r, n_c, spread, recv, fed, new, driven, fields, weights, columns, first, second, carriers, below_gens,
    forward, currents, amps,
):
    rows = fields.shape[1]
    d, c = place_of()
    forward[...] = new[...]
    below = below_gens[...]

    def feeds(k):
        j = n_r - 1 - k
        feed = fed[j * n_c]
        for i in range(1, n_c):
            feed = feed + fed[j * n_c + i]
        return [wide(feed[f : f + 1]) for f in range(F)]

    def share(k):
        return recv[(n_r - 1 - k) * n_c, SUB + 2 : SUB + 3]

    def maps(k, f):
        return toeplitz(gens_sum(recv, n_r - 1 - k, n_c, d, c, 1, below)[4 * f : 4 * f + 4], True)

    sweep(n_r, maps, feeds, share, weights, columns, spread, putter(amps), True)
    at = n_r - 1 - d
    for tile in range(rows // SUB):
        rows_at = slice(SUB * tile, SUB * (tile + 1))
        for f in range(F):
            w = radiated(amps, at, f, first, second, carriers, tile, tile + 1)
            lost = times((fields[2 * F + 1 + 2 * f, rows_at], fields[2 * F + 2 + 2 * f, rows_at]), w)
            currents[2 * f, rows_at] = driven[2 * f, rows_at] - lost[0]
            currents[2 * f + 1, rows_at] = driven[2 * f + 1, rows_at] - lost[1]


def swaps(n):
    first = [(i, i ^ 1) for i in range(n) if i ^ 1 < n]
    second = [(i, i + 1) for i in range(1, n - 1, 2)] + [(i + 1, i) for i in range(1, n - 1, 2)]
    return first, second


def swap(axis, n, a, b):
    first, second = swaps(n)
    b = lax.ppermute(b, axis, second)
    return lax.ppermute(a, axis, first), b


def per_device(n_r, n_c, incident, inverse_diag, previous, heights, neighbours, counts, transmit, angle_weights):
    rows, cols = heights.shape
    patches = rows * cols
    spread = 1.0 / math.sqrt(rows * cols * n_c)
    slots = n_r * n_c
    tall = rows + 2 * SUB
    fields = jnp.concatenate([previous, heights[None], inverse_diag, incident])
    cols_b, cols_a = call(columns_body, [(rows, LANES)] * 2, [VMEM], flops=500_000)(fields)
    cols_a, cols_b, transmit, angle_weights = lax.optimization_barrier((cols_a, cols_b, transmit, angle_weights))
    cols_a, cols_b = swap("xr", n_c, cols_a, cols_b)
    tables, gens = call(
        functools.partial(tables_body, n_r),
        [(6, rows, SUB, LANES), (2 * SUB, LANES)],
        [VMEM],
        [pltpu.VMEM((16 * SUB, patches), f32), pltpu.VMEM((16 * SUB, patches), f32)],
    )(fields)
    params = jnp.concatenate([angle_weights.reshape(2 * F, Q), transmit.reshape(F, Q)])
    weights, share, columns = call(
        params_body, [(2 * F, LANES), (1, LANES), (2 * F, Q, LANES)], [VMEM], flops=500_000
    )(params)
    gens, weights, share, columns = lax.optimization_barrier((gens, weights, share, columns))
    rows_b, rows_a = call(rows_body, [(ROWS_SENT, LANES)] * 2, [VMEM] * 4, flops=500_000)(fields, gens, cols_b, cols_a)
    rows_a, rows_b, neighbours, counts = lax.optimization_barrier((rows_a, rows_b, neighbours, counts))
    rows_a, rows_b = swap("rng", n_r, rows_a, rows_b)
    lists = jnp.concatenate([neighbours, counts[None]])
    (bits,) = call(lists_body, [jax.ShapeDtypeStruct((2, rows, LANES), jnp.int32)], [VMEM], flops=500_000)(lists)
    edges = [pltpu.VMEM((tall, LANES), f32)] * 2
    payload, green, source = call(
        functools.partial(near_body, n_r, n_c),
        [(slots, SLOT, LANES), (4 * OFFSETS, rows, LANES), (2 * F, rows, LANES)],
        [VMEM] * 9,
        [
            pltpu.VMEM((2 * F + 1, tall, LANES), f32),
            *edges,
            pltpu.VMEM(((2 * F + 1) * (2 * H + 1), tall, LANES), f32),
            pltpu.VMEM((2 * F, rows, LANES), f32),
            pltpu.VMEM((4 * SUB, patches), f32),
            pltpu.VMEM((16 * SUB, patches), f32),
            pltpu.VMEM((3 * SUB, LANES), f32),
            pltpu.VMEM((2 * SUB, LANES), f32),
        ],
    )(fields, bits, share, cols_b, cols_a, rows_b, rows_a, gens, tables)
    recv = lax.all_to_all(payload, BOTH, 0, 0)
    tile = (2, SUB, LANES)
    new, driven, payload, second, back_first, back_carriers, below_gens = call(
        functools.partial(new_body, n_r, n_c, spread),
        [
            (2 * F, rows, LANES),
            (2 * F, rows, LANES),
            (slots, 2, LANES),
            (MERGED, SUB - 1, *tile),
            (2, Q // SUB - 1, *tile),
            (2, F, *tile),
            (SUB, LANES),
        ],
        [VMEM] * 11,
        [
            pltpu.VMEM((MERGED, 2 * F, SUB, LANES), f32),
            pltpu.VMEM((MERGED, Q // SUB - 1, *tile), f32),
            pltpu.VMEM((MERGED, F, *tile), f32),
            pltpu.VMEM((n_r, F, 2 * Q, LANES), f32),
            pltpu.VMEM((2 * F + 1, tall, LANES), f32),
            pltpu.VMEM((2 * F, tall, LANES), f32),
            pltpu.VMEM((2 * F * (2 * H + 1), tall, LANES), f32),
            *edges,
            pltpu.VMEM((2 * F, rows, LANES), f32),
            pltpu.VMEM((4 * SUB, patches), f32),
            pltpu.VMEM((16 * SUB, patches), f32),
            pltpu.VMEM((SUB, LANES), f32),
            pltpu.VMEM((2, 2 * SUB, LANES), f32),
        ],
    )(recv, green, source, fields, cols_b, cols_a, rows_b, rows_a, tables, weights, columns)
    fed = lax.all_to_all(payload, BOTH, 0, 0)
    return call(
        functools.partial(last_body, n_r, n_c, spread),
        [(2 * F, rows, LANES), (2 * F, rows, LANES)],
        [VMEM] * 11,
        [pltpu.VMEM((n_r, F, 2 * Q, LANES), f32)],
    )(recv, fed, new, driven, fields, weights, columns, back_first, second, back_carriers, below_gens)


def solution(mesh):
    body = functools.partial(per_device, mesh.shape["rng"], mesh.shape["xr"])
    field = P(None, "rng", "xr")
    return jax.shard_map(
        body,
        mesh=mesh,
        in_specs=(field, field, field, P("rng", "xr"), field, P("rng", "xr"), P("rng", None, None), P()),
        out_specs=(field, field),
        check_vma=False,
    )
```

```python
import functools
import math

import jax
import jax.numpy as jnp
from jax import lax
from jax.experimental import pallas as pl
from jax.experimental.pallas import tpu as pltpu
from jax.sharding import PartitionSpec as P

F = 2
Q = 64
H = 3
LMAX = 24
OFFSETS = 48
SUB = 8
LANES = 128
PERIOD = 64
TOP = SUB
GREEN = 0.25
TURN = 2.0 * math.pi
SLOT = 16
HALO_AT = SUB + 3
HIGHEST = lax.Precision.HIGHEST
BOTH = ("rng", "xr")
f32 = jnp.float32


def iota(shape, dim):
    return lax.broadcasted_iota(jnp.int32, shape, dim)


def roll(x, shift, axis=1):
    shift = shift % x.shape[axis]
    return x if shift == 0 else pltpu.roll(x, shift, axis)


def cos_sin(turns):
    quarter = jnp.floor(4.0 * turns + 0.5)
    rest = turns - 0.25 * quarter
    which = quarter.astype(jnp.int32)
    sq = rest * rest
    s = rest * (TURN + sq * (-(TURN**3) / 6 + sq * (TURN**5 / 120 + sq * (-(TURN**7) / 5040 + sq * (TURN**9 / 362880)))))
    c = 1.0 + sq * (-(TURN**2) / 2 + sq * (TURN**4 / 24 + sq * (-(TURN**6) / 720 + sq * (TURN**8 / 40320))))
    odd = (which & 1) == 1
    cos = jnp.where(odd, s, c)
    sin = jnp.where(odd, c, s)
    cos = jnp.where(((which + 1) & 2) == 2, -cos, cos)
    sin = jnp.where((which & 2) == 2, -sin, sin)
    return cos, sin


def times(a, b):
    return a[0] * b[0] - a[1] * b[1], a[0] * b[1] + a[1] * b[0]


def conj_times(a, b):
    return a[0] * b[0] + a[1] * b[1], a[0] * b[1] - a[1] * b[0]


def wave(step_x, x, step_y, y, lift, heights):
    phase = (step_x * x + step_y * y) & (PERIOD - 1)
    return cos_sin(phase.astype(f32) * (1.0 / PERIOD) + (lift / TURN) * heights)


def offset_of(code):
    full = code + (1 if code >= OFFSETS // 2 else 0)
    return full // (2 * H + 1) - H, full % (2 * H + 1) - H


VMEM = pl.BlockSpec(memory_space=pltpu.VMEM)
PLAIN = pl.BlockSpec()


def call(body, out, ins, scratch=(), flops=2_000_000):
    return pl.pallas_call(
        body,
        out_shape=tuple(jax.ShapeDtypeStruct(s, f32) if isinstance(s, tuple) else s for s in out),
        in_specs=list(ins),
        out_specs=tuple(VMEM for _ in out),
        scratch_shapes=list(scratch),
        compiler_params=pltpu.CompilerParams(vmem_limit_bytes=48 * 1024 * 1024),
        cost_estimate=pl.CostEstimate(flops=flops, bytes_accessed=1 << 20, transcendentals=0),
    )


def place_of():
    return lax.axis_index("rng"), lax.axis_index("xr")


def pack_columns(fields, right):
    rows = fields[0].shape[0]
    lane = iota((rows, LANES), 1)
    packed = jnp.zeros((rows, LANES), f32)
    for k, field in enumerate(fields):
        moved = roll(field, H * k - (LANES - H) if right else H * k)
        packed = jnp.where((lane >= H * k) & (lane < H * (k + 1)), moved, packed)
    return packed


def unpack_columns(from_left, from_right, k):
    lane = iota(from_left.shape, 1)
    left = jnp.where(lane >= LANES - H, roll(from_left, LANES - H - H * k), 0.0)
    return jnp.where(lane < H, roll(from_right, -H * k), left)


def shifted(inner, edge, dy):
    if dy == 0:
        return inner
    lane = iota(inner.shape, 1)
    outside = lane >= LANES - dy if dy > 0 else lane < -dy
    return jnp.where(outside, roll(edge, -dy), roll(inner, -dy))


N_FIELDS = 4 * F + 1
ROWS_SENT = 48
GENS_AT = 40


def columns_body(fields, send_b, send_a):
    values = [fields[k] for k in range(N_FIELDS)]
    right = pack_columns(values, True)
    left = pack_columns(values, False)
    even = (lax.axis_index("xr") & 1) == 0
    send_a[...] = jnp.where(even, right, left)
    send_b[...] = jnp.where(even, left, right)


def rows_body(fields, gens, recv_b, recv_a, send_b, send_a):
    d, c = place_of()
    even_c = (c & 1) == 0
    even_r = (d & 1) == 0
    rows = fields.shape[1]
    values = [fields[k] for k in range(N_FIELDS)]
    values.append(jnp.where(even_c, recv_b[...], recv_a[...]))
    values.append(jnp.where(even_c, recv_a[...], recv_b[...]))
    for k, field in enumerate(values):
        last, first = field[rows - H :], field[:H]
        send_a[H * k : H * (k + 1)] = jnp.where(even_r, last, first)
        send_b[H * k : H * (k + 1)] = jnp.where(even_r, first, last)
    used = H * len(values)
    send_a[used:GENS_AT] = jnp.zeros((GENS_AT - used, LANES), f32)
    send_b[used:GENS_AT] = jnp.zeros((GENS_AT - used, LANES), f32)
    down, up = gens[0:SUB], gens[SUB : 2 * SUB]
    send_a[GENS_AT:] = jnp.where(even_r, down, up)
    send_b[GENS_AT:] = jnp.where(even_r, up, down)


def tables_body(n_r, fields, tables, gens, left_mat, right_mat):
    d, c = place_of()
    turned = [d & 1, (n_r - 1 - d) & 1]
    signs = [jnp.where(t == 1, -1.0, 1.0) for t in turned]
    rows = fields.shape[1]
    x0 = d * rows
    y0 = c * LANES
    angle = iota((2 * SUB, LANES), 0) - SUB
    y = iota((2 * SUB, LANES), 1) + y0
    for i in range(rows):
        x = jnp.full((2 * SUB, LANES), x0 + i, jnp.int32)
        lanes = pl.ds(i * LANES, LANES)
        h2 = jnp.broadcast_to(fields[2 * F, i : i + 1, :], (2 * SUB, LANES)) * angle.astype(f32)
        c2, s2 = wave(0, x, angle, y, 0.03, h2)
        tables[4, i] = c2[SUB:]
        tables[5, i] = s2[SUB:]
        right_mat[0 : 2 * SUB, lanes] = c2
        right_mat[2 * SUB : 4 * SUB, lanes] = s2
        for direction in range(2):
            c1, s1 = wave(angle * (1 - 2 * direction), x, 0, y, 0.24, h2)
            tables[2 * direction, i] = c1[SUB:]
            tables[2 * direction + 1, i] = s1[SUB:]
            s1 = signs[direction] * s1
            for f in range(F):
                zr = fields[2 * F + 1 + 2 * f, i : i + 1, :]
                zi = fields[2 * F + 2 + 2 * f, i : i + 1, :]
                base = (direction * F + f) * 4 * SUB
                left_mat[base : base + 2 * SUB, lanes] = zr * c1 - zi * s1
                left_mat[base + 2 * SUB : base + 4 * SUB, lanes] = zr * s1 + zi * c1
    right_mat[4 * SUB :] = jnp.zeros((right_mat.shape[0] - 4 * SUB, right_mat.shape[1]), f32)
    both = lax.dot_general(
        left_mat[...], right_mat[...], (((1,), (1,)), ((), ())), precision=HIGHEST, preferred_element_type=f32
    )
    lane = iota((SUB, LANES), 1)
    for direction in range(2):
        for f in range(F):
            base = (direction * F + f) * 4 * SUB
            for half in range(2):
                p = both[base + half * SUB : base + (half + 1) * SUB]
                q = both[base + (2 + half) * SUB : base + (3 + half) * SUB]
                for part in range(2):
                    sign = signs[direction]
                    if part == 0:
                        g = p - sign * roll(q, -2 * SUB)
                    else:
                        g = roll(p, -2 * SUB) + sign * q
                    g = jnp.where(lane < 2 * SUB, g, 0.0)
                    g = pltpu.roll(g, 0, 1, stride=2 * SUB, stride_axis=0)
                    row = jnp.sum(g, axis=0, keepdims=True)
                    at = direction * SUB + f * 4 + part * 2 + (1 - half)
                    gens[at : at + 1] = row


def list_bits(lists):
    count = lists[LMAX]
    low = jnp.zeros(count.shape, jnp.int32)
    high = jnp.zeros(count.shape, jnp.int32)
    half = OFFSETS // 2
    one = jnp.ones(count.shape, jnp.int32)
    for slot in range(LMAX):
        code = lists[slot]
        live = count > slot
        is_low = code < half
        bit = lax.shift_left(one, jnp.where(is_low, code, code - half))
        low = low | jnp.where(live & is_low, bit, 0)
        high = high | jnp.where(live & (code >= half), bit, 0)
    return low, high


def params_body(params, weights, share, columns):
    spot = iota((Q, LANES), 0)
    spot = 2 * SUB * (spot // SUB) + (spot & (SUB - 1))
    values = params[...]
    placed = [
        lax.dot_general(
            values,
            (iota((Q, LANES), 1) == spot + SUB * k).astype(f32),
            (((1,), (0,)), ((), ())),
            precision=HIGHEST,
            preferred_element_type=f32,
        )
        for k in range(2)
    ]
    weights[...] = placed[0][: 2 * F] + placed[1][: 2 * F]
    share[...] = placed[0][2 * F : 2 * F + 1] + placed[1][2 * F + 1 : 2 * F + 2]
    for k in range(2 * F):
        for a1, column in enumerate(to_columns(wide(placed[0][k : k + 1]))[::2]):
            columns[k, SUB * a1 : SUB * (a1 + 1)] = wide(column)


def project(left_mat, right_mat, tables, first, cs, rows, f_out):
    for i in range(rows):
        lanes = pl.ds(i * LANES, LANES)
        right_mat[0:SUB, lanes] = tables[4, i]
        right_mat[SUB : 2 * SUB, lanes] = tables[5, i]
        c1, s1 = tables[first, i], tables[first + 1, i]
        for f in range(F):
            re, im = conj_times((c1, s1), (cs[2 * f, i : i + 1, :], cs[2 * f + 1, i : i + 1, :]))
            left_mat[2 * f * SUB : (2 * f + 1) * SUB, lanes] = re
            left_mat[(2 * f + 1) * SUB : (2 * f + 2) * SUB, lanes] = im
    sums = lax.dot_general(
        left_mat[0 : 4 * SUB], right_mat[...], (((1,), (1,)), ((), ())), precision=HIGHEST, preferred_element_type=f32
    )
    lane = iota((SUB, LANES), 1)
    for f in range(F):
        gr = sums[2 * f * SUB : (2 * f + 1) * SUB]
        gi = sums[(2 * f + 1) * SUB : (2 * f + 2) * SUB]
        re = gr + roll(gi, -SUB)
        im = gi - roll(gr, -SUB)
        packed = jnp.where(lane < SUB, re, jnp.where(lane < 2 * SUB, roll(im, SUB), 0.0))
        packed = pltpu.roll(packed, 0, 1, stride=2 * SUB, stride_axis=0)
        f_out(f, jnp.sum(packed, axis=0, keepdims=True))


def carrier(f, direction, x, y, heights):
    sign = 1 - 2 * direction
    return wave(sign * (1 + 2 * f), x, f - 4, y, 0.3 + 0.2 * f, heights)


def place_ids(rows, cols, first_row, first_col, own_rows):
    d, c = place_of()
    x = d * own_rows + first_row + iota((rows, cols), 0)
    y = c * LANES + first_col + iota((rows, cols), 1)
    return x, y


def halo_rows(rows_a, rows_b):
    even = (lax.axis_index("rng") & 1) == 0
    return jnp.where(even, rows_b[...], rows_a[...]), jnp.where(even, rows_a[...], rows_b[...])


def with_halo(ks, fields, cols_a, cols_b, above, below, inner, edge_l, edge_r):
    rows = fields.shape[1]
    even = (lax.axis_index("xr") & 1) == 0
    edge_l[...] = jnp.zeros(edge_l.shape, f32)
    edge_r[...] = jnp.zeros(edge_r.shape, f32)
    edge_l[TOP : TOP + rows] = jnp.where(even, cols_b[...], cols_a[...])
    edge_r[TOP : TOP + rows] = jnp.where(even, cols_a[...], cols_b[...])
    at = H * N_FIELDS
    edge_l[TOP - H : TOP] = above[at : at + H]
    edge_l[TOP + rows : TOP + rows + H] = below[at : at + H]
    edge_r[TOP - H : TOP] = above[at + H : at + 2 * H]
    edge_r[TOP + rows : TOP + rows + H] = below[at + H : at + 2 * H]
    from_left, from_right = edge_l[...], edge_r[...]
    sides = []
    for i, k in enumerate(ks):
        inner[i] = jnp.zeros(inner.shape[1:], f32)
        inner[i, TOP : TOP + rows] = fields[k]
        inner[i, TOP - H : TOP] = above[H * k : H * (k + 1)]
        inner[i, TOP + rows : TOP + rows + H] = below[H * k : H * (k + 1)]
        sides.append(unpack_columns(from_left, from_right, k))
    return sides


PAIRS = [(row, beyond) for row in range(H) for beyond in range(H - row)]
SHIFTS = 2 * H + 1


def pair_rows(top, bottom, beyond):
    which = [pair[1 if beyond else 0] for pair in PAIRS]
    rest = jnp.zeros((SUB - len(PAIRS), LANES), top[0].dtype)
    parts = []
    for edge in (top, bottom):
        parts += [edge[i] for i in which] + [rest]
    return jnp.concatenate(parts, axis=0)


def row_list(array, indices):
    return [array[i : i + 1] for i in indices]


def put_pairs(near, spill, k):
    rows = spill.shape[1]
    spill[k] = jnp.zeros(spill.shape[1:], f32)
    for edge in range(2):
        at = SUB * edge
        for row in range(H):
            count = H - row
            total = near[at : at + 1]
            for i in range(1, count):
                total = total + near[at + i : at + i + 1]
            at += count
            to = rows - 1 - row if edge else row
            spill[k, to : to + 1] = total


def coupling(squared, there):
    inverse_r = lax.rsqrt(squared)
    size = jnp.where(there, GREEN * inverse_r, 0.0)
    off = squared * inverse_r * (1.0 / 16.0) - 0.25
    sq = off * off
    w = (-off * polynomial(SINE, sq), polynomial(COSINE, sq))
    fourth = square(square(w))
    out = []
    for power in (fourth, times(fourth, w)):
        out += [size * power[0], size * power[1]]
    return out


def square(a):
    return a[0] * a[0] - a[1] * a[1], 2.0 * a[0] * a[1]


def polynomial(coefficients, x):
    total = coefficients[-1]
    for value in coefficients[-2::-1]:
        total = total * x + value
    return total


SINE = (6.283185280367426, -41.341680722295834, 81.60248507719457, -76.58139539835082, 39.76160778337109)
COSINE = (1.0, -19.739208548909147, 64.93934662883956, -85.4535715937672, 60.144014415422156, -24.982233003994804)


def add_near(near, g, window):
    for f in range(F):
        got = times((g[2 * f], g[2 * f + 1]), (window(2 * f), window(2 * f + 1)))
        near[2 * f] = near[2 * f] + got[0]
        near[2 * f + 1] = near[2 * f + 1] + got[1]


def side_columns(cols_a, cols_b):
    even = (lax.axis_index("xr") & 1) == 0
    return jnp.where(even, cols_b[...], cols_a[...]), jnp.where(even, cols_a[...], cols_b[...])


def store_shifted(moved, k, middle, side):
    rows = middle.shape[0]
    for dy in range(-H, H + 1):
        moved[k * SHIFTS + dy + H, TOP : TOP + rows] = shifted(middle, side, dy)


def inner_body(fields, lists, cols_b, cols_a, green, near_out, bits, moved):
    rows = fields.shape[1]
    low, high = list_bits(lists)
    bits[0] = low
    bits[1] = high
    from_left, from_right = side_columns(cols_a, cols_b)
    for k in range(2 * F + 1):
        for i in range(SHIFTS):
            moved[k * SHIFTS + i, 0:TOP] = jnp.zeros((TOP, LANES), f32)
            moved[k * SHIFTS + i, TOP + rows :] = jnp.zeros((TOP, LANES), f32)
        store_shifted(moved, k, fields[k], unpack_columns(from_left, from_right, k))
    h = fields[2 * F]
    half = OFFSETS // 2
    row = iota((rows, LANES), 0)
    masked = {}
    for dx in range(-H, H + 1):
        inside = (row + dx >= 0) & (row + dx < rows)
        masked[dx] = (jnp.where(inside, low, 0), jnp.where(inside, high, 0))
    near = [jnp.zeros((rows, LANES), f32) for _ in range(2 * F)]
    for code in range(OFFSETS):
        dx, dy = offset_of(code)
        window = lambda k: moved[k * SHIFTS + dy + H, TOP + dx : TOP + dx + rows]
        lift = window(2 * F) - h
        there = (masked[dx][code // half] & (1 << (code % half))) != 0
        g = coupling(float(dx * dx + dy * dy) + lift * lift, there)
        for k in range(2 * F):
            green[4 * code + k] = g[k]
        add_near(near, g, window)
    for k in range(2 * F):
        near_out[k] = near[k]


def near_body(
    n_r, n_c, fields, bits, inner_near, share, cols_b, cols_a, rows_b, rows_a, gens, tables,
    payload, edge_green, source, spill, cs, left_mat, right_mat, common, halo,
):
    rows = fields.shape[1]
    d, c = place_of()
    above, below = halo_rows(rows_a, rows_b)
    backwards = range(H - 1, -1, -1)
    last_rows = range(rows - 1, rows - 1 - H, -1)
    at = H * N_FIELDS
    from_left, from_right = (
        pair_rows(
            row_list(above[at + H * i : at + H * (i + 1)], backwards),
            row_list(below[at + H * i : at + H * (i + 1)], range(H)),
            True,
        )
        for i in range(2)
    )
    h = fields[2 * F]
    inverse = [fields[2 * F + 1 + k] for k in range(2 * F)]
    incident = [fields[N_FIELDS + k] for k in range(2 * F)]
    h_pairs = pair_rows(row_list(h, range(H)), row_list(h, last_rows), False)
    flags = pair_rows(row_list(bits[0], range(H)), row_list(bits[1], last_rows), False)
    row = iota((2 * SUB, LANES), 0)
    lower = row >= SUB
    nth = row & (SUB - 1)
    reach = jnp.zeros((2 * SUB, LANES), jnp.int32)
    for i, (inside, beyond) in enumerate(PAIRS):
        reach = jnp.where(nth == i, inside + beyond + 1, reach)
    first_bit = jnp.where(lower, (H + reach) * SHIFTS + H - 1 - OFFSETS // 2, (H - reach) * SHIFTS + H)
    moved = []
    for k in range(2 * F + 1):
        middle = pair_rows(
            row_list(above[H * k : H * (k + 1)], backwards), row_list(below[H * k : H * (k + 1)], range(H)), True
        )
        side = unpack_columns(from_left, from_right, k)
        moved.append([shifted(middle, side, dy) for dy in range(-H, H + 1)])
    near = [jnp.zeros((2 * SUB, LANES), f32) for _ in range(2 * F)]
    for dy in range(-H, H + 1):
        lift = moved[2 * F][dy + H] - h_pairs
        there = (lax.shift_right_logical(flags, first_bit + dy) & 1) == 1
        g = coupling((reach * reach + dy * dy).astype(f32) + lift * lift, there & (nth < len(PAIRS)))
        for k in range(2 * F):
            edge_green[4 * (dy + H) + k] = g[k]
        add_near(near, g, lambda k: moved[k][dy + H])
    for k in range(2 * F):
        put_pairs(near[k], spill, k)
    near = [inner_near[k] + spill[k] for k in range(2 * F)]
    x, y = place_ids(rows, LANES, 0, 0, rows)
    sources = []
    for f in range(F):
        z = (inverse[2 * f], inverse[2 * f + 1])
        s = times(z, (incident[2 * f] - near[2 * f], incident[2 * f + 1] - near[2 * f + 1]))
        sources += s
        source[2 * f] = s[0]
        source[2 * f + 1] = s[1]
        got = conj_times(carrier(f, 0, x, y, h), s)
        cs[2 * f] = got[0]
        cs[2 * f + 1] = got[1]

    def keep(f, row):
        common[2 * SUB + f : 2 * SUB + f + 1] = row

    right_mat[2 * SUB :] = jnp.zeros((right_mat.shape[0] - 2 * SUB, right_mat.shape[1]), f32)
    common[2 * SUB :] = jnp.zeros((SUB, LANES), f32)
    project(left_mat, right_mat, tables, 0, cs, rows, keep)
    common[0 : 2 * SUB] = gens[...]
    common[2 * SUB + 2 : 2 * SUB + 3] = share[...]
    tail = common[2 * SUB : 3 * SUB]
    for direction in range(2):
        part = common[direction * SUB : (direction + 1) * SUB]

        def fill(s, _, part=part, tail=tail):
            payload[s, 0:SUB] = part
            payload[s, SUB : 2 * SUB] = tail
            return 0

        if direction == 0:
            lax.fori_loop(d * n_c, n_r * n_c, fill, 0)
        else:
            lax.fori_loop(0, d * n_c, fill, 0)
    lasts = pack_columns(sources, True)
    firsts = pack_columns(sources, False)
    at = HALO_AT

    def send(dr, dc, put):
        dst = (d + dr) * n_c + c + dc
        ok = (d + dr >= 0) & (d + dr < n_r) & (c + dc >= 0) & (c + dc < n_c)

        @pl.when(ok)
        def _():
            put(dst)

    def rows_to(dr):
        for k in range(2 * F):
            s = sources[k]
            halo[H * k : H * (k + 1)] = s[rows - H :] if dr > 0 else s[:H]
        first, rest = halo[0:SUB], halo[SUB : 2 * F * H]

        def put(dst):
            payload[dst, 0:SUB] = first
            payload[dst, at : at + 2 * F * H - SUB] = rest

        return put

    def cols_to(dc):
        packed = lasts if dc > 0 else firsts
        quarter = rows // 4
        parts = [roll(packed, 4 * SUB * i)[quarter * i : quarter * (i + 1)] for i in range(4)]
        packed = parts[0] + parts[1] + parts[2] + parts[3]

        def put(dst):
            payload[dst, at : at + quarter] = packed

        return put

    def corner_to(dr, dc):
        packed = lasts if dc > 0 else firsts

        def put(dst):
            payload[dst, at : at + H] = packed[rows - H :] if dr > 0 else packed[:H]

        return put

    for dr in (-1, 1):
        send(dr, 0, rows_to(dr))
        send(0, dr, cols_to(dr))
        for dc in (-1, 1):
            send(dr, dc, corner_to(dr, dc))


def toeplitz(gens, late):
    lane = iota((SUB, LANES), 1)
    low = (lane & SUB) == 0
    slid = [slide(wide(gens[k : k + 1])) for k in range(4)]
    re, im = slid[0:2], slid[2:4]
    bases = [
        [jnp.where(low, re[half], -roll(im[half], SUB)) for half in range(2)],
        [jnp.where(low, im[half], roll(re[half], SUB)) for half in range(2)],
    ]
    out = []
    for a1 in range(Q // SUB):
        for first, second in bases:
            tile = jnp.where(lane < LANES - 2 * SUB * a1, first, second)
            out.append(tile if late else roll(tile, 2 * SUB * a1))
    return out


def slide(row):
    return pltpu.roll(row, LANES - SUB, 1, stride=1, stride_axis=0)


TILES = 2 * Q // SUB


def diagonal(k):
    return iota((SUB, LANES), 1) == SUB * k + iota((SUB, LANES), 0)


def to_columns(row):
    return [jnp.sum(jnp.where(diagonal(k), row, 0.0), axis=1, keepdims=True) for k in range(TILES)]


def wide(row):
    return jnp.broadcast_to(row, (SUB, LANES))


def tree_sum(parts):
    while len(parts) > 1:
        parts = [sum(parts[i : i + 2]) for i in range(0, len(parts), 2)]
    return parts[0]


def packed_times(wr, wi, row):
    low = (iota((SUB, LANES), 1) & SUB) == 0
    turned = jnp.where(low, -roll(row, -SUB), roll(row, SUB))
    return wr * row + wi * turned


def column_times(weights, columns, f):
    out = []
    for a1 in range(Q // SUB):
        at = slice(SUB * a1, SUB * (a1 + 1))
        out += times((weights[2 * f, at], weights[2 * f + 1, at]), (columns[2 * a1], columns[2 * a1 + 1]))
    return out


def shares_of(row):
    low = (iota((SUB, LANES), 1) & SUB) == 0
    row = wide(row)
    return jnp.where(low, row, roll(row, SUB)), jnp.where(low, roll(row, -SUB), row)


def row_step(maps, feeds, shares, weights, carry, spread, put, late):
    out = []
    for f in range(F):
        full = feeds[f] if carry is None else carry[f] + feeds[f]
        full = [jnp.where(diagonal(k), full, 0.0) for k in range(TILES)]
        if carry is None:
            put(f, [jnp.zeros((SUB, LANES), f32)] * TILES)
        else:
            amp = spread * packed_times(weights[2 * f], weights[2 * f + 1], carry[f])
            put(f, to_columns(amp))
            turns = [roll(amp, -2 * SUB * a1) if late else amp for a1 in range(Q // SUB)]
            full = [part - tile * turns[k // 2] for k, (part, tile) in enumerate(zip(full, maps(f), strict=True))]
        share = [jnp.sum(jnp.where(diagonal(k), shares[f], 0.0), axis=1, keepdims=True) for k in range(0, TILES, 2)]
        out.append([share[k // 2] * jnp.sum(full[k], axis=1, keepdims=True) for k in range(TILES)])
    return out


def column_step(maps, feeds, shares, columns, carry, spread, put, late):
    out = []
    for f in range(F):
        amp = [spread * part for part in column_times(columns, carry[f], f)]
        put(f, amp)
        tiles = maps(f)
        pairs = [tiles[k] * amp[k] + tiles[k + 1] * amp[k + 1] for k in range(0, TILES, 2)]
        parts = [roll(pair, 2 * SUB * a1) if late else pair for a1, pair in enumerate(pairs)]
        kept = [jnp.where(diagonal(k), carry[f][k], 0.0) for k in range(TILES)]
        total = wide(jnp.sum(tree_sum(kept) - tree_sum(parts), axis=0, keepdims=True))
        out.append(shares[f] * (total + feeds[f]))
    return out


def sweep(n_r, maps, feeds, share, weights, columns, spread, put, late):
    rows = [wide(weights[k : k + 1]) for k in range(2 * F)]

    def pair(j, carry):
        between = row_step(
            lambda f: maps(j, f), feeds(j), shares_of(share(j)), rows, carry, spread, lambda f, v: put(j, f, v),
            late,
        )
        return column_step(
            lambda f: maps(j + 1, f), feeds(j + 1), shares_of(share(j + 1)), columns, between, spread,
            lambda f, v: put(j + 1, f, v), late,
        )

    carry = None
    pairs = (n_r - 1) // 2
    if pairs > 0:
        carry = pair(0, carry)
    if n_r <= SUB:
        for i in range(1, pairs):
            carry = pair(2 * i, carry)
    else:
        carry = lax.fori_loop(1, pairs, lambda i, now: tuple(pair(2 * i, now)), tuple(carry))
    if (n_r - 1) % 2:
        j = n_r - 2
        last = row_step(
            lambda f: maps(j, f), feeds(j), shares_of(share(j)), rows, carry, spread, lambda f, v: put(j, f, v),
            late,
        )
        for f in range(F):
            put(n_r - 1, f, [spread * part for part in column_times(columns, last[f], f)])
    elif carry is not None:
        for f in range(F):
            put(n_r - 1, f, to_columns(spread * packed_times(rows[2 * f], rows[2 * f + 1], carry[f])))


def putter(amps):
    def put(j, f, columns):
        for k, column in enumerate(columns):
            amps[j, f, SUB * k : SUB * (k + 1)] = jnp.broadcast_to(column, (SUB, LANES))

    return put


def laps(n, body):
    if n <= SUB:
        for j in range(n):
            body(j)
    else:
        lax.fori_loop(0, n, lambda j, _: (body(j), 0)[1], 0)


def gens_sum(recv, j, n_c, d, c, step, own):
    total = None
    for k in range(n_c):
        part = recv[j * n_c + k, 0:SUB]
        part = jnp.where((j == d + step) & (k == c), own, part)
        total = part if total is None else total + part
    return total


def powers(base, count):
    out = [None, base]
    for _ in range(2, count):
        out.append(times(out[-1], base))
    return out


MERGED = 5


def merged(middle, side):
    sub = iota((SUB, LANES), 0)
    return [
        jnp.where(sub < H, roll(side[0:SUB], H, 0), middle[0:SUB]),
        middle[SUB : 2 * SUB],
        middle[2 * SUB : 3 * SUB],
        jnp.where(sub >= SUB - H, roll(side[3 * SUB :], -H, 0), middle[3 * SUB :]),
        side[SUB : 2 * SUB] + roll(side[2 * SUB : 3 * SUB], LANES // 2),
    ]


def apart(tiles):
    return [roll(tiles[0], -H, 0), tiles[4], roll(tiles[4], LANES // 2), roll(tiles[3], H, 0)]


def merged_places(rows):
    d, c = place_of()
    sub = iota((SUB, LANES), 0)
    lane = iota((SUB, LANES), 1)
    x0 = d * rows + sub
    y0 = c * LANES + lane
    side = y0 + jnp.where(lane < LANES // 2, LANES, -LANES)
    turned = (lane + LANES // 2) & (LANES - 1)
    side_turned = c * LANES + turned + jnp.where(turned < LANES // 2, LANES, -LANES)
    second = (lane >= LANES // 4) & (lane < 3 * LANES // 4)
    return [
        (jnp.where(sub < H, x0 - H, x0 - SUB), jnp.where(sub < H, side, y0)),
        (x0, y0),
        (x0 + SUB, y0),
        (jnp.where(sub >= SUB - H, x0 + rows - (SUB - H), x0 + rows), jnp.where(sub >= SUB - H, side, y0)),
        (jnp.where(second, x0 + SUB, x0), jnp.where(second, side_turned, side)),
    ]


def store_waves(
    fields, cols_a, cols_b, above, below, loss, first, second, carriers, back_first, back_carriers, inner, edge_l, edge_r
):
    rows = fields.shape[1]
    ks = range(2 * F, N_FIELDS)
    sides = with_halo(ks, fields, cols_a, cols_b, above, below, inner, edge_l, edge_r)
    tiles = [merged(inner[i], side) for i, side in enumerate(sides)]
    for k in range(2 * F):
        for t in range(MERGED):
            loss[t, k] = tiles[1 + k][t]

    def keep(out, t, values):
        for k, value in enumerate(values):
            for part in range(2):
                out[t, k, part] = value[part]

    for t, (x, y) in enumerate(merged_places(rows)):
        h = tiles[0][t]
        keep(first, t, powers(wave(1, x, 0, y, 0.24, h), Q // SUB)[1:])
        keep(second, t, powers(wave(0, x, 1, y, 0.03, h), SUB)[1:])
        keep(carriers, t, [carrier(f, 0, x, y, h) for f in range(F)])
        if t in (1, 2):
            keep(back_first, t - 1, powers(wave(-1, x, 0, y, 0.24, h), Q // SUB)[1:])
            keep(back_carriers, t - 1, [carrier(f, 1, x, y, h) for f in range(F)])


def radiated(amps, at, f, first, second, carriers, t, t_second):
    splat = lambda a: wide(amps[at, f, a : a + 1])
    total = None
    for a1 in range(Q // SUB):
        base = 2 * SUB * a1
        inner = (splat(base), splat(base + SUB))
        for a2 in range(1, SUB):
            u2 = (second[t_second, a2 - 1, 0], second[t_second, a2 - 1, 1])
            got = times((splat(base + a2), splat(base + SUB + a2)), u2)
            inner = (inner[0] + got[0], inner[1] + got[1])
        if a1 == 0:
            total = inner
        else:
            got = times((first[t, a1 - 1, 0], first[t, a1 - 1, 1]), inner)
            total = (total[0] + got[0], total[1] + got[1])
    return times((carriers[t, f, 0], carriers[t, f, 1]), total)


def new_body(
    n_r, n_c, spread, recv, green, edge_green, source, fields, cols_b, cols_a, rows_b, rows_a, tables, weights, columns,
    forward, driven, payload, second, back_first, back_carriers, below_gens,
    loss, first, carriers, amps, held, inner, moved, edge_l, edge_r, spill, cs, left_mat, right_mat, common, halo,
):
    rows = fields.shape[1]
    d, c = place_of()
    above_rows, below_rows = halo_rows(rows_a, rows_b)
    above = above_rows[GENS_AT:]
    below_gens[...] = below_rows[GENS_AT:]
    store_waves(
        fields, cols_a, cols_b, above_rows, below_rows,
        loss, first, second, carriers, back_first, back_carriers, held, edge_l, edge_r,
    )

    if n_r <= SUB:
        sums = [gens_sum(recv, j, n_c, d, c, -1, above) for j in range(n_r - 1)]

    def maps(j, f):
        gens = sums[j] if n_r <= SUB else gens_sum(recv, j, n_c, d, c, -1, above)
        return toeplitz(gens[4 * f : 4 * f + 4], False)

    def feeds(j):
        feed = recv[j * n_c, SUB : 2 * SUB]
        for k in range(1, n_c):
            feed = feed + recv[j * n_c + k, SUB : 2 * SUB]
        return [wide(feed[f : f + 1]) for f in range(F)]

    sweep(n_r, maps, feeds, lambda j: recv[j * n_c, SUB + 2 : SUB + 3], weights, columns, spread, putter(amps), False)

    at = HALO_AT

    def got(dr, dc, start, size):
        src = jnp.clip(d + dr, 0, n_r - 1) * n_c + jnp.clip(c + dc, 0, n_c - 1)
        ok = (d + dr >= 0) & (d + dr < n_r) & (c + dc >= 0) & (c + dc < n_c)
        return jnp.where(ok, recv[src, start : start + size], 0.0)

    edge_l[...] = jnp.zeros(edge_l.shape, f32)
    edge_r[...] = jnp.zeros(edge_r.shape, f32)
    quarter = rows // 4
    for edge, dc in ((edge_l, -1), (edge_r, 1)):
        side = got(0, dc, at, quarter)
        for i in range(4):
            edge[TOP + quarter * i : TOP + quarter * (i + 1)] = roll(side, -4 * SUB * i)
        edge[TOP - H : TOP] = got(-1, dc, at, H)
        edge[TOP + rows : TOP + rows + H] = got(1, dc, at, H)
    from_left, from_right = edge_l[...], edge_r[...]
    for i, dr in enumerate((-1, 1)):
        halo[i, 0:SUB] = got(dr, 0, 0, SUB)
        halo[i, SUB : 2 * F * H] = got(dr, 0, at, 2 * F * H - SUB)
    for k in range(2 * F):
        inner[k] = jnp.zeros(inner.shape[1:], f32)
        inner[k, TOP : TOP + rows] = source[k]
        inner[k, TOP - H : TOP] = halo[0, H * k : H * (k + 1)]
        inner[k, TOP + rows : TOP + rows + H] = halo[1, H * k : H * (k + 1)]
    sides = [unpack_columns(from_left, from_right, k) for k in range(2 * F)]

    weak = {}
    lost = {}
    for t, step in enumerate((-1, 0, 0, 1, 0)):
        at = jnp.clip(d + step, 0, n_r - 1)
        for f in range(F):
            w = radiated(amps, at, f, first, second, carriers, t, t)
            got = times((loss[t, 2 * f], loss[t, 2 * f + 1]), w)
            for part in range(2):
                weak[t, 2 * f + part] = w[part]
                lost[t, 2 * f + part] = got[part]
    beyond = []
    for k in range(2 * F):
        tiles = [lost[t, k] for t in range(MERGED)]
        side = sides[k] - jnp.concatenate(apart(tiles), axis=0)
        middle = inner[k] - jnp.concatenate(tiles[:4], axis=0)
        forward[k] = middle[TOP : TOP + rows]
        for i in range(SHIFTS):
            moved[k * SHIFTS + i, 0:TOP] = jnp.zeros((TOP, LANES), f32)
            moved[k * SHIFTS + i, TOP + rows :] = jnp.zeros((TOP, LANES), f32)
        store_shifted(moved, k, middle[TOP : TOP + rows], side[TOP : TOP + rows])
        above_edge = range(TOP - 1, TOP - 1 - H, -1)
        below_edge = range(TOP + rows, TOP + rows + H)
        pairs = [pair_rows(row_list(part, above_edge), row_list(part, below_edge), True) for part in (middle, side)]
        beyond.append([shifted(*pairs, dy) for dy in range(-H, H + 1)])
    near = [jnp.zeros((2 * SUB, LANES), f32) for _ in range(2 * F)]
    for dy in range(-H, H + 1):
        add_near(near, [edge_green[4 * (dy + H) + k] for k in range(2 * F)], lambda k: beyond[k][dy + H])
    for k in range(2 * F):
        put_pairs(near[k], spill, k)
    near = [spill[k] for k in range(2 * F)]
    for code in range(OFFSETS):
        dx, dy = offset_of(code)
        add_near(
            near,
            [green[4 * code + k] for k in range(2 * F)],
            lambda k: moved[k * SHIFTS + dy + H, TOP + dx : TOP + dx + rows],
        )
    for f in range(F):
        rest = []
        for part in range(2):
            k = 2 * f + part
            w = jnp.concatenate([weak[1, k], weak[2, k]], axis=0)
            rest.append(fields[N_FIELDS + k] - near[k] - w)
        s = times((fields[2 * F + 1 + 2 * f], fields[2 * F + 2 + 2 * f]), rest)
        driven[2 * f] = s[0]
        driven[2 * f + 1] = s[1]
        base = [jnp.concatenate([back_carriers[t, f, part] for t in range(2)], axis=0) for part in range(2)]
        add = conj_times(base, s)
        cs[2 * f] = add[0]
        cs[2 * f + 1] = add[1]

    def keep(f, row):
        common[f : f + 1] = row

    right_mat[2 * SUB :] = jnp.zeros((right_mat.shape[0] - 2 * SUB, right_mat.shape[1]), f32)
    project(left_mat, right_mat, tables, 2, cs, rows, keep)
    pair = common[0:2]

    def fill(s, _):
        payload[s] = pair
        return 0

    lax.fori_loop(0, n_r * n_c, fill, 0)


def last_body(
    n_r, n_c, spread, recv, fed, new, driven, fields, weights, columns, first, second, carriers, below_gens,
    forward, currents, amps,
):
    rows = fields.shape[1]
    d, c = place_of()
    forward[...] = new[...]
    below = below_gens[...]

    def feeds(k):
        j = n_r - 1 - k
        feed = fed[j * n_c]
        for i in range(1, n_c):
            feed = feed + fed[j * n_c + i]
        return [wide(feed[f : f + 1]) for f in range(F)]

    def share(k):
        return recv[(n_r - 1 - k) * n_c, SUB + 2 : SUB + 3]

    def maps(k, f):
        return toeplitz(gens_sum(recv, n_r - 1 - k, n_c, d, c, 1, below)[4 * f : 4 * f + 4], True)

    sweep(n_r, maps, feeds, share, weights, columns, spread, putter(amps), True)
    at = n_r - 1 - d
    for tile in range(rows // SUB):
        rows_at = slice(SUB * tile, SUB * (tile + 1))
        for f in range(F):
            w = radiated(amps, at, f, first, second, carriers, tile, tile + 1)
            lost = times((fields[2 * F + 1 + 2 * f, rows_at], fields[2 * F + 2 + 2 * f, rows_at]), w)
            currents[2 * f, rows_at] = driven[2 * f, rows_at] - lost[0]
            currents[2 * f + 1, rows_at] = driven[2 * f + 1, rows_at] - lost[1]


def swaps(n):
    first = [(i, i ^ 1) for i in range(n) if i ^ 1 < n]
    second = [(i, i + 1) for i in range(1, n - 1, 2)] + [(i + 1, i) for i in range(1, n - 1, 2)]
    return first, second


def swap(axis, n, a, b):
    first, second = swaps(n)
    b = lax.ppermute(b, axis, second)
    return lax.ppermute(a, axis, first), b


def per_device(n_r, n_c, incident, inverse_diag, previous, heights, neighbours, counts, transmit, angle_weights):
    rows, cols = heights.shape
    patches = rows * cols
    spread = 1.0 / math.sqrt(rows * cols * n_c)
    slots = n_r * n_c
    tall = rows + 2 * SUB
    fields = jnp.concatenate([previous, heights[None], inverse_diag, incident])
    cols_b, cols_a = call(columns_body, [(rows, LANES)] * 2, [VMEM], flops=500_000)(fields)
    cols_a, cols_b, transmit, angle_weights = lax.optimization_barrier((cols_a, cols_b, transmit, angle_weights))
    cols_a, cols_b = swap("xr", n_c, cols_a, cols_b)
    tables, gens = call(
        functools.partial(tables_body, n_r),
        [(6, rows, SUB, LANES), (2 * SUB, LANES)],
        [VMEM],
        [pltpu.VMEM((16 * SUB, patches), f32), pltpu.VMEM((16 * SUB, patches), f32)],
    )(fields)
    params = jnp.concatenate([angle_weights.reshape(2 * F, Q), transmit.reshape(F, Q)])
    weights, share, columns = call(
        params_body, [(2 * F, LANES), (1, LANES), (2 * F, Q, LANES)], [VMEM], flops=500_000
    )(params)
    gens, weights, share, columns = lax.optimization_barrier((gens, weights, share, columns))
    rows_b, rows_a = call(rows_body, [(ROWS_SENT, LANES)] * 2, [VMEM] * 4, flops=500_000)(fields, gens, cols_b, cols_a)
    rows_a, rows_b, neighbours, counts = lax.optimization_barrier((rows_a, rows_b, neighbours, counts))
    rows_a, rows_b = swap("rng", n_r, rows_a, rows_b)
    lists = jnp.concatenate([neighbours, counts[None]])
    green, inner_near, bits = call(
        inner_body,
        [
            (4 * OFFSETS, rows, LANES),
            (2 * F, rows, LANES),
            jax.ShapeDtypeStruct((2, rows, LANES), jnp.int32),
        ],
        [VMEM] * 4,
        [pltpu.VMEM(((2 * F + 1) * SHIFTS, tall, LANES), f32)],
        500_000,
    )(fields, lists, cols_b, cols_a)
    edges = [pltpu.VMEM((tall, LANES), f32)] * 2
    payload, edge_green, source = call(
        functools.partial(near_body, n_r, n_c),
        [(slots, SLOT, LANES), (4 * SHIFTS, 2 * SUB, LANES), (2 * F, rows, LANES)],
        [VMEM] * 10,
        [
            pltpu.VMEM((2 * F, rows, LANES), f32),
            pltpu.VMEM((2 * F, rows, LANES), f32),
            pltpu.VMEM((4 * SUB, patches), f32),
            pltpu.VMEM((16 * SUB, patches), f32),
            pltpu.VMEM((3 * SUB, LANES), f32),
            pltpu.VMEM((2 * SUB, LANES), f32),
        ],
    )(fields, bits, inner_near, share, cols_b, cols_a, rows_b, rows_a, gens, tables)
    recv = lax.all_to_all(payload, BOTH, 0, 0)
    tile = (2, SUB, LANES)
    new, driven, payload, second, back_first, back_carriers, below_gens = call(
        functools.partial(new_body, n_r, n_c, spread),
        [
            (2 * F, rows, LANES),
            (2 * F, rows, LANES),
            (slots, 2, LANES),
            (MERGED, SUB - 1, *tile),
            (2, Q // SUB - 1, *tile),
            (2, F, *tile),
            (SUB, LANES),
        ],
        [VMEM] * 12,
        [
            pltpu.VMEM((MERGED, 2 * F, SUB, LANES), f32),
            pltpu.VMEM((MERGED, Q // SUB - 1, *tile), f32),
            pltpu.VMEM((MERGED, F, *tile), f32),
            pltpu.VMEM((n_r, F, 2 * Q, LANES), f32),
            pltpu.VMEM((2 * F + 1, tall, LANES), f32),
            pltpu.VMEM((2 * F, tall, LANES), f32),
            pltpu.VMEM((2 * F * (2 * H + 1), tall, LANES), f32),
            *edges,
            pltpu.VMEM((2 * F, rows, LANES), f32),
            pltpu.VMEM((2 * F, rows, LANES), f32),
            pltpu.VMEM((4 * SUB, patches), f32),
            pltpu.VMEM((16 * SUB, patches), f32),
            pltpu.VMEM((SUB, LANES), f32),
            pltpu.VMEM((2, 2 * SUB, LANES), f32),
        ],
    )(recv, green, edge_green, source, fields, cols_b, cols_a, rows_b, rows_a, tables, weights, columns)
    fed = lax.all_to_all(payload, BOTH, 0, 0)
    return call(
        functools.partial(last_body, n_r, n_c, spread),
        [(2 * F, rows, LANES), (2 * F, rows, LANES)],
        [VMEM] * 11,
        [pltpu.VMEM((n_r, F, 2 * Q, LANES), f32)],
    )(recv, fed, new, driven, fields, weights, columns, back_first, second, back_carriers, below_gens)


def solution(mesh):
    body = functools.partial(per_device, mesh.shape["rng"], mesh.shape["xr"])
    field = P(None, "rng", "xr")
    return jax.shard_map(
        body,
        mesh=mesh,
        in_specs=(field, field, field, P("rng", "xr"), field, P("rng", "xr"), P("rng", None, None), P()),
        out_specs=(field, field),
        check_vma=False,
    )
```

```python
import functools
import math

import jax
import jax.numpy as jnp
from jax import lax
from jax.experimental import pallas as pl
from jax.experimental.pallas import tpu as pltpu
from jax.sharding import PartitionSpec as P

F = 2
Q = 64
H = 3
LMAX = 24
OFFSETS = 48
SUB = 8
LANES = 128
PERIOD = 64
TOP = SUB
GREEN = 0.25
TURN = 2.0 * math.pi
SLOT = 16
HALO_AT = SUB + 3
HIGHEST = lax.Precision.HIGHEST
BOTH = ("rng", "xr")
f32 = jnp.float32


def iota(shape, dim):
    return lax.broadcasted_iota(jnp.int32, shape, dim)


def roll(x, shift, axis=1):
    shift = shift % x.shape[axis]
    return x if shift == 0 else pltpu.roll(x, shift, axis)


def cos_sin(turns):
    quarter = jnp.floor(4.0 * turns + 0.5)
    rest = turns - 0.25 * quarter
    which = quarter.astype(jnp.int32)
    sq = rest * rest
    s = rest * (TURN + sq * (-(TURN**3) / 6 + sq * (TURN**5 / 120 + sq * (-(TURN**7) / 5040 + sq * (TURN**9 / 362880)))))
    c = 1.0 + sq * (-(TURN**2) / 2 + sq * (TURN**4 / 24 + sq * (-(TURN**6) / 720 + sq * (TURN**8 / 40320))))
    odd = (which & 1) == 1
    cos = jnp.where(odd, s, c)
    sin = jnp.where(odd, c, s)
    cos = jnp.where(((which + 1) & 2) == 2, -cos, cos)
    sin = jnp.where((which & 2) == 2, -sin, sin)
    return cos, sin


def times(a, b):
    return a[0] * b[0] - a[1] * b[1], a[0] * b[1] + a[1] * b[0]


def conj_times(a, b):
    return a[0] * b[0] + a[1] * b[1], a[0] * b[1] - a[1] * b[0]


def wave(step_x, x, step_y, y, lift, heights):
    phase = (step_x * x + step_y * y) & (PERIOD - 1)
    return cos_sin(phase.astype(f32) * (1.0 / PERIOD) + (lift / TURN) * heights)


def offset_of(code):
    full = code + (1 if code >= OFFSETS // 2 else 0)
    return full // (2 * H + 1) - H, full % (2 * H + 1) - H


VMEM = pl.BlockSpec(memory_space=pltpu.VMEM)
PLAIN = pl.BlockSpec()


def call(body, out, ins, scratch=(), flops=2_000_000):
    return pl.pallas_call(
        body,
        out_shape=tuple(jax.ShapeDtypeStruct(s, f32) if isinstance(s, tuple) else s for s in out),
        in_specs=list(ins),
        out_specs=tuple(VMEM for _ in out),
        scratch_shapes=list(scratch),
        compiler_params=pltpu.CompilerParams(vmem_limit_bytes=48 * 1024 * 1024),
        cost_estimate=pl.CostEstimate(flops=flops, bytes_accessed=1 << 20, transcendentals=0),
    )


def place_of():
    return lax.axis_index("rng"), lax.axis_index("xr")


def pack_columns(fields, right):
    rows = fields[0].shape[0]
    lane = iota((rows, LANES), 1)
    packed = jnp.zeros((rows, LANES), f32)
    for k, field in enumerate(fields):
        moved = roll(field, H * k - (LANES - H) if right else H * k)
        packed = jnp.where((lane >= H * k) & (lane < H * (k + 1)), moved, packed)
    return packed


def unpack_columns(from_left, from_right, k):
    lane = iota(from_left.shape, 1)
    left = jnp.where(lane >= LANES - H, roll(from_left, LANES - H - H * k), 0.0)
    return jnp.where(lane < H, roll(from_right, -H * k), left)


def shifted(inner, edge, dy):
    if dy == 0:
        return inner
    lane = iota(inner.shape, 1)
    outside = lane >= LANES - dy if dy > 0 else lane < -dy
    return jnp.where(outside, roll(edge, -dy), roll(inner, -dy))


N_FIELDS = 4 * F + 1
ROWS_SENT = 48
GENS_AT = 40


def columns_body(fields, send_b, send_a):
    values = [fields[k] for k in range(N_FIELDS)]
    right = pack_columns(values, True)
    left = pack_columns(values, False)
    even = (lax.axis_index("xr") & 1) == 0
    send_a[...] = jnp.where(even, right, left)
    send_b[...] = jnp.where(even, left, right)


def rows_body(fields, gens, recv_b, recv_a, send_b, send_a):
    d, c = place_of()
    even_c = (c & 1) == 0
    even_r = (d & 1) == 0
    rows = fields.shape[1]
    values = [fields[k] for k in range(N_FIELDS)]
    values.append(jnp.where(even_c, recv_b[...], recv_a[...]))
    values.append(jnp.where(even_c, recv_a[...], recv_b[...]))
    for k, field in enumerate(values):
        last, first = field[rows - H :], field[:H]
        send_a[H * k : H * (k + 1)] = jnp.where(even_r, last, first)
        send_b[H * k : H * (k + 1)] = jnp.where(even_r, first, last)
    used = H * len(values)
    send_a[used:GENS_AT] = jnp.zeros((GENS_AT - used, LANES), f32)
    send_b[used:GENS_AT] = jnp.zeros((GENS_AT - used, LANES), f32)
    down, up = gens[0:SUB], gens[SUB : 2 * SUB]
    send_a[GENS_AT:] = jnp.where(even_r, down, up)
    send_b[GENS_AT:] = jnp.where(even_r, up, down)


def tables_body(n_r, fields, tables, gens, left_mat, right_mat):
    d, c = place_of()
    turned = [d & 1, (n_r - 1 - d) & 1]
    signs = [jnp.where(t == 1, -1.0, 1.0) for t in turned]
    rows = fields.shape[1]
    x0 = d * rows
    y0 = c * LANES
    angle = iota((2 * SUB, LANES), 0) - SUB
    y = iota((2 * SUB, LANES), 1) + y0
    for i in range(rows):
        x = jnp.full((2 * SUB, LANES), x0 + i, jnp.int32)
        lanes = pl.ds(i * LANES, LANES)
        h2 = jnp.broadcast_to(fields[2 * F, i : i + 1, :], (2 * SUB, LANES)) * angle.astype(f32)
        c2, s2 = wave(0, x, angle, y, 0.03, h2)
        tables[4, i] = c2[SUB:]
        tables[5, i] = s2[SUB:]
        right_mat[0 : 2 * SUB, lanes] = c2
        right_mat[2 * SUB : 4 * SUB, lanes] = s2
        for direction in range(2):
            c1, s1 = wave(angle * (1 - 2 * direction), x, 0, y, 0.24, h2)
            tables[2 * direction, i] = c1[SUB:]
            tables[2 * direction + 1, i] = s1[SUB:]
            s1 = signs[direction] * s1
            for f in range(F):
                zr = fields[2 * F + 1 + 2 * f, i : i + 1, :]
                zi = fields[2 * F + 2 + 2 * f, i : i + 1, :]
                base = (direction * F + f) * 4 * SUB
                left_mat[base : base + 2 * SUB, lanes] = zr * c1 - zi * s1
                left_mat[base + 2 * SUB : base + 4 * SUB, lanes] = zr * s1 + zi * c1
    right_mat[4 * SUB :] = jnp.zeros((right_mat.shape[0] - 4 * SUB, right_mat.shape[1]), f32)
    both = lax.dot_general(
        left_mat[...], right_mat[...], (((1,), (1,)), ((), ())), precision=HIGHEST, preferred_element_type=f32
    )
    lane = iota((SUB, LANES), 1)
    for direction in range(2):
        for f in range(F):
            base = (direction * F + f) * 4 * SUB
            for half in range(2):
                p = both[base + half * SUB : base + (half + 1) * SUB]
                q = both[base + (2 + half) * SUB : base + (3 + half) * SUB]
                for part in range(2):
                    sign = signs[direction]
                    if part == 0:
                        g = p - sign * roll(q, -2 * SUB)
                    else:
                        g = roll(p, -2 * SUB) + sign * q
                    g = jnp.where(lane < 2 * SUB, g, 0.0)
                    g = pltpu.roll(g, 0, 1, stride=2 * SUB, stride_axis=0)
                    row = jnp.sum(g, axis=0, keepdims=True)
                    at = direction * SUB + f * 4 + part * 2 + (1 - half)
                    gens[at : at + 1] = row


def list_bits(lists):
    count = lists[LMAX]
    low = jnp.zeros(count.shape, jnp.int32)
    high = jnp.zeros(count.shape, jnp.int32)
    half = OFFSETS // 2
    one = jnp.ones(count.shape, jnp.int32)
    for slot in range(LMAX):
        code = lists[slot]
        live = count > slot
        is_low = code < half
        bit = lax.shift_left(one, jnp.where(is_low, code, code - half))
        low = low | jnp.where(live & is_low, bit, 0)
        high = high | jnp.where(live & (code >= half), bit, 0)
    return low, high


def params_body(fields, weights, share, columns):
    spot = iota((LANES, LANES), 0)
    spot = jnp.where(spot < Q, 2 * SUB * (spot // SUB) + (spot & (SUB - 1)), 2 * LANES)
    base = N_FIELDS + 2 * F
    values = jnp.concatenate([fields[base + i, 0:2] for i in range(F + 1)] + [fields[base + F, 2:4]], axis=0)
    placed = [
        lax.dot_general(
            values,
            (iota((LANES, LANES), 1) == spot + SUB * k).astype(f32),
            (((1,), (0,)), ((), ())),
            precision=HIGHEST,
            preferred_element_type=f32,
        )
        for k in range(2)
    ]
    weights[...] = placed[0][: 2 * F] + placed[1][: 2 * F]
    share[...] = placed[0][2 * F : 2 * F + 1] + placed[1][2 * F + 1 : 2 * F + 2]
    for k in range(2 * F):
        for a1, column in enumerate(to_columns(wide(placed[0][k : k + 1]))[::2]):
            columns[k, SUB * a1 : SUB * (a1 + 1)] = wide(column)


def project(left_mat, right_mat, tables, first, cs, rows, f_out):
    for i in range(rows):
        lanes = pl.ds(i * LANES, LANES)
        right_mat[0:SUB, lanes] = tables[4, i]
        right_mat[SUB : 2 * SUB, lanes] = tables[5, i]
        c1, s1 = tables[first, i], tables[first + 1, i]
        for f in range(F):
            re, im = conj_times((c1, s1), (cs[2 * f, i : i + 1, :], cs[2 * f + 1, i : i + 1, :]))
            left_mat[2 * f * SUB : (2 * f + 1) * SUB, lanes] = re
            left_mat[(2 * f + 1) * SUB : (2 * f + 2) * SUB, lanes] = im
    sums = lax.dot_general(
        left_mat[0 : 4 * SUB], right_mat[...], (((1,), (1,)), ((), ())), precision=HIGHEST, preferred_element_type=f32
    )
    lane = iota((SUB, LANES), 1)
    for f in range(F):
        gr = sums[2 * f * SUB : (2 * f + 1) * SUB]
        gi = sums[(2 * f + 1) * SUB : (2 * f + 2) * SUB]
        re = gr + roll(gi, -SUB)
        im = gi - roll(gr, -SUB)
        packed = jnp.where(lane < SUB, re, jnp.where(lane < 2 * SUB, roll(im, SUB), 0.0))
        packed = pltpu.roll(packed, 0, 1, stride=2 * SUB, stride_axis=0)
        f_out(f, jnp.sum(packed, axis=0, keepdims=True))


def carrier(f, direction, x, y, heights):
    sign = 1 - 2 * direction
    return wave(sign * (1 + 2 * f), x, f - 4, y, 0.3 + 0.2 * f, heights)


def place_ids(rows, cols, first_row, first_col, own_rows):
    d, c = place_of()
    x = d * own_rows + first_row + iota((rows, cols), 0)
    y = c * LANES + first_col + iota((rows, cols), 1)
    return x, y


def halo_rows(rows_a, rows_b):
    even = (lax.axis_index("rng") & 1) == 0
    return jnp.where(even, rows_b[...], rows_a[...]), jnp.where(even, rows_a[...], rows_b[...])


def with_halo(ks, fields, cols_a, cols_b, above, below, inner, edge_l, edge_r):
    rows = fields.shape[1]
    even = (lax.axis_index("xr") & 1) == 0
    edge_l[...] = jnp.zeros(edge_l.shape, f32)
    edge_r[...] = jnp.zeros(edge_r.shape, f32)
    edge_l[TOP : TOP + rows] = jnp.where(even, cols_b[...], cols_a[...])
    edge_r[TOP : TOP + rows] = jnp.where(even, cols_a[...], cols_b[...])
    at = H * N_FIELDS
    edge_l[TOP - H : TOP] = above[at : at + H]
    edge_l[TOP + rows : TOP + rows + H] = below[at : at + H]
    edge_r[TOP - H : TOP] = above[at + H : at + 2 * H]
    edge_r[TOP + rows : TOP + rows + H] = below[at + H : at + 2 * H]
    from_left, from_right = edge_l[...], edge_r[...]
    sides = []
    for i, k in enumerate(ks):
        inner[i] = jnp.zeros(inner.shape[1:], f32)
        inner[i, TOP : TOP + rows] = fields[k]
        inner[i, TOP - H : TOP] = above[H * k : H * (k + 1)]
        inner[i, TOP + rows : TOP + rows + H] = below[H * k : H * (k + 1)]
        sides.append(unpack_columns(from_left, from_right, k))
    return sides


PAIRS = [(row, beyond) for row in range(H) for beyond in range(H - row)]
SHIFTS = 2 * H + 1


def pair_rows(top, bottom, beyond):
    which = [pair[1 if beyond else 0] for pair in PAIRS]
    rest = jnp.zeros((SUB - len(PAIRS), LANES), top[0].dtype)
    parts = []
    for edge in (top, bottom):
        parts += [edge[i] for i in which] + [rest]
    return jnp.concatenate(parts, axis=0)


def row_list(array, indices):
    return [array[i : i + 1] for i in indices]


def put_pairs(near, spill, k):
    rows = spill.shape[1]
    spill[k] = jnp.zeros(spill.shape[1:], f32)
    for edge in range(2):
        at = SUB * edge
        for row in range(H):
            count = H - row
            total = near[at : at + 1]
            for i in range(1, count):
                total = total + near[at + i : at + i + 1]
            at += count
            to = rows - 1 - row if edge else row
            spill[k, to : to + 1] = total


def coupling(squared, there):
    inverse_r = lax.rsqrt(squared)
    size = jnp.where(there, GREEN * inverse_r, 0.0)
    off = squared * inverse_r * (1.0 / 16.0) - 0.25
    sq = off * off
    w = (-off * polynomial(SINE, sq), polynomial(COSINE, sq))
    fourth = square(square(w))
    out = []
    for power in (fourth, times(fourth, w)):
        out += [size * power[0], size * power[1]]
    return out


def square(a):
    return a[0] * a[0] - a[1] * a[1], 2.0 * a[0] * a[1]


def polynomial(coefficients, x):
    total = coefficients[-1]
    for value in coefficients[-2::-1]:
        total = total * x + value
    return total


SINE = (6.283185280367426, -41.341680722295834, 81.60248507719457, -76.58139539835082, 39.76160778337109)
COSINE = (1.0, -19.739208548909147, 64.93934662883956, -85.4535715937672, 60.144014415422156, -24.982233003994804)


def add_near(near, g, window):
    for f in range(F):
        got = times((g[2 * f], g[2 * f + 1]), (window(2 * f), window(2 * f + 1)))
        near[2 * f] = near[2 * f] + got[0]
        near[2 * f + 1] = near[2 * f + 1] + got[1]


def side_columns(cols_a, cols_b):
    even = (lax.axis_index("xr") & 1) == 0
    return jnp.where(even, cols_b[...], cols_a[...]), jnp.where(even, cols_a[...], cols_b[...])


def store_shifted(moved, k, middle, side):
    rows = middle.shape[0]
    for dy in range(-H, H + 1):
        moved[k * SHIFTS + dy + H, TOP : TOP + rows] = shifted(middle, side, dy)


def inner_body(fields, lists, cols_b, cols_a, green, near_out, bits, moved):
    rows = fields.shape[1]
    low, high = list_bits(lists)
    bits[0] = low
    bits[1] = high
    from_left, from_right = side_columns(cols_a, cols_b)
    for k in range(2 * F + 1):
        for i in range(SHIFTS):
            moved[k * SHIFTS + i, 0:TOP] = jnp.zeros((TOP, LANES), f32)
            moved[k * SHIFTS + i, TOP + rows :] = jnp.zeros((TOP, LANES), f32)
        store_shifted(moved, k, fields[k], unpack_columns(from_left, from_right, k))
    h = fields[2 * F]
    half = OFFSETS // 2
    row = iota((rows, LANES), 0)
    masked = {}
    for dx in range(-H, H + 1):
        inside = (row + dx >= 0) & (row + dx < rows)
        masked[dx] = (jnp.where(inside, low, 0), jnp.where(inside, high, 0))
    near = [jnp.zeros((rows, LANES), f32) for _ in range(2 * F)]
    for code in range(OFFSETS):
        dx, dy = offset_of(code)
        window = lambda k: moved[k * SHIFTS + dy + H, TOP + dx : TOP + dx + rows]
        lift = window(2 * F) - h
        there = (masked[dx][code // half] & (1 << (code % half))) != 0
        g = coupling(float(dx * dx + dy * dy) + lift * lift, there)
        for k in range(2 * F):
            green[4 * code + k] = g[k]
        add_near(near, g, window)
    for k in range(2 * F):
        near_out[k] = near[k]


def near_body(
    n_r, n_c, fields, bits, inner_near, share, cols_b, cols_a, rows_b, rows_a, gens, tables,
    payload, edge_green, source, spill, cs, left_mat, right_mat, common, halo,
):
    rows = fields.shape[1]
    d, c = place_of()
    above, below = halo_rows(rows_a, rows_b)
    backwards = range(H - 1, -1, -1)
    last_rows = range(rows - 1, rows - 1 - H, -1)
    at = H * N_FIELDS
    from_left, from_right = (
        pair_rows(
            row_list(above[at + H * i : at + H * (i + 1)], backwards),
            row_list(below[at + H * i : at + H * (i + 1)], range(H)),
            True,
        )
        for i in range(2)
    )
    h = fields[2 * F]
    inverse = [fields[2 * F + 1 + k] for k in range(2 * F)]
    incident = [fields[N_FIELDS + k] for k in range(2 * F)]
    h_pairs = pair_rows(row_list(h, range(H)), row_list(h, last_rows), False)
    flags = pair_rows(row_list(bits[0], range(H)), row_list(bits[1], last_rows), False)
    row = iota((2 * SUB, LANES), 0)
    lower = row >= SUB
    nth = row & (SUB - 1)
    reach = jnp.zeros((2 * SUB, LANES), jnp.int32)
    for i, (inside, beyond) in enumerate(PAIRS):
        reach = jnp.where(nth == i, inside + beyond + 1, reach)
    first_bit = jnp.where(lower, (H + reach) * SHIFTS + H - 1 - OFFSETS // 2, (H - reach) * SHIFTS + H)
    moved = []
    for k in range(2 * F + 1):
        middle = pair_rows(
            row_list(above[H * k : H * (k + 1)], backwards), row_list(below[H * k : H * (k + 1)], range(H)), True
        )
        side = unpack_columns(from_left, from_right, k)
        moved.append([shifted(middle, side, dy) for dy in range(-H, H + 1)])
    near = [jnp.zeros((2 * SUB, LANES), f32) for _ in range(2 * F)]
    for dy in range(-H, H + 1):
        lift = moved[2 * F][dy + H] - h_pairs
        there = (lax.shift_right_logical(flags, first_bit + dy) & 1) == 1
        g = coupling((reach * reach + dy * dy).astype(f32) + lift * lift, there & (nth < len(PAIRS)))
        for k in range(2 * F):
            edge_green[4 * (dy + H) + k] = g[k]
        add_near(near, g, lambda k: moved[k][dy + H])
    for k in range(2 * F):
        put_pairs(near[k], spill, k)
    near = [inner_near[k] + spill[k] for k in range(2 * F)]
    x, y = place_ids(rows, LANES, 0, 0, rows)
    sources = []
    for f in range(F):
        z = (inverse[2 * f], inverse[2 * f + 1])
        s = times(z, (incident[2 * f] - near[2 * f], incident[2 * f + 1] - near[2 * f + 1]))
        sources += s
        source[2 * f] = s[0]
        source[2 * f + 1] = s[1]
        got = conj_times(carrier(f, 0, x, y, h), s)
        cs[2 * f] = got[0]
        cs[2 * f + 1] = got[1]

    def keep(f, row):
        common[2 * SUB + f : 2 * SUB + f + 1] = row

    right_mat[2 * SUB :] = jnp.zeros((right_mat.shape[0] - 2 * SUB, right_mat.shape[1]), f32)
    common[2 * SUB :] = jnp.zeros((SUB, LANES), f32)
    project(left_mat, right_mat, tables, 0, cs, rows, keep)
    common[0 : 2 * SUB] = gens[...]
    common[2 * SUB + 2 : 2 * SUB + 3] = share[...]
    tail = common[2 * SUB : 3 * SUB]
    down, up = common[0:SUB], common[SUB : 2 * SUB]

    def fill(s):
        payload[s, 0:SUB] = jnp.where(s >= d * n_c, down, up)
        payload[s, SUB : 2 * SUB] = tail

    laps(n_r * n_c, fill, 8 * SUB)
    lasts = pack_columns(sources, True)
    firsts = pack_columns(sources, False)
    at = HALO_AT

    def send(dr, dc, put):
        dst = (d + dr) * n_c + c + dc
        ok = (d + dr >= 0) & (d + dr < n_r) & (c + dc >= 0) & (c + dc < n_c)

        @pl.when(ok)
        def _():
            put(dst)

    def rows_to(dr):
        for k in range(2 * F):
            s = sources[k]
            halo[H * k : H * (k + 1)] = s[rows - H :] if dr > 0 else s[:H]
        first, rest = halo[0:SUB], halo[SUB : 2 * F * H]

        def put(dst):
            payload[dst, 0:SUB] = first
            payload[dst, at : at + 2 * F * H - SUB] = rest

        return put

    def cols_to(dc):
        packed = lasts if dc > 0 else firsts
        quarter = rows // 4
        parts = [roll(packed, 4 * SUB * i)[quarter * i : quarter * (i + 1)] for i in range(4)]
        packed = parts[0] + parts[1] + parts[2] + parts[3]

        def put(dst):
            payload[dst, at : at + quarter] = packed

        return put

    def corner_to(dr, dc):
        packed = lasts if dc > 0 else firsts

        def put(dst):
            payload[dst, at : at + H] = packed[rows - H :] if dr > 0 else packed[:H]

        return put

    for dr in (-1, 1):
        send(dr, 0, rows_to(dr))
        send(0, dr, cols_to(dr))
        for dc in (-1, 1):
            send(dr, dc, corner_to(dr, dc))


def toeplitz(gens, late):
    lane = iota((SUB, LANES), 1)
    low = (lane & SUB) == 0
    slid = [slide(wide(gens[k : k + 1])) for k in range(4)]
    re, im = slid[0:2], slid[2:4]
    bases = [
        [jnp.where(low, re[half], -roll(im[half], SUB)) for half in range(2)],
        [jnp.where(low, im[half], roll(re[half], SUB)) for half in range(2)],
    ]
    out = []
    for a1 in range(Q // SUB):
        for first, second in bases:
            tile = jnp.where(lane < LANES - 2 * SUB * a1, first, second)
            out.append(tile if late else roll(tile, 2 * SUB * a1))
    return out


def slide(row):
    return pltpu.roll(row, LANES - SUB, 1, stride=1, stride_axis=0)


TILES = 2 * Q // SUB


def diagonal(k):
    return iota((SUB, LANES), 1) == SUB * k + iota((SUB, LANES), 0)


def to_columns(row):
    return [jnp.sum(jnp.where(diagonal(k), row, 0.0), axis=1, keepdims=True) for k in range(TILES)]


def wide(row):
    return jnp.broadcast_to(row, (SUB, LANES))


def tree_sum(parts):
    while len(parts) > 1:
        parts = [sum(parts[i : i + 2]) for i in range(0, len(parts), 2)]
    return parts[0]


def packed_times(wr, wi, row):
    low = (iota((SUB, LANES), 1) & SUB) == 0
    turned = jnp.where(low, -roll(row, -SUB), roll(row, SUB))
    return wr * row + wi * turned


def column_times(weights, columns, f):
    out = []
    for a1 in range(Q // SUB):
        at = slice(SUB * a1, SUB * (a1 + 1))
        out += times((weights[2 * f, at], weights[2 * f + 1, at]), (columns[2 * a1], columns[2 * a1 + 1]))
    return out


def shares_of(row):
    low = (iota((SUB, LANES), 1) & SUB) == 0
    row = wide(row)
    return jnp.where(low, row, roll(row, SUB)), jnp.where(low, roll(row, -SUB), row)


def row_step(maps, feeds, shares, weights, carry, spread, put, late):
    out = []
    for f in range(F):
        full = feeds[f] if carry is None else carry[f] + feeds[f]
        full = [jnp.where(diagonal(k), full, 0.0) for k in range(TILES)]
        if carry is None:
            put(f, jnp.zeros((SUB, LANES), f32))
        else:
            amp = spread * packed_times(weights[2 * f], weights[2 * f + 1], carry[f])
            put(f, amp)
            turns = [roll(amp, -2 * SUB * a1) if late else amp for a1 in range(Q // SUB)]
            full = [part - tile * turns[k // 2] for k, (part, tile) in enumerate(zip(full, maps(f), strict=True))]
        share = [jnp.sum(jnp.where(diagonal(k), shares[f], 0.0), axis=1, keepdims=True) for k in range(0, TILES, 2)]
        out.append([share[k // 2] * jnp.sum(full[k], axis=1, keepdims=True) for k in range(TILES)])
    return out


def column_step(maps, feeds, shares, columns, carry, spread, put, late):
    out = []
    for f in range(F):
        amp = [spread * part for part in column_times(columns, carry[f], f)]
        put(f, amp)
        tiles = maps(f)
        pairs = [tiles[k] * amp[k] + tiles[k + 1] * amp[k + 1] for k in range(0, TILES, 2)]
        parts = [roll(pair, 2 * SUB * a1) if late else pair for a1, pair in enumerate(pairs)]
        kept = [jnp.where(diagonal(k), carry[f][k], 0.0) for k in range(TILES)]
        total = wide(jnp.sum(tree_sum(kept) - tree_sum(parts), axis=0, keepdims=True))
        out.append(shares[f] * (total + feeds[f]))
    return out


def sweep(n_r, maps, feeds, share, weights, columns, spread, put, late):
    rows = [wide(weights[k : k + 1]) for k in range(2 * F)]

    def pair(j, carry):
        between = row_step(
            lambda f: maps(j, f), feeds(j), shares_of(share(j)), rows, carry, spread, lambda f, v: put(j, f, v),
            late,
        )
        return column_step(
            lambda f: maps(j + 1, f), feeds(j + 1), shares_of(share(j + 1)), columns, between, spread,
            lambda f, v: put(j + 1, f, v), late,
        )

    carry = None
    pairs = (n_r - 1) // 2
    if pairs > 0:
        carry = pair(0, carry)
    if n_r <= SUB:
        for i in range(1, pairs):
            carry = pair(2 * i, carry)
    else:
        carry = lax.fori_loop(1, pairs, lambda i, now: tuple(pair(2 * i, now)), tuple(carry))
    if (n_r - 1) % 2:
        j = n_r - 2
        last = row_step(
            lambda f: maps(j, f), feeds(j), shares_of(share(j)), rows, carry, spread, lambda f, v: put(j, f, v),
            late,
        )
        for f in range(F):
            put(n_r - 1, f, [spread * part for part in column_times(columns, last[f], f)])
    elif carry is not None:
        for f in range(F):
            put(n_r - 1, f, spread * packed_times(rows[2 * f], rows[2 * f + 1], carry[f]))


def putter(amps, held):
    def put(j, f, value):
        if isinstance(value, list):
            put_columns(amps, j, f, value)
        else:
            held[j // 2, f] = value

    return put


def put_columns(amps, j, f, columns):
    for k, column in enumerate(columns):
        amps[j, f, SUB * k : SUB * (k + 1)] = jnp.broadcast_to(column, (SUB, LANES))


def take_rows(amps, held, j):
    for f in range(F):
        put_columns(amps, j, f, to_columns(held[j // 2, f]))


def laps(n, body, few):
    if n <= few:
        for j in range(n):
            body(j)
    else:
        lax.fori_loop(0, n, lambda j, _: (body(j), 0)[1], 0)


def gens_sum(recv, j, n_c, d, c, step, own):
    total = None
    for k in range(n_c):
        part = recv[j * n_c + k, 0:SUB]
        part = jnp.where((j == d + step) & (k == c), own, part)
        total = part if total is None else total + part
    return total


def powers(base, count):
    out = [None, base]
    for _ in range(2, count):
        out.append(times(out[-1], base))
    return out


MERGED = 5


def merged(middle, side):
    sub = iota((SUB, LANES), 0)
    return [
        jnp.where(sub < H, roll(side[0:SUB], H, 0), middle[0:SUB]),
        middle[SUB : 2 * SUB],
        middle[2 * SUB : 3 * SUB],
        jnp.where(sub >= SUB - H, roll(side[3 * SUB :], -H, 0), middle[3 * SUB :]),
        side[SUB : 2 * SUB] + roll(side[2 * SUB : 3 * SUB], LANES // 2),
    ]


def apart(tiles):
    return [roll(tiles[0], -H, 0), tiles[4], roll(tiles[4], LANES // 2), roll(tiles[3], H, 0)]


def merged_places(rows):
    d, c = place_of()
    sub = iota((SUB, LANES), 0)
    lane = iota((SUB, LANES), 1)
    x0 = d * rows + sub
    y0 = c * LANES + lane
    side = y0 + jnp.where(lane < LANES // 2, LANES, -LANES)
    turned = (lane + LANES // 2) & (LANES - 1)
    side_turned = c * LANES + turned + jnp.where(turned < LANES // 2, LANES, -LANES)
    second = (lane >= LANES // 4) & (lane < 3 * LANES // 4)
    return [
        (jnp.where(sub < H, x0 - H, x0 - SUB), jnp.where(sub < H, side, y0)),
        (x0, y0),
        (x0 + SUB, y0),
        (jnp.where(sub >= SUB - H, x0 + rows - (SUB - H), x0 + rows), jnp.where(sub >= SUB - H, side, y0)),
        (jnp.where(second, x0 + SUB, x0), jnp.where(second, side_turned, side)),
    ]


def store_waves(
    fields, cols_a, cols_b, above, below, loss, first, second, carriers, back_first, back_carriers, inner, edge_l, edge_r
):
    rows = fields.shape[1]
    ks = range(2 * F, N_FIELDS)
    sides = with_halo(ks, fields, cols_a, cols_b, above, below, inner, edge_l, edge_r)
    tiles = [merged(inner[i], side) for i, side in enumerate(sides)]
    for k in range(2 * F):
        for t in range(MERGED):
            loss[t, k] = tiles[1 + k][t]

    def keep(out, t, values):
        for k, value in enumerate(values):
            for part in range(2):
                out[t, k, part] = value[part]

    for t, (x, y) in enumerate(merged_places(rows)):
        h = tiles[0][t]
        keep(first, t, powers(wave(1, x, 0, y, 0.24, h), Q // SUB)[1:])
        keep(second, t, powers(wave(0, x, 1, y, 0.03, h), SUB)[1:])
        keep(carriers, t, [carrier(f, 0, x, y, h) for f in range(F)])
        if t in (1, 2):
            keep(back_first, t - 1, powers(wave(-1, x, 0, y, 0.24, h), Q // SUB)[1:])
            keep(back_carriers, t - 1, [carrier(f, 1, x, y, h) for f in range(F)])


def radiated(amps, at, f, first, second, carriers, t, t_second):
    splat = lambda a: wide(amps[at, f, a : a + 1])
    total = None
    for a1 in range(Q // SUB):
        base = 2 * SUB * a1
        inner = (splat(base), splat(base + SUB))
        for a2 in range(1, SUB):
            u2 = (second[t_second, a2 - 1, 0], second[t_second, a2 - 1, 1])
            got = times((splat(base + a2), splat(base + SUB + a2)), u2)
            inner = (inner[0] + got[0], inner[1] + got[1])
        if a1 == 0:
            total = inner
        else:
            got = times((first[t, a1 - 1, 0], first[t, a1 - 1, 1]), inner)
            total = (total[0] + got[0], total[1] + got[1])
    return times((carriers[t, f, 0], carriers[t, f, 1]), total)


def new_body(
    n_r, n_c, spread, recv, green, edge_green, source, fields, cols_b, cols_a, rows_b, rows_a, tables, weights, columns,
    forward, driven, payload, second, back_first, back_carriers, below_gens,
    loss, first, carriers, amps, kept, held, inner, moved, edge_l, edge_r, spill, cs, left_mat, right_mat, common, halo,
):
    rows = fields.shape[1]
    d, c = place_of()
    above_rows, below_rows = halo_rows(rows_a, rows_b)
    above = above_rows[GENS_AT:]
    below_gens[...] = below_rows[GENS_AT:]
    store_waves(
        fields, cols_a, cols_b, above_rows, below_rows,
        loss, first, second, carriers, back_first, back_carriers, held, edge_l, edge_r,
    )

    if n_r <= SUB:
        sums = [gens_sum(recv, j, n_c, d, c, -1, above) for j in range(n_r - 1)]

    def maps(j, f):
        gens = sums[j] if n_r <= SUB else gens_sum(recv, j, n_c, d, c, -1, above)
        return toeplitz(gens[4 * f : 4 * f + 4], False)

    def feeds(j):
        feed = recv[j * n_c, SUB : 2 * SUB]
        for k in range(1, n_c):
            feed = feed + recv[j * n_c + k, SUB : 2 * SUB]
        return [wide(feed[f : f + 1]) for f in range(F)]

    sweep(n_r, maps, feeds, lambda j: recv[j * n_c, SUB + 2 : SUB + 3], weights, columns, spread, putter(amps, kept), False)
    even = d - (d & 1)
    take_rows(amps, kept, even)
    take_rows(amps, kept, jnp.minimum(even + 2 * (d & 1), n_r - 1 - ((n_r - 1) & 1)))

    at = HALO_AT

    def got(dr, dc, start, size):
        src = jnp.clip(d + dr, 0, n_r - 1) * n_c + jnp.clip(c + dc, 0, n_c - 1)
        ok = (d + dr >= 0) & (d + dr < n_r) & (c + dc >= 0) & (c + dc < n_c)
        return jnp.where(ok, recv[src, start : start + size], 0.0)

    edge_l[...] = jnp.zeros(edge_l.shape, f32)
    edge_r[...] = jnp.zeros(edge_r.shape, f32)
    quarter = rows // 4
    for edge, dc in ((edge_l, -1), (edge_r, 1)):
        side = got(0, dc, at, quarter)
        for i in range(4):
            edge[TOP + quarter * i : TOP + quarter * (i + 1)] = roll(side, -4 * SUB * i)
        edge[TOP - H : TOP] = got(-1, dc, at, H)
        edge[TOP + rows : TOP + rows + H] = got(1, dc, at, H)
    from_left, from_right = edge_l[...], edge_r[...]
    for i, dr in enumerate((-1, 1)):
        halo[i, 0:SUB] = got(dr, 0, 0, SUB)
        halo[i, SUB : 2 * F * H] = got(dr, 0, at, 2 * F * H - SUB)
    for k in range(2 * F):
        inner[k] = jnp.zeros(inner.shape[1:], f32)
        inner[k, TOP : TOP + rows] = source[k]
        inner[k, TOP - H : TOP] = halo[0, H * k : H * (k + 1)]
        inner[k, TOP + rows : TOP + rows + H] = halo[1, H * k : H * (k + 1)]
    sides = [unpack_columns(from_left, from_right, k) for k in range(2 * F)]

    weak = {}
    lost = {}
    for t, step in enumerate((-1, 0, 0, 1, 0)):
        at = jnp.clip(d + step, 0, n_r - 1)
        for f in range(F):
            w = radiated(amps, at, f, first, second, carriers, t, t)
            got = times((loss[t, 2 * f], loss[t, 2 * f + 1]), w)
            for part in range(2):
                weak[t, 2 * f + part] = w[part]
                lost[t, 2 * f + part] = got[part]
    beyond = []
    for k in range(2 * F):
        tiles = [lost[t, k] for t in range(MERGED)]
        side = sides[k] - jnp.concatenate(apart(tiles), axis=0)
        middle = inner[k] - jnp.concatenate(tiles[:4], axis=0)
        forward[k] = middle[TOP : TOP + rows]
        for i in range(SHIFTS):
            moved[k * SHIFTS + i, 0:TOP] = jnp.zeros((TOP, LANES), f32)
            moved[k * SHIFTS + i, TOP + rows :] = jnp.zeros((TOP, LANES), f32)
        store_shifted(moved, k, middle[TOP : TOP + rows], side[TOP : TOP + rows])
        above_edge = range(TOP - 1, TOP - 1 - H, -1)
        below_edge = range(TOP + rows, TOP + rows + H)
        pairs = [pair_rows(row_list(part, above_edge), row_list(part, below_edge), True) for part in (middle, side)]
        beyond.append([shifted(*pairs, dy) for dy in range(-H, H + 1)])
    near = [jnp.zeros((2 * SUB, LANES), f32) for _ in range(2 * F)]
    for dy in range(-H, H + 1):
        add_near(near, [edge_green[4 * (dy + H) + k] for k in range(2 * F)], lambda k: beyond[k][dy + H])
    for k in range(2 * F):
        put_pairs(near[k], spill, k)
    near = [spill[k] for k in range(2 * F)]
    for code in range(OFFSETS):
        dx, dy = offset_of(code)
        add_near(
            near,
            [green[4 * code + k] for k in range(2 * F)],
            lambda k: moved[k * SHIFTS + dy + H, TOP + dx : TOP + dx + rows],
        )
    for f in range(F):
        rest = []
        for part in range(2):
            k = 2 * f + part
            w = jnp.concatenate([weak[1, k], weak[2, k]], axis=0)
            rest.append(fields[N_FIELDS + k] - near[k] - w)
        s = times((fields[2 * F + 1 + 2 * f], fields[2 * F + 2 + 2 * f]), rest)
        driven[2 * f] = s[0]
        driven[2 * f + 1] = s[1]
        base = [jnp.concatenate([back_carriers[t, f, part] for t in range(2)], axis=0) for part in range(2)]
        add = conj_times(base, s)
        cs[2 * f] = add[0]
        cs[2 * f + 1] = add[1]

    def keep(f, row):
        common[f : f + 1] = row

    right_mat[2 * SUB :] = jnp.zeros((right_mat.shape[0] - 2 * SUB, right_mat.shape[1]), f32)
    project(left_mat, right_mat, tables, 2, cs, rows, keep)
    pair = common[0:2]

    def fill(s):
        payload[s] = pair

    laps(n_r * n_c, fill, 8 * SUB)


def last_body(
    n_r, n_c, spread, recv, fed, new, driven, fields, weights, columns, first, second, carriers, below_gens,
    forward, currents, amps, kept,
):
    rows = fields.shape[1]
    d, c = place_of()
    forward[...] = new[...]
    below = below_gens[...]

    def feeds(k):
        j = n_r - 1 - k
        feed = fed[j * n_c]
        for i in range(1, n_c):
            feed = feed + fed[j * n_c + i]
        return [wide(feed[f : f + 1]) for f in range(F)]

    def share(k):
        return recv[(n_r - 1 - k) * n_c, SUB + 2 : SUB + 3]

    def maps(k, f):
        return toeplitz(gens_sum(recv, n_r - 1 - k, n_c, d, c, 1, below)[4 * f : 4 * f + 4], True)

    sweep(n_r, maps, feeds, share, weights, columns, spread, putter(amps, kept), True)
    at = n_r - 1 - d
    take_rows(amps, kept, at - (at & 1))
    for tile in range(rows // SUB):
        rows_at = slice(SUB * tile, SUB * (tile + 1))
        for f in range(F):
            w = radiated(amps, at, f, first, second, carriers, tile, tile + 1)
            lost = times((fields[2 * F + 1 + 2 * f, rows_at], fields[2 * F + 2 + 2 * f, rows_at]), w)
            currents[2 * f, rows_at] = driven[2 * f, rows_at] - lost[0]
            currents[2 * f + 1, rows_at] = driven[2 * f + 1, rows_at] - lost[1]


def swaps(n):
    first = [(i, i ^ 1) for i in range(n) if i ^ 1 < n]
    second = [(i, i + 1) for i in range(1, n - 1, 2)] + [(i + 1, i) for i in range(1, n - 1, 2)]
    return first, second


def swap(axis, n, a, b):
    first, second = swaps(n)
    b = lax.ppermute(b, axis, second)
    return lax.ppermute(a, axis, first), b


def stacked(arrays):
    rows, cols = arrays[0].shape[1:]
    total = sum(array.shape[0] for array in arrays)
    out, at = None, 0
    for array in arrays:
        count = array.shape[0]
        wide_array = jnp.pad(
            array, ((at, total - at - count), (0, rows - array.shape[1]), (0, cols - array.shape[2]))
        )
        out = wide_array if out is None else out + wide_array
        at += count
    return out


def per_device(n_r, n_c, incident, inverse_diag, previous, heights, neighbours, counts, transmit, angle_weights):
    rows, cols = heights.shape
    patches = rows * cols
    spread = 1.0 / math.sqrt(rows * cols * n_c)
    slots = n_r * n_c
    tall = rows + 2 * SUB
    fields = stacked([previous, heights[None], inverse_diag, incident, angle_weights, transmit])
    cols_b, cols_a = call(columns_body, [(rows, LANES)] * 2, [VMEM], flops=500_000)(fields)
    cols_a, cols_b = swap("xr", n_c, cols_a, cols_b)
    tables, gens = call(
        functools.partial(tables_body, n_r),
        [(6, rows, SUB, LANES), (2 * SUB, LANES)],
        [VMEM],
        [pltpu.VMEM((16 * SUB, patches), f32), pltpu.VMEM((16 * SUB, patches), f32)],
    )(fields)
    weights, share, columns = call(
        params_body, [(2 * F, LANES), (1, LANES), (2 * F, Q, LANES)], [VMEM], flops=500_000
    )(fields)
    gens, weights, share, columns = lax.optimization_barrier((gens, weights, share, columns))
    rows_b, rows_a = call(rows_body, [(ROWS_SENT, LANES)] * 2, [VMEM] * 4, flops=500_000)(fields, gens, cols_b, cols_a)
    rows_a, rows_b, neighbours, counts = lax.optimization_barrier((rows_a, rows_b, neighbours, counts))
    rows_a, rows_b = swap("rng", n_r, rows_a, rows_b)
    lists = jnp.concatenate([neighbours, counts[None]])
    green, inner_near, bits = call(
        inner_body,
        [
            (4 * OFFSETS, rows, LANES),
            (2 * F, rows, LANES),
            jax.ShapeDtypeStruct((2, rows, LANES), jnp.int32),
        ],
        [VMEM] * 4,
        [pltpu.VMEM(((2 * F + 1) * SHIFTS, tall, LANES), f32)],
        500_000,
    )(fields, lists, cols_b, cols_a)
    edges = [pltpu.VMEM((tall, LANES), f32)] * 2
    payload, edge_green, source = call(
        functools.partial(near_body, n_r, n_c),
        [(slots, SLOT, LANES), (4 * SHIFTS, 2 * SUB, LANES), (2 * F, rows, LANES)],
        [VMEM] * 10,
        [
            pltpu.VMEM((2 * F, rows, LANES), f32),
            pltpu.VMEM((2 * F, rows, LANES), f32),
            pltpu.VMEM((4 * SUB, patches), f32),
            pltpu.VMEM((16 * SUB, patches), f32),
            pltpu.VMEM((3 * SUB, LANES), f32),
            pltpu.VMEM((2 * SUB, LANES), f32),
        ],
    )(fields, bits, inner_near, share, cols_b, cols_a, rows_b, rows_a, gens, tables)
    recv = lax.all_to_all(payload, BOTH, 0, 0)
    tile = (2, SUB, LANES)
    new, driven, payload, second, back_first, back_carriers, below_gens = call(
        functools.partial(new_body, n_r, n_c, spread),
        [
            (2 * F, rows, LANES),
            (2 * F, rows, LANES),
            (slots, 2, LANES),
            (MERGED, SUB - 1, *tile),
            (2, Q // SUB - 1, *tile),
            (2, F, *tile),
            (SUB, LANES),
        ],
        [VMEM] * 12,
        [
            pltpu.VMEM((MERGED, 2 * F, SUB, LANES), f32),
            pltpu.VMEM((MERGED, Q // SUB - 1, *tile), f32),
            pltpu.VMEM((MERGED, F, *tile), f32),
            pltpu.VMEM((n_r, F, 2 * Q, LANES), f32),
            pltpu.VMEM(((n_r + 1) // 2, F, SUB, LANES), f32),
            pltpu.VMEM((2 * F + 1, tall, LANES), f32),
            pltpu.VMEM((2 * F, tall, LANES), f32),
            pltpu.VMEM((2 * F * (2 * H + 1), tall, LANES), f32),
            *edges,
            pltpu.VMEM((2 * F, rows, LANES), f32),
            pltpu.VMEM((2 * F, rows, LANES), f32),
            pltpu.VMEM((4 * SUB, patches), f32),
            pltpu.VMEM((16 * SUB, patches), f32),
            pltpu.VMEM((SUB, LANES), f32),
            pltpu.VMEM((2, 2 * SUB, LANES), f32),
        ],
    )(recv, green, edge_green, source, fields, cols_b, cols_a, rows_b, rows_a, tables, weights, columns)
    fed = lax.all_to_all(payload, BOTH, 0, 0)
    return call(
        functools.partial(last_body, n_r, n_c, spread),
        [(2 * F, rows, LANES), (2 * F, rows, LANES)],
        [VMEM] * 11,
        [pltpu.VMEM((n_r, F, 2 * Q, LANES), f32), pltpu.VMEM(((n_r + 1) // 2, F, SUB, LANES), f32)],
    )(recv, fed, new, driven, fields, weights, columns, back_first, second, back_carriers, below_gens)


def solution(mesh):
    body = functools.partial(per_device, mesh.shape["rng"], mesh.shape["xr"])
    field = P(None, "rng", "xr")
    return jax.shard_map(
        body,
        mesh=mesh,
        in_specs=(field, field, field, P("rng", "xr"), field, P("rng", "xr"), P("rng", None, None), P()),
        out_specs=(field, field),
        check_vma=False,
    )
```

```python
import functools
import math

import jax
import jax.numpy as jnp
from jax import lax
from jax.experimental import pallas as pl
from jax.experimental.pallas import tpu as pltpu
from jax.sharding import PartitionSpec as P

F = 2
Q = 64
H = 3
LMAX = 24
OFFSETS = 48
SUB = 8
LANES = 128
PERIOD = 64
TOP = SUB
GREEN = 0.25
TURN = 2.0 * math.pi
SLOT = 16
HALO_AT = SUB + 3
HIGHEST = lax.Precision.HIGHEST
BOTH = ("rng", "xr")
f32 = jnp.float32


def iota(shape, dim):
    return lax.broadcasted_iota(jnp.int32, shape, dim)


def roll(x, shift, axis=1):
    shift = shift % x.shape[axis]
    return x if shift == 0 else pltpu.roll(x, shift, axis)


def cos_sin(turns):
    quarter = jnp.floor(4.0 * turns + 0.5)
    rest = turns - 0.25 * quarter
    which = quarter.astype(jnp.int32)
    sq = rest * rest
    s = rest * (TURN + sq * (-(TURN**3) / 6 + sq * (TURN**5 / 120 + sq * (-(TURN**7) / 5040 + sq * (TURN**9 / 362880)))))
    c = 1.0 + sq * (-(TURN**2) / 2 + sq * (TURN**4 / 24 + sq * (-(TURN**6) / 720 + sq * (TURN**8 / 40320))))
    odd = (which & 1) == 1
    cos = jnp.where(odd, s, c)
    sin = jnp.where(odd, c, s)
    cos = jnp.where(((which + 1) & 2) == 2, -cos, cos)
    sin = jnp.where((which & 2) == 2, -sin, sin)
    return cos, sin


def times(a, b):
    return a[0] * b[0] - a[1] * b[1], a[0] * b[1] + a[1] * b[0]


def conj_times(a, b):
    return a[0] * b[0] + a[1] * b[1], a[0] * b[1] - a[1] * b[0]


def wave(step_x, x, step_y, y, lift, heights):
    phase = (step_x * x + step_y * y) & (PERIOD - 1)
    return cos_sin(phase.astype(f32) * (1.0 / PERIOD) + (lift / TURN) * heights)


def offset_of(code):
    full = code + (1 if code >= OFFSETS // 2 else 0)
    return full // (2 * H + 1) - H, full % (2 * H + 1) - H


VMEM = pl.BlockSpec(memory_space=pltpu.VMEM)
PLAIN = pl.BlockSpec()


def call(body, out, ins, scratch=(), flops=2_000_000_000):
    return pl.pallas_call(
        body,
        out_shape=tuple(jax.ShapeDtypeStruct(s, f32) if isinstance(s, tuple) else s for s in out),
        in_specs=list(ins),
        out_specs=tuple(VMEM for _ in out),
        scratch_shapes=list(scratch),
        compiler_params=pltpu.CompilerParams(vmem_limit_bytes=48 * 1024 * 1024),
        cost_estimate=pl.CostEstimate(flops=flops, bytes_accessed=1 << 20, transcendentals=0),
    )


def place_of():
    return lax.axis_index("rng"), lax.axis_index("xr")


def pack_columns(fields, right):
    rows = fields[0].shape[0]
    lane = iota((rows, LANES), 1)
    packed = jnp.zeros((rows, LANES), f32)
    for k, field in enumerate(fields):
        moved = roll(field, H * k - (LANES - H) if right else H * k)
        packed = jnp.where((lane >= H * k) & (lane < H * (k + 1)), moved, packed)
    return packed


def unpack_columns(from_left, from_right, k):
    lane = iota(from_left.shape, 1)
    left = jnp.where(lane >= LANES - H, roll(from_left, LANES - H - H * k), 0.0)
    return jnp.where(lane < H, roll(from_right, -H * k), left)


def shifted(inner, edge, dy):
    if dy == 0:
        return inner
    lane = iota(inner.shape, 1)
    outside = lane >= LANES - dy if dy > 0 else lane < -dy
    return jnp.where(outside, roll(edge, -dy), roll(inner, -dy))


N_FIELDS = 4 * F + 1
ROWS_SENT = 48
GENS_AT = 40


def columns_body(fields, send_b, send_a):
    values = [fields[k] for k in range(N_FIELDS)]
    right = pack_columns(values, True)
    left = pack_columns(values, False)
    even = (lax.axis_index("xr") & 1) == 0
    send_a[...] = jnp.where(even, right, left)
    send_b[...] = jnp.where(even, left, right)


def rows_body(fields, gens, recv_b, recv_a, send_b, send_a):
    d, c = place_of()
    even_c = (c & 1) == 0
    even_r = (d & 1) == 0
    rows = fields.shape[1]
    values = [fields[k] for k in range(N_FIELDS)]
    values.append(jnp.where(even_c, recv_b[...], recv_a[...]))
    values.append(jnp.where(even_c, recv_a[...], recv_b[...]))
    for k, field in enumerate(values):
        last, first = field[rows - H :], field[:H]
        send_a[H * k : H * (k + 1)] = jnp.where(even_r, last, first)
        send_b[H * k : H * (k + 1)] = jnp.where(even_r, first, last)
    used = H * len(values)
    send_a[used:GENS_AT] = jnp.zeros((GENS_AT - used, LANES), f32)
    send_b[used:GENS_AT] = jnp.zeros((GENS_AT - used, LANES), f32)
    down, up = gens[0:SUB], gens[SUB : 2 * SUB]
    send_a[GENS_AT:] = jnp.where(even_r, down, up)
    send_b[GENS_AT:] = jnp.where(even_r, up, down)


def tables_body(n_r, fields, tables, gens, left_mat, right_mat):
    d, c = place_of()
    turned = [d & 1, (n_r - 1 - d) & 1]
    signs = [jnp.where(t == 1, -1.0, 1.0) for t in turned]
    rows = fields.shape[1]
    x0 = d * rows
    y0 = c * LANES
    angle = iota((2 * SUB, LANES), 0) - SUB
    y = iota((2 * SUB, LANES), 1) + y0
    for i in range(rows):
        x = jnp.full((2 * SUB, LANES), x0 + i, jnp.int32)
        lanes = pl.ds(i * LANES, LANES)
        h2 = jnp.broadcast_to(fields[2 * F, i : i + 1, :], (2 * SUB, LANES)) * angle.astype(f32)
        c2, s2 = wave(0, x, angle, y, 0.03, h2)
        tables[4, i] = c2[SUB:]
        tables[5, i] = s2[SUB:]
        right_mat[0 : 2 * SUB, lanes] = c2
        right_mat[2 * SUB : 4 * SUB, lanes] = s2
        for direction in range(2):
            c1, s1 = wave(angle * (1 - 2 * direction), x, 0, y, 0.24, h2)
            tables[2 * direction, i] = c1[SUB:]
            tables[2 * direction + 1, i] = s1[SUB:]
            s1 = signs[direction] * s1
            for f in range(F):
                zr = fields[2 * F + 1 + 2 * f, i : i + 1, :]
                zi = fields[2 * F + 2 + 2 * f, i : i + 1, :]
                base = (direction * F + f) * 4 * SUB
                left_mat[base : base + 2 * SUB, lanes] = zr * c1 - zi * s1
                left_mat[base + 2 * SUB : base + 4 * SUB, lanes] = zr * s1 + zi * c1
    right_mat[4 * SUB :] = jnp.zeros((right_mat.shape[0] - 4 * SUB, right_mat.shape[1]), f32)
    both = lax.dot_general(
        left_mat[...], right_mat[...], (((1,), (1,)), ((), ())), precision=HIGHEST, preferred_element_type=f32
    )
    lane = iota((SUB, LANES), 1)
    for direction in range(2):
        for f in range(F):
            base = (direction * F + f) * 4 * SUB
            for half in range(2):
                p = both[base + half * SUB : base + (half + 1) * SUB]
                q = both[base + (2 + half) * SUB : base + (3 + half) * SUB]
                for part in range(2):
                    sign = signs[direction]
                    if part == 0:
                        g = p - sign * roll(q, -2 * SUB)
                    else:
                        g = roll(p, -2 * SUB) + sign * q
                    g = jnp.where(lane < 2 * SUB, g, 0.0)
                    g = pltpu.roll(g, 0, 1, stride=2 * SUB, stride_axis=0)
                    row = jnp.sum(g, axis=0, keepdims=True)
                    at = direction * SUB + f * 4 + part * 2 + (1 - half)
                    gens[at : at + 1] = row


def list_bits(neighbours, counts):
    count = counts[...]
    low = jnp.zeros(count.shape, jnp.int32)
    high = jnp.zeros(count.shape, jnp.int32)
    half = OFFSETS // 2
    one = jnp.ones(count.shape, jnp.int32)
    for slot in range(LMAX):
        code = neighbours[slot]
        live = count > slot
        is_low = code < half
        bit = lax.shift_left(one, jnp.where(is_low, code, code - half))
        low = low | jnp.where(live & is_low, bit, 0)
        high = high | jnp.where(live & (code >= half), bit, 0)
    return low, high


def params_body(fields, weights, share, columns):
    spot = iota((LANES, LANES), 0)
    spot = jnp.where(spot < Q, 2 * SUB * (spot // SUB) + (spot & (SUB - 1)), 2 * LANES)
    base = N_FIELDS + 2 * F
    values = jnp.concatenate([fields[base + i, 0:2] for i in range(F + 1)] + [fields[base + F, 2:4]], axis=0)
    placed = [
        lax.dot_general(
            values,
            (iota((LANES, LANES), 1) == spot + SUB * k).astype(f32),
            (((1,), (0,)), ((), ())),
            precision=HIGHEST,
            preferred_element_type=f32,
        )
        for k in range(2)
    ]
    weights[...] = placed[0][: 2 * F] + placed[1][: 2 * F]
    share[...] = placed[0][2 * F : 2 * F + 1] + placed[1][2 * F + 1 : 2 * F + 2]
    for k in range(2 * F):
        for a1, column in enumerate(to_columns(wide(placed[0][k : k + 1]))[::2]):
            columns[k, SUB * a1 : SUB * (a1 + 1)] = wide(column)


def project(left_mat, right_mat, tables, first, cs, rows, f_out):
    for i in range(rows):
        lanes = pl.ds(i * LANES, LANES)
        right_mat[0:SUB, lanes] = tables[4, i]
        right_mat[SUB : 2 * SUB, lanes] = tables[5, i]
        c1, s1 = tables[first, i], tables[first + 1, i]
        for f in range(F):
            re, im = conj_times((c1, s1), (cs[2 * f, i : i + 1, :], cs[2 * f + 1, i : i + 1, :]))
            left_mat[2 * f * SUB : (2 * f + 1) * SUB, lanes] = re
            left_mat[(2 * f + 1) * SUB : (2 * f + 2) * SUB, lanes] = im
    sums = lax.dot_general(
        left_mat[0 : 4 * SUB], right_mat[...], (((1,), (1,)), ((), ())), precision=HIGHEST, preferred_element_type=f32
    )
    lane = iota((SUB, LANES), 1)
    for f in range(F):
        gr = sums[2 * f * SUB : (2 * f + 1) * SUB]
        gi = sums[(2 * f + 1) * SUB : (2 * f + 2) * SUB]
        re = gr + roll(gi, -SUB)
        im = gi - roll(gr, -SUB)
        packed = jnp.where(lane < SUB, re, jnp.where(lane < 2 * SUB, roll(im, SUB), 0.0))
        packed = pltpu.roll(packed, 0, 1, stride=2 * SUB, stride_axis=0)
        f_out(f, jnp.sum(packed, axis=0, keepdims=True))


def carrier(f, direction, x, y, heights):
    sign = 1 - 2 * direction
    return wave(sign * (1 + 2 * f), x, f - 4, y, 0.3 + 0.2 * f, heights)


def place_ids(rows, cols, first_row, first_col, own_rows):
    d, c = place_of()
    x = d * own_rows + first_row + iota((rows, cols), 0)
    y = c * LANES + first_col + iota((rows, cols), 1)
    return x, y


def halo_rows(rows_a, rows_b):
    even = (lax.axis_index("rng") & 1) == 0
    return jnp.where(even, rows_b[...], rows_a[...]), jnp.where(even, rows_a[...], rows_b[...])


def with_halo(ks, fields, cols_a, cols_b, above, below, inner, edge_l, edge_r):
    rows = fields.shape[1]
    even = (lax.axis_index("xr") & 1) == 0
    edge_l[...] = jnp.zeros(edge_l.shape, f32)
    edge_r[...] = jnp.zeros(edge_r.shape, f32)
    edge_l[TOP : TOP + rows] = jnp.where(even, cols_b[...], cols_a[...])
    edge_r[TOP : TOP + rows] = jnp.where(even, cols_a[...], cols_b[...])
    at = H * N_FIELDS
    edge_l[TOP - H : TOP] = above[at : at + H]
    edge_l[TOP + rows : TOP + rows + H] = below[at : at + H]
    edge_r[TOP - H : TOP] = above[at + H : at + 2 * H]
    edge_r[TOP + rows : TOP + rows + H] = below[at + H : at + 2 * H]
    from_left, from_right = edge_l[...], edge_r[...]
    sides = []
    for i, k in enumerate(ks):
        inner[i] = jnp.zeros(inner.shape[1:], f32)
        inner[i, TOP : TOP + rows] = fields[k]
        inner[i, TOP - H : TOP] = above[H * k : H * (k + 1)]
        inner[i, TOP + rows : TOP + rows + H] = below[H * k : H * (k + 1)]
        sides.append(unpack_columns(from_left, from_right, k))
    return sides


PAIRS = [(row, beyond) for row in range(H) for beyond in range(H - row)]
SHIFTS = 2 * H + 1


def pair_rows(top, bottom, beyond):
    which = [pair[1 if beyond else 0] for pair in PAIRS]
    rest = jnp.zeros((SUB - len(PAIRS), LANES), top[0].dtype)
    parts = []
    for edge in (top, bottom):
        parts += [edge[i] for i in which] + [rest]
    return jnp.concatenate(parts, axis=0)


def row_list(array, indices):
    return [array[i : i + 1] for i in indices]


def put_pairs(near, spill, k):
    rows = spill.shape[1]
    spill[k] = jnp.zeros(spill.shape[1:], f32)
    for edge in range(2):
        at = SUB * edge
        for row in range(H):
            count = H - row
            total = near[at : at + 1]
            for i in range(1, count):
                total = total + near[at + i : at + i + 1]
            at += count
            to = rows - 1 - row if edge else row
            spill[k, to : to + 1] = total


def coupling(squared, there):
    inverse_r = lax.rsqrt(squared)
    size = jnp.where(there, GREEN * inverse_r, 0.0)
    off = squared * inverse_r * (1.0 / 16.0) - 0.25
    sq = off * off
    w = (-off * polynomial(SINE, sq), polynomial(COSINE, sq))
    fourth = square(square(w))
    out = []
    for power in (fourth, times(fourth, w)):
        out += [size * power[0], size * power[1]]
    return out


def square(a):
    return a[0] * a[0] - a[1] * a[1], 2.0 * a[0] * a[1]


def polynomial(coefficients, x):
    total = coefficients[-1]
    for value in coefficients[-2::-1]:
        total = total * x + value
    return total


SINE = (6.283185280367426, -41.341680722295834, 81.60248507719457, -76.58139539835082, 39.76160778337109)
COSINE = (1.0, -19.739208548909147, 64.93934662883956, -85.4535715937672, 60.144014415422156, -24.982233003994804)


def add_near(near, g, window):
    for f in range(F):
        got = times((g[2 * f], g[2 * f + 1]), (window(2 * f), window(2 * f + 1)))
        near[2 * f] = near[2 * f] + got[0]
        near[2 * f + 1] = near[2 * f + 1] + got[1]


def side_columns(cols_a, cols_b):
    even = (lax.axis_index("xr") & 1) == 0
    return jnp.where(even, cols_b[...], cols_a[...]), jnp.where(even, cols_a[...], cols_b[...])


def store_shifted(moved, k, middle, side):
    rows = middle.shape[0]
    for dy in range(-H, H + 1):
        moved[k * SHIFTS + dy + H, TOP : TOP + rows] = shifted(middle, side, dy)


def inner_body(fields, neighbours, counts, cols_b, cols_a, green, near_out, bits, moved):
    rows = fields.shape[1]
    low, high = list_bits(neighbours, counts)
    bits[0] = low
    bits[1] = high
    from_left, from_right = side_columns(cols_a, cols_b)
    for k in range(2 * F + 1):
        for i in range(SHIFTS):
            moved[k * SHIFTS + i, 0:TOP] = jnp.zeros((TOP, LANES), f32)
            moved[k * SHIFTS + i, TOP + rows :] = jnp.zeros((TOP, LANES), f32)
        store_shifted(moved, k, fields[k], unpack_columns(from_left, from_right, k))
    h = fields[2 * F]
    half = OFFSETS // 2
    row = iota((rows, LANES), 0)
    masked = {}
    for dx in range(-H, H + 1):
        inside = (row + dx >= 0) & (row + dx < rows)
        masked[dx] = (jnp.where(inside, low, 0), jnp.where(inside, high, 0))
    near = [jnp.zeros((rows, LANES), f32) for _ in range(2 * F)]
    for code in range(OFFSETS):
        dx, dy = offset_of(code)
        window = lambda k: moved[k * SHIFTS + dy + H, TOP + dx : TOP + dx + rows]
        lift = window(2 * F) - h
        there = (masked[dx][code // half] & (1 << (code % half))) != 0
        g = coupling(float(dx * dx + dy * dy) + lift * lift, there)
        for k in range(2 * F):
            green[4 * code + k] = g[k]
        add_near(near, g, window)
    for k in range(2 * F):
        near_out[k] = near[k]


def near_body(
    n_r, n_c, fields, bits, inner_near, share, cols_b, cols_a, rows_b, rows_a, gens, tables,
    payload, edge_green, source, spill, cs, left_mat, right_mat, common, halo,
):
    rows = fields.shape[1]
    d, c = place_of()
    above, below = halo_rows(rows_a, rows_b)
    backwards = range(H - 1, -1, -1)
    last_rows = range(rows - 1, rows - 1 - H, -1)
    at = H * N_FIELDS
    from_left, from_right = (
        pair_rows(
            row_list(above[at + H * i : at + H * (i + 1)], backwards),
            row_list(below[at + H * i : at + H * (i + 1)], range(H)),
            True,
        )
        for i in range(2)
    )
    h = fields[2 * F]
    inverse = [fields[2 * F + 1 + k] for k in range(2 * F)]
    incident = [fields[N_FIELDS + k] for k in range(2 * F)]
    h_pairs = pair_rows(row_list(h, range(H)), row_list(h, last_rows), False)
    flags = pair_rows(row_list(bits[0], range(H)), row_list(bits[1], last_rows), False)
    row = iota((2 * SUB, LANES), 0)
    lower = row >= SUB
    nth = row & (SUB - 1)
    reach = jnp.zeros((2 * SUB, LANES), jnp.int32)
    for i, (inside, beyond) in enumerate(PAIRS):
        reach = jnp.where(nth == i, inside + beyond + 1, reach)
    first_bit = jnp.where(lower, (H + reach) * SHIFTS + H - 1 - OFFSETS // 2, (H - reach) * SHIFTS + H)
    moved = []
    for k in range(2 * F + 1):
        middle = pair_rows(
            row_list(above[H * k : H * (k + 1)], backwards), row_list(below[H * k : H * (k + 1)], range(H)), True
        )
        side = unpack_columns(from_left, from_right, k)
        moved.append([shifted(middle, side, dy) for dy in range(-H, H + 1)])
    near = [jnp.zeros((2 * SUB, LANES), f32) for _ in range(2 * F)]
    for dy in range(-H, H + 1):
        lift = moved[2 * F][dy + H] - h_pairs
        there = (lax.shift_right_logical(flags, first_bit + dy) & 1) == 1
        g = coupling((reach * reach + dy * dy).astype(f32) + lift * lift, there & (nth < len(PAIRS)))
        for k in range(2 * F):
            edge_green[4 * (dy + H) + k] = g[k]
        add_near(near, g, lambda k: moved[k][dy + H])
    for k in range(2 * F):
        put_pairs(near[k], spill, k)
    near = [inner_near[k] + spill[k] for k in range(2 * F)]
    x, y = place_ids(rows, LANES, 0, 0, rows)
    sources = []
    for f in range(F):
        z = (inverse[2 * f], inverse[2 * f + 1])
        s = times(z, (incident[2 * f] - near[2 * f], incident[2 * f + 1] - near[2 * f + 1]))
        sources += s
        source[2 * f] = s[0]
        source[2 * f + 1] = s[1]
        got = conj_times(carrier(f, 0, x, y, h), s)
        cs[2 * f] = got[0]
        cs[2 * f + 1] = got[1]

    def keep(f, row):
        common[2 * SUB + f : 2 * SUB + f + 1] = row

    right_mat[2 * SUB :] = jnp.zeros((right_mat.shape[0] - 2 * SUB, right_mat.shape[1]), f32)
    common[2 * SUB :] = jnp.zeros((SUB, LANES), f32)
    project(left_mat, right_mat, tables, 0, cs, rows, keep)
    common[0 : 2 * SUB] = gens[...]
    common[2 * SUB + 2 : 2 * SUB + 3] = share[...]
    tail = common[2 * SUB : 3 * SUB]
    down, up = common[0:SUB], common[SUB : 2 * SUB]

    def fill(s):
        payload[s, 0:SUB] = jnp.where(s >= d * n_c, down, up)
        payload[s, SUB : 2 * SUB] = tail

    laps(n_r * n_c, fill, 8 * SUB)
    lasts = pack_columns(sources, True)
    firsts = pack_columns(sources, False)
    at = HALO_AT

    def send(dr, dc, put):
        dst = (d + dr) * n_c + c + dc
        ok = (d + dr >= 0) & (d + dr < n_r) & (c + dc >= 0) & (c + dc < n_c)

        @pl.when(ok)
        def _():
            put(dst)

    def rows_to(dr):
        for k in range(2 * F):
            s = sources[k]
            halo[H * k : H * (k + 1)] = s[rows - H :] if dr > 0 else s[:H]
        first, rest = halo[0:SUB], halo[SUB : 2 * F * H]

        def put(dst):
            payload[dst, 0:SUB] = first
            payload[dst, at : at + 2 * F * H - SUB] = rest

        return put

    def cols_to(dc):
        packed = lasts if dc > 0 else firsts
        quarter = rows // 4
        parts = [roll(packed, 4 * SUB * i)[quarter * i : quarter * (i + 1)] for i in range(4)]
        packed = parts[0] + parts[1] + parts[2] + parts[3]

        def put(dst):
            payload[dst, at : at + quarter] = packed

        return put

    def corner_to(dr, dc):
        packed = lasts if dc > 0 else firsts

        def put(dst):
            payload[dst, at : at + H] = packed[rows - H :] if dr > 0 else packed[:H]

        return put

    for dr in (-1, 1):
        send(dr, 0, rows_to(dr))
        send(0, dr, cols_to(dr))
        for dc in (-1, 1):
            send(dr, dc, corner_to(dr, dc))


def toeplitz(gens, late):
    lane = iota((SUB, LANES), 1)
    low = (lane & SUB) == 0
    slid = [slide(wide(gens[k : k + 1])) for k in range(4)]
    re, im = slid[0:2], slid[2:4]
    bases = [
        [jnp.where(low, re[half], -roll(im[half], SUB)) for half in range(2)],
        [jnp.where(low, im[half], roll(re[half], SUB)) for half in range(2)],
    ]
    out = []
    for a1 in range(Q // SUB):
        for first, second in bases:
            tile = jnp.where(lane < LANES - 2 * SUB * a1, first, second)
            out.append(tile if late else roll(tile, 2 * SUB * a1))
    return out


def slide(row):
    return pltpu.roll(row, LANES - SUB, 1, stride=1, stride_axis=0)


TILES = 2 * Q // SUB


def diagonal(k):
    return iota((SUB, LANES), 1) == SUB * k + iota((SUB, LANES), 0)


def to_columns(row):
    return [jnp.sum(jnp.where(diagonal(k), row, 0.0), axis=1, keepdims=True) for k in range(TILES)]


def wide(row):
    return jnp.broadcast_to(row, (SUB, LANES))


def tree_sum(parts):
    while len(parts) > 1:
        parts = [sum(parts[i : i + 2]) for i in range(0, len(parts), 2)]
    return parts[0]


def packed_times(wr, wi, row):
    low = (iota((SUB, LANES), 1) & SUB) == 0
    turned = jnp.where(low, -roll(row, -SUB), roll(row, SUB))
    return wr * row + wi * turned


def column_times(weights, columns, f):
    out = []
    for a1 in range(Q // SUB):
        at = slice(SUB * a1, SUB * (a1 + 1))
        out += times((weights[2 * f, at], weights[2 * f + 1, at]), (columns[2 * a1], columns[2 * a1 + 1]))
    return out


def shares_of(row):
    low = (iota((SUB, LANES), 1) & SUB) == 0
    row = wide(row)
    return jnp.where(low, row, roll(row, SUB)), jnp.where(low, roll(row, -SUB), row)


def row_step(maps, feeds, shares, weights, carry, spread, put, late):
    out = []
    for f in range(F):
        full = feeds[f] if carry is None else carry[f] + feeds[f]
        full = [jnp.where(diagonal(k), full, 0.0) for k in range(TILES)]
        if carry is None:
            put(f, jnp.zeros((SUB, LANES), f32))
        else:
            amp = spread * packed_times(weights[2 * f], weights[2 * f + 1], carry[f])
            put(f, amp)
            turns = [roll(amp, -2 * SUB * a1) if late else amp for a1 in range(Q // SUB)]
            full = [part - tile * turns[k // 2] for k, (part, tile) in enumerate(zip(full, maps(f), strict=True))]
        share = [jnp.sum(jnp.where(diagonal(k), shares[f], 0.0), axis=1, keepdims=True) for k in range(0, TILES, 2)]
        out.append([share[k // 2] * jnp.sum(full[k], axis=1, keepdims=True) for k in range(TILES)])
    return out


def column_step(maps, feeds, shares, columns, carry, spread, put, late):
    out = []
    for f in range(F):
        amp = [spread * part for part in column_times(columns, carry[f], f)]
        put(f, amp)
        tiles = maps(f)
        pairs = [tiles[k] * amp[k] + tiles[k + 1] * amp[k + 1] for k in range(0, TILES, 2)]
        parts = [roll(pair, 2 * SUB * a1) if late else pair for a1, pair in enumerate(pairs)]
        kept = [jnp.where(diagonal(k), carry[f][k], 0.0) for k in range(TILES)]
        total = wide(jnp.sum(tree_sum(kept) - tree_sum(parts), axis=0, keepdims=True))
        out.append(shares[f] * (total + feeds[f]))
    return out


def sweep(n_r, maps, feeds, share, weights, columns, spread, put, late):
    rows = [wide(weights[k : k + 1]) for k in range(2 * F)]

    def pair(j, carry):
        between = row_step(
            lambda f: maps(j, f), feeds(j), shares_of(share(j)), rows, carry, spread, lambda f, v: put(j, f, v),
            late,
        )
        return column_step(
            lambda f: maps(j + 1, f), feeds(j + 1), shares_of(share(j + 1)), columns, between, spread,
            lambda f, v: put(j + 1, f, v), late,
        )

    carry = None
    pairs = (n_r - 1) // 2
    if pairs > 0:
        carry = pair(0, carry)
    if n_r <= SUB:
        for i in range(1, pairs):
            carry = pair(2 * i, carry)
    else:
        carry = lax.fori_loop(1, pairs, lambda i, now: tuple(pair(2 * i, now)), tuple(carry))
    if (n_r - 1) % 2:
        j = n_r - 2
        last = row_step(
            lambda f: maps(j, f), feeds(j), shares_of(share(j)), rows, carry, spread, lambda f, v: put(j, f, v),
            late,
        )
        for f in range(F):
            put(n_r - 1, f, [spread * part for part in column_times(columns, last[f], f)])
    elif carry is not None:
        for f in range(F):
            put(n_r - 1, f, spread * packed_times(rows[2 * f], rows[2 * f + 1], carry[f]))


def putter(amps, held):
    def put(j, f, value):
        if isinstance(value, list):
            put_columns(amps, j, f, value)
        else:
            held[j // 2, f] = value

    return put


def put_columns(amps, j, f, columns):
    for k, column in enumerate(columns):
        amps[j, f, SUB * k : SUB * (k + 1)] = jnp.broadcast_to(column, (SUB, LANES))


def take_rows(amps, held, j):
    for f in range(F):
        put_columns(amps, j, f, to_columns(held[j // 2, f]))


def laps(n, body, few):
    if n <= few:
        for j in range(n):
            body(j)
    else:
        lax.fori_loop(0, n, lambda j, _: (body(j), 0)[1], 0)


def gens_sum(recv, j, n_c, d, c, step, own):
    total = None
    for k in range(n_c):
        part = recv[j * n_c + k, 0:SUB]
        part = jnp.where((j == d + step) & (k == c), own, part)
        total = part if total is None else total + part
    return total


def powers(base, count):
    out = [None, base]
    for _ in range(2, count):
        out.append(times(out[-1], base))
    return out


MERGED = 5


def merged(middle, side):
    sub = iota((SUB, LANES), 0)
    return [
        jnp.where(sub < H, roll(side[0:SUB], H, 0), middle[0:SUB]),
        middle[SUB : 2 * SUB],
        middle[2 * SUB : 3 * SUB],
        jnp.where(sub >= SUB - H, roll(side[3 * SUB :], -H, 0), middle[3 * SUB :]),
        side[SUB : 2 * SUB] + roll(side[2 * SUB : 3 * SUB], LANES // 2),
    ]


def apart(tiles):
    return [roll(tiles[0], -H, 0), tiles[4], roll(tiles[4], LANES // 2), roll(tiles[3], H, 0)]


def merged_places(rows):
    d, c = place_of()
    sub = iota((SUB, LANES), 0)
    lane = iota((SUB, LANES), 1)
    x0 = d * rows + sub
    y0 = c * LANES + lane
    side = y0 + jnp.where(lane < LANES // 2, LANES, -LANES)
    turned = (lane + LANES // 2) & (LANES - 1)
    side_turned = c * LANES + turned + jnp.where(turned < LANES // 2, LANES, -LANES)
    second = (lane >= LANES // 4) & (lane < 3 * LANES // 4)
    return [
        (jnp.where(sub < H, x0 - H, x0 - SUB), jnp.where(sub < H, side, y0)),
        (x0, y0),
        (x0 + SUB, y0),
        (jnp.where(sub >= SUB - H, x0 + rows - (SUB - H), x0 + rows), jnp.where(sub >= SUB - H, side, y0)),
        (jnp.where(second, x0 + SUB, x0), jnp.where(second, side_turned, side)),
    ]


def store_waves(
    fields, cols_a, cols_b, above, below, loss, first, second, carriers, back_first, back_carriers, back_plain, inner, edge_l, edge_r
):
    rows = fields.shape[1]
    ks = range(2 * F, N_FIELDS)
    sides = with_halo(ks, fields, cols_a, cols_b, above, below, inner, edge_l, edge_r)
    tiles = [merged(inner[i], side) for i, side in enumerate(sides)]
    for k in range(2 * F):
        for t in range(MERGED):
            loss[t, k] = tiles[1 + k][t]

    def keep(out, t, values):
        for k, value in enumerate(values):
            for part in range(2):
                out[t, k, part] = value[part]

    for t, (x, y) in enumerate(merged_places(rows)):
        h = tiles[0][t]
        keep(first, t, powers(wave(1, x, 0, y, 0.24, h), Q // SUB)[1:])
        odd = [cos_sin((y & (2 * PERIOD - 1)).astype(f32) * (0.5 / PERIOD) + (0.015 / TURN) * h)]
        whole = square(odd[0])
        for _ in range(SUB // 2 - 1):
            odd.append(times(odd[-1], whole))
        keep(second, t, odd)
        keep(carriers, t, [times(carrier(f, 0, x, y, h), odd[-1]) for f in range(F)])
        if t in (1, 2):
            keep(back_first, t - 1, powers(wave(-1, x, 0, y, 0.24, h), Q // SUB)[1:])
            plain = [carrier(f, 1, x, y, h) for f in range(F)]
            keep(back_plain, t - 1, plain)
            keep(back_carriers, t - 1, [times(part, odd[-1]) for part in plain])


def radiated(amps, at, f, first, second, carriers, tiles, shift):
    splat = lambda a: wide(amps[at, f, a : a + 1])
    totals = [None] * len(tiles)
    for a1 in range(Q // SUB):
        base = 2 * SUB * a1
        pairs = []
        for i in range(SUB // 2):
            up, low = SUB // 2 + i, SUB // 2 - 1 - i
            re = splat(base + up), splat(base + low)
            im = splat(base + SUB + up), splat(base + SUB + low)
            pairs.append((re[0] + re[1], re[0] - re[1], im[0] + im[1], im[0] - im[1]))
        for n, t in enumerate(tiles):
            inner = None
            for i, (re_sum, re_gap, im_sum, im_gap) in enumerate(pairs):
                cos, sin = second[t + shift, i, 0], second[t + shift, i, 1]
                got = (re_sum * cos - im_gap * sin, im_sum * cos + re_gap * sin)
                inner = got if inner is None else (inner[0] + got[0], inner[1] + got[1])
            if a1 > 0:
                got = times((first[t, a1 - 1, 0], first[t, a1 - 1, 1]), inner)
                inner = (totals[n][0] + got[0], totals[n][1] + got[1])
            totals[n] = inner
    return [times((carriers[t, f, 0], carriers[t, f, 1]), total) for t, total in zip(tiles, totals, strict=True)]


def new_body(
    n_r, n_c, spread, recv, green, edge_green, source, fields, cols_b, cols_a, rows_b, rows_a, tables, weights, columns,
    forward, driven, payload, second, back_first, back_carriers, below_gens,
    loss, first, carriers, back_plain, amps, kept, held, inner, moved, edge_l, edge_r, spill, cs, left_mat, right_mat, common, halo,
):
    rows = fields.shape[1]
    d, c = place_of()
    above_rows, below_rows = halo_rows(rows_a, rows_b)
    above = above_rows[GENS_AT:]
    below_gens[...] = below_rows[GENS_AT:]
    store_waves(
        fields, cols_a, cols_b, above_rows, below_rows,
        loss, first, second, carriers, back_first, back_carriers, back_plain, held, edge_l, edge_r,
    )

    if n_r <= SUB:
        sums = [gens_sum(recv, j, n_c, d, c, -1, above) for j in range(n_r - 1)]

    def maps(j, f):
        gens = sums[j] if n_r <= SUB else gens_sum(recv, j, n_c, d, c, -1, above)
        return toeplitz(gens[4 * f : 4 * f + 4], False)

    def feeds(j):
        feed = recv[j * n_c, SUB : 2 * SUB]
        for k in range(1, n_c):
            feed = feed + recv[j * n_c + k, SUB : 2 * SUB]
        return [wide(feed[f : f + 1]) for f in range(F)]

    sweep(n_r, maps, feeds, lambda j: recv[j * n_c, SUB + 2 : SUB + 3], weights, columns, spread, putter(amps, kept), False)
    even = d - (d & 1)
    take_rows(amps, kept, even)
    take_rows(amps, kept, jnp.minimum(even + 2 * (d & 1), n_r - 1 - ((n_r - 1) & 1)))

    at = HALO_AT

    def got(dr, dc, start, size):
        src = jnp.clip(d + dr, 0, n_r - 1) * n_c + jnp.clip(c + dc, 0, n_c - 1)
        ok = (d + dr >= 0) & (d + dr < n_r) & (c + dc >= 0) & (c + dc < n_c)
        return jnp.where(ok, recv[src, start : start + size], 0.0)

    edge_l[...] = jnp.zeros(edge_l.shape, f32)
    edge_r[...] = jnp.zeros(edge_r.shape, f32)
    quarter = rows // 4
    for edge, dc in ((edge_l, -1), (edge_r, 1)):
        side = got(0, dc, at, quarter)
        for i in range(4):
            edge[TOP + quarter * i : TOP + quarter * (i + 1)] = roll(side, -4 * SUB * i)
        edge[TOP - H : TOP] = got(-1, dc, at, H)
        edge[TOP + rows : TOP + rows + H] = got(1, dc, at, H)
    from_left, from_right = edge_l[...], edge_r[...]
    for i, dr in enumerate((-1, 1)):
        halo[i, 0:SUB] = got(dr, 0, 0, SUB)
        halo[i, SUB : 2 * F * H] = got(dr, 0, at, 2 * F * H - SUB)
    for k in range(2 * F):
        inner[k] = jnp.zeros(inner.shape[1:], f32)
        inner[k, TOP : TOP + rows] = source[k]
        inner[k, TOP - H : TOP] = halo[0, H * k : H * (k + 1)]
        inner[k, TOP + rows : TOP + rows + H] = halo[1, H * k : H * (k + 1)]
    sides = [unpack_columns(from_left, from_right, k) for k in range(2 * F)]

    weak = {}
    lost = {}
    for step, group in ((-1, (0,)), (0, (1, 2, 4)), (1, (3,))):
        at = jnp.clip(d + step, 0, n_r - 1)
        for f in range(F):
            for t, w in zip(group, radiated(amps, at, f, first, second, carriers, group, 0), strict=True):
                got = times((loss[t, 2 * f], loss[t, 2 * f + 1]), w)
                for part in range(2):
                    weak[t, 2 * f + part] = w[part]
                    lost[t, 2 * f + part] = got[part]
    beyond = []
    for k in range(2 * F):
        tiles = [lost[t, k] for t in range(MERGED)]
        side = sides[k] - jnp.concatenate(apart(tiles), axis=0)
        middle = inner[k] - jnp.concatenate(tiles[:4], axis=0)
        forward[k] = middle[TOP : TOP + rows]
        for i in range(SHIFTS):
            moved[k * SHIFTS + i, 0:TOP] = jnp.zeros((TOP, LANES), f32)
            moved[k * SHIFTS + i, TOP + rows :] = jnp.zeros((TOP, LANES), f32)
        store_shifted(moved, k, middle[TOP : TOP + rows], side[TOP : TOP + rows])
        above_edge = range(TOP - 1, TOP - 1 - H, -1)
        below_edge = range(TOP + rows, TOP + rows + H)
        pairs = [pair_rows(row_list(part, above_edge), row_list(part, below_edge), True) for part in (middle, side)]
        beyond.append([shifted(*pairs, dy) for dy in range(-H, H + 1)])
    near = [jnp.zeros((2 * SUB, LANES), f32) for _ in range(2 * F)]
    for dy in range(-H, H + 1):
        add_near(near, [edge_green[4 * (dy + H) + k] for k in range(2 * F)], lambda k: beyond[k][dy + H])
    for k in range(2 * F):
        put_pairs(near[k], spill, k)
    near = [spill[k] for k in range(2 * F)]
    for code in range(OFFSETS):
        dx, dy = offset_of(code)
        add_near(
            near,
            [green[4 * code + k] for k in range(2 * F)],
            lambda k: moved[k * SHIFTS + dy + H, TOP + dx : TOP + dx + rows],
        )
    for f in range(F):
        rest = []
        for part in range(2):
            k = 2 * f + part
            w = jnp.concatenate([weak[1, k], weak[2, k]], axis=0)
            rest.append(fields[N_FIELDS + k] - near[k] - w)
        s = times((fields[2 * F + 1 + 2 * f], fields[2 * F + 2 + 2 * f]), rest)
        driven[2 * f] = s[0]
        driven[2 * f + 1] = s[1]
        base = [jnp.concatenate([back_plain[t, f, part] for t in range(2)], axis=0) for part in range(2)]
        add = conj_times(base, s)
        cs[2 * f] = add[0]
        cs[2 * f + 1] = add[1]

    def keep(f, row):
        common[f : f + 1] = row

    right_mat[2 * SUB :] = jnp.zeros((right_mat.shape[0] - 2 * SUB, right_mat.shape[1]), f32)
    project(left_mat, right_mat, tables, 2, cs, rows, keep)
    pair = common[0:2]

    def fill(s):
        payload[s] = pair

    laps(n_r * n_c, fill, 8 * SUB)


def last_body(
    n_r, n_c, spread, recv, fed, new, driven, fields, weights, columns, first, second, carriers, below_gens,
    forward, currents, amps, kept,
):
    rows = fields.shape[1]
    d, c = place_of()
    forward[...] = new[...]
    below = below_gens[...]

    def feeds(k):
        j = n_r - 1 - k
        feed = fed[j * n_c]
        for i in range(1, n_c):
            feed = feed + fed[j * n_c + i]
        return [wide(feed[f : f + 1]) for f in range(F)]

    def share(k):
        return recv[(n_r - 1 - k) * n_c, SUB + 2 : SUB + 3]

    def maps(k, f):
        return toeplitz(gens_sum(recv, n_r - 1 - k, n_c, d, c, 1, below)[4 * f : 4 * f + 4], True)

    sweep(n_r, maps, feeds, share, weights, columns, spread, putter(amps, kept), True)
    at = n_r - 1 - d
    take_rows(amps, kept, at - (at & 1))
    tiles = tuple(range(rows // SUB))
    for f in range(F):
        for tile, w in zip(tiles, radiated(amps, at, f, first, second, carriers, tiles, 1), strict=True):
            rows_at = slice(SUB * tile, SUB * (tile + 1))
            lost = times((fields[2 * F + 1 + 2 * f, rows_at], fields[2 * F + 2 + 2 * f, rows_at]), w)
            currents[2 * f, rows_at] = driven[2 * f, rows_at] - lost[0]
            currents[2 * f + 1, rows_at] = driven[2 * f + 1, rows_at] - lost[1]


def swaps(n):
    first = [(i, i ^ 1) for i in range(n) if i ^ 1 < n]
    second = [(i, i + 1) for i in range(1, n - 1, 2)] + [(i + 1, i) for i in range(1, n - 1, 2)]
    return first, second


def swap(axis, n, a, b):
    first, second = swaps(n)
    b = lax.ppermute(b, axis, second)
    return lax.ppermute(a, axis, first), b


def stacked(arrays):
    rows, cols = arrays[0].shape[1:]
    total = sum(array.shape[0] for array in arrays)
    out, at = None, 0
    for array in arrays:
        count = array.shape[0]
        wide_array = jnp.pad(
            array, ((at, total - at - count), (0, rows - array.shape[1]), (0, cols - array.shape[2]))
        )
        out = wide_array if out is None else out + wide_array
        at += count
    return out


def per_device(n_r, n_c, incident, inverse_diag, previous, heights, neighbours, counts, transmit, angle_weights):
    rows, cols = heights.shape
    patches = rows * cols
    spread = 1.0 / math.sqrt(rows * cols * n_c)
    slots = n_r * n_c
    tall = rows + 2 * SUB
    fields = stacked([previous, heights[None], inverse_diag, incident, angle_weights, transmit])
    cols_b, cols_a = call(columns_body, [(rows, LANES)] * 2, [VMEM], flops=400_000_000)(fields)
    cols_a, cols_b = swap("xr", n_c, cols_a, cols_b)
    tables, gens = call(
        functools.partial(tables_body, n_r),
        [(6, rows, SUB, LANES), (2 * SUB, LANES)],
        [VMEM],
        [pltpu.VMEM((16 * SUB, patches), f32), pltpu.VMEM((16 * SUB, patches), f32)],
    )(fields)
    weights, share, columns = call(
        params_body, [(2 * F, LANES), (1, LANES), (2 * F, Q, LANES)], [VMEM], flops=400_000_000
    )(fields)
    gens, weights, share, columns = lax.optimization_barrier((gens, weights, share, columns))
    rows_b, rows_a = call(rows_body, [(ROWS_SENT, LANES)] * 2, [VMEM] * 4, flops=400_000_000)(fields, gens, cols_b, cols_a)
    rows_a, rows_b = swap("rng", n_r, rows_a, rows_b)
    green, inner_near, bits = call(
        inner_body,
        [
            (4 * OFFSETS, rows, LANES),
            (2 * F, rows, LANES),
            jax.ShapeDtypeStruct((2, rows, LANES), jnp.int32),
        ],
        [VMEM] * 5,
        [pltpu.VMEM(((2 * F + 1) * SHIFTS, tall, LANES), f32)],
        400_000_000,
    )(fields, neighbours, counts, cols_b, cols_a)
    edges = [pltpu.VMEM((tall, LANES), f32)] * 2
    payload, edge_green, source = call(
        functools.partial(near_body, n_r, n_c),
        [(slots, SLOT, LANES), (4 * SHIFTS, 2 * SUB, LANES), (2 * F, rows, LANES)],
        [VMEM] * 10,
        [
            pltpu.VMEM((2 * F, rows, LANES), f32),
            pltpu.VMEM((2 * F, rows, LANES), f32),
            pltpu.VMEM((4 * SUB, patches), f32),
            pltpu.VMEM((16 * SUB, patches), f32),
            pltpu.VMEM((3 * SUB, LANES), f32),
            pltpu.VMEM((2 * SUB, LANES), f32),
        ],
    )(fields, bits, inner_near, share, cols_b, cols_a, rows_b, rows_a, gens, tables)
    recv = lax.all_to_all(payload, BOTH, 0, 0)
    tile = (2, SUB, LANES)
    new, driven, payload, second, back_first, back_carriers, below_gens = call(
        functools.partial(new_body, n_r, n_c, spread),
        [
            (2 * F, rows, LANES),
            (2 * F, rows, LANES),
            (slots, 2, LANES),
            (MERGED, SUB // 2, *tile),
            (2, Q // SUB - 1, *tile),
            (2, F, *tile),
            (SUB, LANES),
        ],
        [VMEM] * 12,
        [
            pltpu.VMEM((MERGED, 2 * F, SUB, LANES), f32),
            pltpu.VMEM((MERGED, Q // SUB - 1, *tile), f32),
            pltpu.VMEM((MERGED, F, *tile), f32),
            pltpu.VMEM((2, F, *tile), f32),
            pltpu.VMEM((n_r, F, 2 * Q, LANES), f32),
            pltpu.VMEM(((n_r + 1) // 2, F, SUB, LANES), f32),
            pltpu.VMEM((2 * F + 1, tall, LANES), f32),
            pltpu.VMEM((2 * F, tall, LANES), f32),
            pltpu.VMEM((2 * F * (2 * H + 1), tall, LANES), f32),
            *edges,
            pltpu.VMEM((2 * F, rows, LANES), f32),
            pltpu.VMEM((2 * F, rows, LANES), f32),
            pltpu.VMEM((4 * SUB, patches), f32),
            pltpu.VMEM((16 * SUB, patches), f32),
            pltpu.VMEM((SUB, LANES), f32),
            pltpu.VMEM((2, 2 * SUB, LANES), f32),
        ],
    )(recv, green, edge_green, source, fields, cols_b, cols_a, rows_b, rows_a, tables, weights, columns)
    fed = lax.all_to_all(payload, BOTH, 0, 0)
    return call(
        functools.partial(last_body, n_r, n_c, spread),
        [(2 * F, rows, LANES), (2 * F, rows, LANES)],
        [VMEM] * 11,
        [pltpu.VMEM((n_r, F, 2 * Q, LANES), f32), pltpu.VMEM(((n_r + 1) // 2, F, SUB, LANES), f32)],
    )(recv, fed, new, driven, fields, weights, columns, back_first, second, back_carriers, below_gens)


def solution(mesh):
    body = functools.partial(per_device, mesh.shape["rng"], mesh.shape["xr"])
    field = P(None, "rng", "xr")
    return jax.shard_map(
        body,
        mesh=mesh,
        in_specs=(field, field, field, P("rng", "xr"), field, P("rng", "xr"), P("rng", None, None), P()),
        out_specs=(field, field),
        check_vma=False,
    )
```

```python
import functools
import math

import jax
import jax.numpy as jnp
from jax import lax
from jax.experimental import pallas as pl
from jax.experimental.pallas import tpu as pltpu
from jax.sharding import PartitionSpec as P

F = 2
Q = 64
H = 3
LMAX = 24
OFFSETS = 48
SUB = 8
LANES = 128
PERIOD = 64
TOP = SUB
GREEN = 0.25
TURN = 2.0 * math.pi
SLOT = 16
HALO_AT = SUB + 3
HIGHEST = lax.Precision.HIGHEST
BOTH = ("rng", "xr")
f32 = jnp.float32


def iota(shape, dim):
    return lax.broadcasted_iota(jnp.int32, shape, dim)


def roll(x, shift, axis=1):
    shift = shift % x.shape[axis]
    return x if shift == 0 else pltpu.roll(x, shift, axis)


def cos_sin(turns):
    quarter = jnp.floor(4.0 * turns + 0.5)
    rest = turns - 0.25 * quarter
    which = quarter.astype(jnp.int32)
    sq = rest * rest
    s = rest * (TURN + sq * (-(TURN**3) / 6 + sq * (TURN**5 / 120 + sq * (-(TURN**7) / 5040 + sq * (TURN**9 / 362880)))))
    c = 1.0 + sq * (-(TURN**2) / 2 + sq * (TURN**4 / 24 + sq * (-(TURN**6) / 720 + sq * (TURN**8 / 40320))))
    odd = (which & 1) == 1
    cos = jnp.where(odd, s, c)
    sin = jnp.where(odd, c, s)
    cos = jnp.where(((which + 1) & 2) == 2, -cos, cos)
    sin = jnp.where((which & 2) == 2, -sin, sin)
    return cos, sin


def times(a, b):
    return a[0] * b[0] - a[1] * b[1], a[0] * b[1] + a[1] * b[0]


def conj_times(a, b):
    return a[0] * b[0] + a[1] * b[1], a[0] * b[1] - a[1] * b[0]


def wave(step_x, x, step_y, y, lift, heights):
    phase = (step_x * x + step_y * y) & (PERIOD - 1)
    return cos_sin(phase.astype(f32) * (1.0 / PERIOD) + (lift / TURN) * heights)


def offset_of(code):
    full = code + (1 if code >= OFFSETS // 2 else 0)
    return full // (2 * H + 1) - H, full % (2 * H + 1) - H


VMEM = pl.BlockSpec(memory_space=pltpu.VMEM)
PLAIN = pl.BlockSpec()


def call(body, out, ins, scratch=(), flops=2_000_000_000):
    return pl.pallas_call(
        body,
        out_shape=tuple(jax.ShapeDtypeStruct(s, f32) if isinstance(s, tuple) else s for s in out),
        in_specs=list(ins),
        out_specs=tuple(VMEM for _ in out),
        scratch_shapes=list(scratch),
        compiler_params=pltpu.CompilerParams(vmem_limit_bytes=48 * 1024 * 1024),
        cost_estimate=pl.CostEstimate(flops=flops, bytes_accessed=1 << 20, transcendentals=0),
    )


def place_of():
    return lax.axis_index("rng"), lax.axis_index("xr")


def pack_columns(fields, right):
    rows = fields[0].shape[0]
    lane = iota((rows, LANES), 1)
    packed = jnp.zeros((rows, LANES), f32)
    for k, field in enumerate(fields):
        moved = roll(field, H * k - (LANES - H) if right else H * k)
        packed = jnp.where((lane >= H * k) & (lane < H * (k + 1)), moved, packed)
    return packed


def unpack_columns(from_left, from_right, k):
    lane = iota(from_left.shape, 1)
    left = jnp.where(lane >= LANES - H, roll(from_left, LANES - H - H * k), 0.0)
    return jnp.where(lane < H, roll(from_right, -H * k), left)


def shifted(inner, edge, dy):
    if dy == 0:
        return inner
    lane = iota(inner.shape, 1)
    outside = lane >= LANES - dy if dy > 0 else lane < -dy
    return jnp.where(outside, roll(edge, -dy), roll(inner, -dy))


N_FIELDS = 4 * F + 1
ROWS_SENT = 48
GENS_AT = 40


def columns_body(fields, send_b, send_a):
    values = [fields[k] for k in range(N_FIELDS)]
    right = pack_columns(values, True)
    left = pack_columns(values, False)
    even = (lax.axis_index("xr") & 1) == 0
    send_a[...] = jnp.where(even, right, left)
    send_b[...] = jnp.where(even, left, right)


def rows_body(fields, gens, recv_b, recv_a, send_b, send_a):
    d, c = place_of()
    even_c = (c & 1) == 0
    even_r = (d & 1) == 0
    rows = fields.shape[1]
    values = [fields[k] for k in range(N_FIELDS)]
    values.append(jnp.where(even_c, recv_b[...], recv_a[...]))
    values.append(jnp.where(even_c, recv_a[...], recv_b[...]))
    for k, field in enumerate(values):
        last, first = field[rows - H :], field[:H]
        send_a[H * k : H * (k + 1)] = jnp.where(even_r, last, first)
        send_b[H * k : H * (k + 1)] = jnp.where(even_r, first, last)
    used = H * len(values)
    send_a[used:GENS_AT] = jnp.zeros((GENS_AT - used, LANES), f32)
    send_b[used:GENS_AT] = jnp.zeros((GENS_AT - used, LANES), f32)
    down, up = gens[0:SUB], gens[SUB : 2 * SUB]
    send_a[GENS_AT:] = jnp.where(even_r, down, up)
    send_b[GENS_AT:] = jnp.where(even_r, up, down)


def tables_body(n_r, fields, tables, gens, left_mat, right_mat):
    d, c = place_of()
    turned = [d & 1, (n_r - 1 - d) & 1]
    signs = [jnp.where(t == 1, -1.0, 1.0) for t in turned]
    rows = fields.shape[1]
    x0 = d * rows
    y0 = c * LANES
    angle = iota((2 * SUB, LANES), 0) - SUB
    y = iota((2 * SUB, LANES), 1) + y0
    for i in range(rows):
        x = jnp.full((2 * SUB, LANES), x0 + i, jnp.int32)
        lanes = pl.ds(i * LANES, LANES)
        h2 = jnp.broadcast_to(fields[2 * F, i : i + 1, :], (2 * SUB, LANES)) * angle.astype(f32)
        c2, s2 = wave(0, x, angle, y, 0.03, h2)
        tables[4, i] = c2[SUB:]
        tables[5, i] = s2[SUB:]
        right_mat[0 : 2 * SUB, lanes] = c2
        right_mat[2 * SUB : 4 * SUB, lanes] = s2
        for direction in range(2):
            c1, s1 = wave(angle * (1 - 2 * direction), x, 0, y, 0.24, h2)
            tables[2 * direction, i] = c1[SUB:]
            tables[2 * direction + 1, i] = s1[SUB:]
            s1 = signs[direction] * s1
            for f in range(F):
                zr = fields[2 * F + 1 + 2 * f, i : i + 1, :]
                zi = fields[2 * F + 2 + 2 * f, i : i + 1, :]
                base = (direction * F + f) * 4 * SUB
                left_mat[base : base + 2 * SUB, lanes] = zr * c1 - zi * s1
                left_mat[base + 2 * SUB : base + 4 * SUB, lanes] = zr * s1 + zi * c1
    both = lax.dot_general(
        left_mat[...], right_mat[...], (((1,), (1,)), ((), ())), precision=HIGHEST, preferred_element_type=f32
    )
    both = jnp.concatenate([both, jnp.zeros((16 * SUB, LANES - 4 * SUB), f32)], axis=1)
    lane = iota((SUB, LANES), 1)
    for direction in range(2):
        for f in range(F):
            base = (direction * F + f) * 4 * SUB
            for half in range(2):
                p = both[base + half * SUB : base + (half + 1) * SUB]
                q = both[base + (2 + half) * SUB : base + (3 + half) * SUB]
                for part in range(2):
                    sign = signs[direction]
                    if part == 0:
                        g = p - sign * roll(q, -2 * SUB)
                    else:
                        g = roll(p, -2 * SUB) + sign * q
                    g = jnp.where(lane < 2 * SUB, g, 0.0)
                    g = pltpu.roll(g, 0, 1, stride=2 * SUB, stride_axis=0)
                    row = jnp.sum(g, axis=0, keepdims=True)
                    at = direction * SUB + f * 4 + part * 2 + (1 - half)
                    gens[at : at + 1] = row


def list_bits(neighbours, counts):
    count = counts[...]
    low = jnp.zeros(count.shape, jnp.int32)
    high = jnp.zeros(count.shape, jnp.int32)
    half = OFFSETS // 2
    one = jnp.ones(count.shape, jnp.int32)
    for slot in range(LMAX):
        code = neighbours[slot]
        live = count > slot
        is_low = code < half
        bit = lax.shift_left(one, jnp.where(is_low, code, code - half))
        low = low | jnp.where(live & is_low, bit, 0)
        high = high | jnp.where(live & (code >= half), bit, 0)
    return low, high


def params_body(fields, weights, share, columns):
    spot = iota((LANES, LANES), 0)
    spot = jnp.where(spot < Q, 2 * SUB * (spot // SUB) + (spot & (SUB - 1)), 2 * LANES)
    base = N_FIELDS + 2 * F
    values = jnp.concatenate([fields[base + i, 0:2] for i in range(F + 1)] + [fields[base + F, 2:4]], axis=0)
    placed = [
        lax.dot_general(
            values,
            (iota((LANES, LANES), 1) == spot + SUB * k).astype(f32),
            (((1,), (0,)), ((), ())),
            precision=HIGHEST,
            preferred_element_type=f32,
        )
        for k in range(2)
    ]
    weights[...] = placed[0][: 2 * F] + placed[1][: 2 * F]
    share[...] = placed[0][2 * F : 2 * F + 1] + placed[1][2 * F + 1 : 2 * F + 2]
    for k in range(2 * F):
        for a1, column in enumerate(to_columns(wide(placed[0][k : k + 1]))[::2]):
            columns[k, SUB * a1 : SUB * (a1 + 1)] = wide(column)


def project(left_mat, right_mat, tables, first, cs, rows, f_out):
    for i in range(rows):
        lanes = pl.ds(i * LANES, LANES)
        right_mat[0:SUB, lanes] = tables[4, i]
        right_mat[SUB : 2 * SUB, lanes] = tables[5, i]
        c1, s1 = tables[first, i], tables[first + 1, i]
        for f in range(F):
            re, im = conj_times((c1, s1), (cs[2 * f, i : i + 1, :], cs[2 * f + 1, i : i + 1, :]))
            left_mat[2 * f * SUB : (2 * f + 1) * SUB, lanes] = re
            left_mat[(2 * f + 1) * SUB : (2 * f + 2) * SUB, lanes] = im
    sums = lax.dot_general(
        left_mat[0 : 4 * SUB], right_mat[...], (((1,), (1,)), ((), ())), precision=HIGHEST, preferred_element_type=f32
    )
    sums = jnp.concatenate([sums, jnp.zeros((4 * SUB, LANES - 2 * SUB), f32)], axis=1)
    lane = iota((SUB, LANES), 1)
    for f in range(F):
        gr = sums[2 * f * SUB : (2 * f + 1) * SUB]
        gi = sums[(2 * f + 1) * SUB : (2 * f + 2) * SUB]
        re = gr + roll(gi, -SUB)
        im = gi - roll(gr, -SUB)
        packed = jnp.where(lane < SUB, re, jnp.where(lane < 2 * SUB, roll(im, SUB), 0.0))
        packed = pltpu.roll(packed, 0, 1, stride=2 * SUB, stride_axis=0)
        f_out(f, jnp.sum(packed, axis=0, keepdims=True))


def carrier(f, direction, x, y, heights):
    sign = 1 - 2 * direction
    return wave(sign * (1 + 2 * f), x, f - 4, y, 0.3 + 0.2 * f, heights)


def place_ids(rows, cols, first_row, first_col, own_rows):
    d, c = place_of()
    x = d * own_rows + first_row + iota((rows, cols), 0)
    y = c * LANES + first_col + iota((rows, cols), 1)
    return x, y


def halo_rows(rows_a, rows_b):
    even = (lax.axis_index("rng") & 1) == 0
    return jnp.where(even, rows_b[...], rows_a[...]), jnp.where(even, rows_a[...], rows_b[...])


def with_halo(ks, fields, cols_a, cols_b, above, below, inner, edge_l, edge_r):
    rows = fields.shape[1]
    even = (lax.axis_index("xr") & 1) == 0
    edge_l[...] = jnp.zeros(edge_l.shape, f32)
    edge_r[...] = jnp.zeros(edge_r.shape, f32)
    edge_l[TOP : TOP + rows] = jnp.where(even, cols_b[...], cols_a[...])
    edge_r[TOP : TOP + rows] = jnp.where(even, cols_a[...], cols_b[...])
    at = H * N_FIELDS
    edge_l[TOP - H : TOP] = above[at : at + H]
    edge_l[TOP + rows : TOP + rows + H] = below[at : at + H]
    edge_r[TOP - H : TOP] = above[at + H : at + 2 * H]
    edge_r[TOP + rows : TOP + rows + H] = below[at + H : at + 2 * H]
    from_left, from_right = edge_l[...], edge_r[...]
    sides = []
    for i, k in enumerate(ks):
        inner[i] = jnp.zeros(inner.shape[1:], f32)
        inner[i, TOP : TOP + rows] = fields[k]
        inner[i, TOP - H : TOP] = above[H * k : H * (k + 1)]
        inner[i, TOP + rows : TOP + rows + H] = below[H * k : H * (k + 1)]
        sides.append(unpack_columns(from_left, from_right, k))
    return sides


PAIRS = [(row, beyond) for row in range(H) for beyond in range(H - row)]
SHIFTS = 2 * H + 1


def pair_rows(top, bottom, beyond):
    which = [pair[1 if beyond else 0] for pair in PAIRS]
    rest = jnp.zeros((SUB - len(PAIRS), LANES), top[0].dtype)
    parts = []
    for edge in (top, bottom):
        parts += [edge[i] for i in which] + [rest]
    return jnp.concatenate(parts, axis=0)


def row_list(array, indices):
    return [array[i : i + 1] for i in indices]


def put_pairs(near, spill, k):
    rows = spill.shape[1]
    spill[k] = jnp.zeros(spill.shape[1:], f32)
    for edge in range(2):
        at = SUB * edge
        for row in range(H):
            count = H - row
            total = near[at : at + 1]
            for i in range(1, count):
                total = total + near[at + i : at + i + 1]
            at += count
            to = rows - 1 - row if edge else row
            spill[k, to : to + 1] = total


def coupling(squared, there):
    inverse_r = lax.rsqrt(squared)
    size = jnp.where(there, GREEN * inverse_r, 0.0)
    off = squared * inverse_r * (1.0 / 16.0) - 0.25
    sq = off * off
    w = (-off * polynomial(SINE, sq), polynomial(COSINE, sq))
    fourth = square(square(w))
    out = []
    for power in (fourth, times(fourth, w)):
        out += [size * power[0], size * power[1]]
    return out


def square(a):
    return a[0] * a[0] - a[1] * a[1], 2.0 * a[0] * a[1]


def polynomial(coefficients, x):
    total = coefficients[-1]
    for value in coefficients[-2::-1]:
        total = total * x + value
    return total


SINE = (6.283185280367426, -41.341680722295834, 81.60248507719457, -76.58139539835082, 39.76160778337109)
COSINE = (1.0, -19.739208548909147, 64.93934662883956, -85.4535715937672, 60.144014415422156, -24.982233003994804)


def add_near(near, g, window):
    for f in range(F):
        got = times((g[2 * f], g[2 * f + 1]), (window(2 * f), window(2 * f + 1)))
        near[2 * f] = near[2 * f] + got[0]
        near[2 * f + 1] = near[2 * f + 1] + got[1]


def side_columns(cols_a, cols_b):
    even = (lax.axis_index("xr") & 1) == 0
    return jnp.where(even, cols_b[...], cols_a[...]), jnp.where(even, cols_a[...], cols_b[...])


def store_shifted(moved, k, middle, side):
    rows = middle.shape[0]
    for dy in range(-H, H + 1):
        moved[k * SHIFTS + dy + H, TOP : TOP + rows] = shifted(middle, side, dy)


def inner_body(fields, neighbours, counts, cols_b, cols_a, green, near_out, bits, moved):
    rows = fields.shape[1]
    low, high = list_bits(neighbours, counts)
    bits[0] = low
    bits[1] = high
    from_left, from_right = side_columns(cols_a, cols_b)
    for k in range(2 * F + 1):
        for i in range(SHIFTS):
            moved[k * SHIFTS + i, 0:TOP] = jnp.zeros((TOP, LANES), f32)
            moved[k * SHIFTS + i, TOP + rows :] = jnp.zeros((TOP, LANES), f32)
        store_shifted(moved, k, fields[k], unpack_columns(from_left, from_right, k))
    h = fields[2 * F]
    half = OFFSETS // 2
    row = iota((rows, LANES), 0)
    masked = {}
    for dx in range(-H, H + 1):
        inside = (row + dx >= 0) & (row + dx < rows)
        masked[dx] = (jnp.where(inside, low, 0), jnp.where(inside, high, 0))
    near = [jnp.zeros((rows, LANES), f32) for _ in range(2 * F)]
    for code in range(OFFSETS):
        dx, dy = offset_of(code)
        window = lambda k: moved[k * SHIFTS + dy + H, TOP + dx : TOP + dx + rows]
        lift = window(2 * F) - h
        there = (masked[dx][code // half] & (1 << (code % half))) != 0
        g = coupling(float(dx * dx + dy * dy) + lift * lift, there)
        for k in range(2 * F):
            green[4 * code + k] = g[k]
        add_near(near, g, window)
    for k in range(2 * F):
        near_out[k] = near[k]


def near_body(
    n_r, n_c, fields, bits, inner_near, share, cols_b, cols_a, rows_b, rows_a, gens, tables,
    payload, edge_green, source, spill, cs, left_mat, right_mat, common, halo,
):
    rows = fields.shape[1]
    d, c = place_of()
    above, below = halo_rows(rows_a, rows_b)
    backwards = range(H - 1, -1, -1)
    last_rows = range(rows - 1, rows - 1 - H, -1)
    at = H * N_FIELDS
    from_left, from_right = (
        pair_rows(
            row_list(above[at + H * i : at + H * (i + 1)], backwards),
            row_list(below[at + H * i : at + H * (i + 1)], range(H)),
            True,
        )
        for i in range(2)
    )
    h = fields[2 * F]
    inverse = [fields[2 * F + 1 + k] for k in range(2 * F)]
    incident = [fields[N_FIELDS + k] for k in range(2 * F)]
    h_pairs = pair_rows(row_list(h, range(H)), row_list(h, last_rows), False)
    flags = pair_rows(row_list(bits[0], range(H)), row_list(bits[1], last_rows), False)
    row = iota((2 * SUB, LANES), 0)
    lower = row >= SUB
    nth = row & (SUB - 1)
    reach = jnp.zeros((2 * SUB, LANES), jnp.int32)
    for i, (inside, beyond) in enumerate(PAIRS):
        reach = jnp.where(nth == i, inside + beyond + 1, reach)
    first_bit = jnp.where(lower, (H + reach) * SHIFTS + H - 1 - OFFSETS // 2, (H - reach) * SHIFTS + H)
    moved = []
    for k in range(2 * F + 1):
        middle = pair_rows(
            row_list(above[H * k : H * (k + 1)], backwards), row_list(below[H * k : H * (k + 1)], range(H)), True
        )
        side = unpack_columns(from_left, from_right, k)
        moved.append([shifted(middle, side, dy) for dy in range(-H, H + 1)])
    near = [jnp.zeros((2 * SUB, LANES), f32) for _ in range(2 * F)]
    for dy in range(-H, H + 1):
        lift = moved[2 * F][dy + H] - h_pairs
        there = (lax.shift_right_logical(flags, first_bit + dy) & 1) == 1
        g = coupling((reach * reach + dy * dy).astype(f32) + lift * lift, there & (nth < len(PAIRS)))
        for k in range(2 * F):
            edge_green[4 * (dy + H) + k] = g[k]
        add_near(near, g, lambda k: moved[k][dy + H])
    for k in range(2 * F):
        put_pairs(near[k], spill, k)
    near = [inner_near[k] + spill[k] for k in range(2 * F)]
    x, y = place_ids(rows, LANES, 0, 0, rows)
    sources = []
    for f in range(F):
        z = (inverse[2 * f], inverse[2 * f + 1])
        s = times(z, (incident[2 * f] - near[2 * f], incident[2 * f + 1] - near[2 * f + 1]))
        sources += s
        source[2 * f] = s[0]
        source[2 * f + 1] = s[1]
        got = conj_times(carrier(f, 0, x, y, h), s)
        cs[2 * f] = got[0]
        cs[2 * f + 1] = got[1]

    def keep(f, row):
        common[2 * SUB + f : 2 * SUB + f + 1] = row

    common[2 * SUB :] = jnp.zeros((SUB, LANES), f32)
    project(left_mat, right_mat, tables, 0, cs, rows, keep)
    common[0 : 2 * SUB] = gens[...]
    common[2 * SUB + 2 : 2 * SUB + 3] = share[...]
    tail = common[2 * SUB : 3 * SUB]
    down, up = common[0:SUB], common[SUB : 2 * SUB]

    def fill(s):
        payload[s, 0:SUB] = jnp.where(s >= d * n_c, down, up)
        payload[s, SUB : 2 * SUB] = tail

    laps(n_r * n_c, fill, 8 * SUB)
    lasts = pack_columns(sources, True)
    firsts = pack_columns(sources, False)
    at = HALO_AT

    def send(dr, dc, put):
        dst = (d + dr) * n_c + c + dc
        ok = (d + dr >= 0) & (d + dr < n_r) & (c + dc >= 0) & (c + dc < n_c)

        @pl.when(ok)
        def _():
            put(dst)

    def rows_to(dr):
        for k in range(2 * F):
            s = sources[k]
            halo[H * k : H * (k + 1)] = s[rows - H :] if dr > 0 else s[:H]
        first, rest = halo[0:SUB], halo[SUB : 2 * F * H]

        def put(dst):
            payload[dst, 0:SUB] = first
            payload[dst, at : at + 2 * F * H - SUB] = rest

        return put

    def cols_to(dc):
        packed = lasts if dc > 0 else firsts
        quarter = rows // 4
        parts = [roll(packed, 4 * SUB * i)[quarter * i : quarter * (i + 1)] for i in range(4)]
        packed = parts[0] + parts[1] + parts[2] + parts[3]

        def put(dst):
            payload[dst, at : at + quarter] = packed

        return put

    def corner_to(dr, dc):
        packed = lasts if dc > 0 else firsts

        def put(dst):
            payload[dst, at : at + H] = packed[rows - H :] if dr > 0 else packed[:H]

        return put

    for dr in (-1, 1):
        send(dr, 0, rows_to(dr))
        send(0, dr, cols_to(dr))
        for dc in (-1, 1):
            send(dr, dc, corner_to(dr, dc))


def toeplitz(gens, late):
    lane = iota((SUB, LANES), 1)
    low = (lane & SUB) == 0
    slid = [slide(wide(gens[k : k + 1])) for k in range(4)]
    re, im = slid[0:2], slid[2:4]
    bases = [
        [jnp.where(low, re[half], -roll(im[half], SUB)) for half in range(2)],
        [jnp.where(low, im[half], roll(re[half], SUB)) for half in range(2)],
    ]
    out = []
    for a1 in range(Q // SUB):
        for first, second in bases:
            tile = jnp.where(lane < LANES - 2 * SUB * a1, first, second)
            out.append(tile if late else roll(tile, 2 * SUB * a1))
    return out


def slide(row):
    return pltpu.roll(row, LANES - SUB, 1, stride=1, stride_axis=0)


TILES = 2 * Q // SUB


def diagonal(k):
    return iota((SUB, LANES), 1) == SUB * k + iota((SUB, LANES), 0)


def to_columns(row):
    return [jnp.sum(jnp.where(diagonal(k), row, 0.0), axis=1, keepdims=True) for k in range(TILES)]


def wide(row):
    return jnp.broadcast_to(row, (SUB, LANES))


def tree_sum(parts):
    while len(parts) > 1:
        parts = [sum(parts[i : i + 2]) for i in range(0, len(parts), 2)]
    return parts[0]


def packed_times(wr, wi, row):
    low = (iota((SUB, LANES), 1) & SUB) == 0
    turned = jnp.where(low, -roll(row, -SUB), roll(row, SUB))
    return wr * row + wi * turned


def column_times(weights, columns, f):
    out = []
    for a1 in range(Q // SUB):
        at = slice(SUB * a1, SUB * (a1 + 1))
        out += times((weights[2 * f, at], weights[2 * f + 1, at]), (columns[2 * a1], columns[2 * a1 + 1]))
    return out


def shares_of(row):
    low = (iota((SUB, LANES), 1) & SUB) == 0
    row = wide(row)
    return jnp.where(low, row, roll(row, SUB)), jnp.where(low, roll(row, -SUB), row)


def row_step(maps, feeds, shares, weights, carry, spread, put, late):
    out = []
    for f in range(F):
        full = feeds[f] if carry is None else carry[f] + feeds[f]
        full = [jnp.where(diagonal(k), full, 0.0) for k in range(TILES)]
        if carry is None:
            put(f, jnp.zeros((SUB, LANES), f32))
        else:
            amp = spread * packed_times(weights[2 * f], weights[2 * f + 1], carry[f])
            put(f, amp)
            turns = [roll(amp, -2 * SUB * a1) if late else amp for a1 in range(Q // SUB)]
            full = [part - tile * turns[k // 2] for k, (part, tile) in enumerate(zip(full, maps(f), strict=True))]
        share = [jnp.sum(jnp.where(diagonal(k), shares[f], 0.0), axis=1, keepdims=True) for k in range(0, TILES, 2)]
        out.append([share[k // 2] * jnp.sum(full[k], axis=1, keepdims=True) for k in range(TILES)])
    return out


def column_step(maps, feeds, shares, columns, carry, spread, put, late):
    out = []
    for f in range(F):
        amp = [spread * part for part in column_times(columns, carry[f], f)]
        put(f, amp)
        tiles = maps(f)
        pairs = [tiles[k] * amp[k] + tiles[k + 1] * amp[k + 1] for k in range(0, TILES, 2)]
        parts = [roll(pair, 2 * SUB * a1) if late else pair for a1, pair in enumerate(pairs)]
        kept = [jnp.where(diagonal(k), carry[f][k], 0.0) for k in range(TILES)]
        total = wide(jnp.sum(tree_sum(kept) - tree_sum(parts), axis=0, keepdims=True))
        out.append(shares[f] * (total + feeds[f]))
    return out


def sweep(n_r, maps, feeds, share, weights, columns, spread, put, late):
    rows = [wide(weights[k : k + 1]) for k in range(2 * F)]

    def pair(j, carry):
        between = row_step(
            lambda f: maps(j, f), feeds(j), shares_of(share(j)), rows, carry, spread, lambda f, v: put(j, f, v),
            late,
        )
        return column_step(
            lambda f: maps(j + 1, f), feeds(j + 1), shares_of(share(j + 1)), columns, between, spread,
            lambda f, v: put(j + 1, f, v), late,
        )

    carry = None
    pairs = (n_r - 1) // 2
    if pairs > 0:
        carry = pair(0, carry)
    if n_r <= SUB:
        for i in range(1, pairs):
            carry = pair(2 * i, carry)
    else:
        carry = lax.fori_loop(1, pairs, lambda i, now: tuple(pair(2 * i, now)), tuple(carry))
    if (n_r - 1) % 2:
        j = n_r - 2
        last = row_step(
            lambda f: maps(j, f), feeds(j), shares_of(share(j)), rows, carry, spread, lambda f, v: put(j, f, v),
            late,
        )
        for f in range(F):
            put(n_r - 1, f, [spread * part for part in column_times(columns, last[f], f)])
    elif carry is not None:
        for f in range(F):
            put(n_r - 1, f, spread * packed_times(rows[2 * f], rows[2 * f + 1], carry[f]))


def putter(amps, held):
    def put(j, f, value):
        if isinstance(value, list):
            put_columns(amps, j, f, value)
        else:
            held[j // 2, f] = value

    return put


def put_columns(amps, j, f, columns):
    for k, column in enumerate(columns):
        amps[j, f, SUB * k : SUB * (k + 1)] = jnp.broadcast_to(column, (SUB, LANES))


def take_rows(amps, held, j):
    for f in range(F):
        put_columns(amps, j, f, to_columns(held[j // 2, f]))


def laps(n, body, few):
    if n <= few:
        for j in range(n):
            body(j)
    else:
        lax.fori_loop(0, n, lambda j, _: (body(j), 0)[1], 0)


def gens_sum(recv, j, n_c, d, c, step, own):
    total = None
    for k in range(n_c):
        part = recv[j * n_c + k, 0:SUB]
        part = jnp.where((j == d + step) & (k == c), own, part)
        total = part if total is None else total + part
    return total


def powers(base, count):
    out = [None, base]
    for _ in range(2, count):
        out.append(times(out[-1], base))
    return out


MERGED = 5


def merged(middle, side):
    sub = iota((SUB, LANES), 0)
    return [
        jnp.where(sub < H, roll(side[0:SUB], H, 0), middle[0:SUB]),
        middle[SUB : 2 * SUB],
        middle[2 * SUB : 3 * SUB],
        jnp.where(sub >= SUB - H, roll(side[3 * SUB :], -H, 0), middle[3 * SUB :]),
        side[SUB : 2 * SUB] + roll(side[2 * SUB : 3 * SUB], LANES // 2),
    ]


def apart(tiles):
    return [roll(tiles[0], -H, 0), tiles[4], roll(tiles[4], LANES // 2), roll(tiles[3], H, 0)]


def merged_places(rows):
    d, c = place_of()
    sub = iota((SUB, LANES), 0)
    lane = iota((SUB, LANES), 1)
    x0 = d * rows + sub
    y0 = c * LANES + lane
    side = y0 + jnp.where(lane < LANES // 2, LANES, -LANES)
    turned = (lane + LANES // 2) & (LANES - 1)
    side_turned = c * LANES + turned + jnp.where(turned < LANES // 2, LANES, -LANES)
    second = (lane >= LANES // 4) & (lane < 3 * LANES // 4)
    return [
        (jnp.where(sub < H, x0 - H, x0 - SUB), jnp.where(sub < H, side, y0)),
        (x0, y0),
        (x0 + SUB, y0),
        (jnp.where(sub >= SUB - H, x0 + rows - (SUB - H), x0 + rows), jnp.where(sub >= SUB - H, side, y0)),
        (jnp.where(second, x0 + SUB, x0), jnp.where(second, side_turned, side)),
    ]


def store_waves(
    fields, cols_a, cols_b, above, below, loss, first, second, carriers, back_first, back_carriers, back_plain, inner, edge_l, edge_r
):
    rows = fields.shape[1]
    ks = range(2 * F, N_FIELDS)
    sides = with_halo(ks, fields, cols_a, cols_b, above, below, inner, edge_l, edge_r)
    tiles = [merged(inner[i], side) for i, side in enumerate(sides)]
    for k in range(2 * F):
        for t in range(MERGED):
            loss[t, k] = tiles[1 + k][t]

    def keep(out, t, values):
        for k, value in enumerate(values):
            for part in range(2):
                out[t, k, part] = value[part]

    for t, (x, y) in enumerate(merged_places(rows)):
        h = tiles[0][t]
        keep(first, t, powers(wave(1, x, 0, y, 0.24, h), Q // SUB)[1:])
        odd = [cos_sin((y & (2 * PERIOD - 1)).astype(f32) * (0.5 / PERIOD) + (0.015 / TURN) * h)]
        whole = square(odd[0])
        for _ in range(SUB // 2 - 1):
            odd.append(times(odd[-1], whole))
        keep(second, t, odd)
        keep(carriers, t, [times(carrier(f, 0, x, y, h), odd[-1]) for f in range(F)])
        if t in (1, 2):
            keep(back_first, t - 1, powers(wave(-1, x, 0, y, 0.24, h), Q // SUB)[1:])
            plain = [carrier(f, 1, x, y, h) for f in range(F)]
            keep(back_plain, t - 1, plain)
            keep(back_carriers, t - 1, [times(part, odd[-1]) for part in plain])


def radiated(amps, at, f, first, second, carriers, tiles, shift):
    splat = lambda a: wide(amps[at, f, a : a + 1])
    totals = [None] * len(tiles)
    for a1 in range(Q // SUB):
        base = 2 * SUB * a1
        pairs = []
        for i in range(SUB // 2):
            up, low = SUB // 2 + i, SUB // 2 - 1 - i
            re = splat(base + up), splat(base + low)
            im = splat(base + SUB + up), splat(base + SUB + low)
            pairs.append((re[0] + re[1], re[0] - re[1], im[0] + im[1], im[0] - im[1]))
        for n, t in enumerate(tiles):
            inner = None
            for i, (re_sum, re_gap, im_sum, im_gap) in enumerate(pairs):
                cos, sin = second[t + shift, i, 0], second[t + shift, i, 1]
                got = (re_sum * cos - im_gap * sin, im_sum * cos + re_gap * sin)
                inner = got if inner is None else (inner[0] + got[0], inner[1] + got[1])
            if a1 > 0:
                got = times((first[t, a1 - 1, 0], first[t, a1 - 1, 1]), inner)
                inner = (totals[n][0] + got[0], totals[n][1] + got[1])
            totals[n] = inner
    return [times((carriers[t, f, 0], carriers[t, f, 1]), total) for t, total in zip(tiles, totals, strict=True)]


def new_body(
    n_r, n_c, spread, recv, green, edge_green, source, fields, cols_b, cols_a, rows_b, rows_a, tables, weights, columns,
    forward, driven, payload, second, back_first, back_carriers, below_gens,
    loss, first, carriers, back_plain, amps, kept, held, inner, moved, edge_l, edge_r, spill, cs, left_mat, right_mat, common, halo,
):
    rows = fields.shape[1]
    d, c = place_of()
    above_rows, below_rows = halo_rows(rows_a, rows_b)
    above = above_rows[GENS_AT:]
    below_gens[...] = below_rows[GENS_AT:]
    store_waves(
        fields, cols_a, cols_b, above_rows, below_rows,
        loss, first, second, carriers, back_first, back_carriers, back_plain, held, edge_l, edge_r,
    )

    if n_r <= SUB:
        sums = [gens_sum(recv, j, n_c, d, c, -1, above) for j in range(n_r - 1)]

    def maps(j, f):
        gens = sums[j] if n_r <= SUB else gens_sum(recv, j, n_c, d, c, -1, above)
        return toeplitz(gens[4 * f : 4 * f + 4], False)

    def feeds(j):
        feed = recv[j * n_c, SUB : 2 * SUB]
        for k in range(1, n_c):
            feed = feed + recv[j * n_c + k, SUB : 2 * SUB]
        return [wide(feed[f : f + 1]) for f in range(F)]

    sweep(n_r, maps, feeds, lambda j: recv[j * n_c, SUB + 2 : SUB + 3], weights, columns, spread, putter(amps, kept), False)
    even = d - (d & 1)
    take_rows(amps, kept, even)
    take_rows(amps, kept, jnp.minimum(even + 2 * (d & 1), n_r - 1 - ((n_r - 1) & 1)))

    at = HALO_AT

    def got(dr, dc, start, size):
        src = jnp.clip(d + dr, 0, n_r - 1) * n_c + jnp.clip(c + dc, 0, n_c - 1)
        ok = (d + dr >= 0) & (d + dr < n_r) & (c + dc >= 0) & (c + dc < n_c)
        return jnp.where(ok, recv[src, start : start + size], 0.0)

    edge_l[...] = jnp.zeros(edge_l.shape, f32)
    edge_r[...] = jnp.zeros(edge_r.shape, f32)
    quarter = rows // 4
    for edge, dc in ((edge_l, -1), (edge_r, 1)):
        side = got(0, dc, at, quarter)
        for i in range(4):
            edge[TOP + quarter * i : TOP + quarter * (i + 1)] = roll(side, -4 * SUB * i)
        edge[TOP - H : TOP] = got(-1, dc, at, H)
        edge[TOP + rows : TOP + rows + H] = got(1, dc, at, H)
    from_left, from_right = edge_l[...], edge_r[...]
    for i, dr in enumerate((-1, 1)):
        halo[i, 0:SUB] = got(dr, 0, 0, SUB)
        halo[i, SUB : 2 * F * H] = got(dr, 0, at, 2 * F * H - SUB)
    for k in range(2 * F):
        inner[k] = jnp.zeros(inner.shape[1:], f32)
        inner[k, TOP : TOP + rows] = source[k]
        inner[k, TOP - H : TOP] = halo[0, H * k : H * (k + 1)]
        inner[k, TOP + rows : TOP + rows + H] = halo[1, H * k : H * (k + 1)]
    sides = [unpack_columns(from_left, from_right, k) for k in range(2 * F)]

    weak = {}
    lost = {}
    for step, group in ((-1, (0,)), (0, (1, 2, 4)), (1, (3,))):
        at = jnp.clip(d + step, 0, n_r - 1)
        for f in range(F):
            for t, w in zip(group, radiated(amps, at, f, first, second, carriers, group, 0), strict=True):
                got = times((loss[t, 2 * f], loss[t, 2 * f + 1]), w)
                for part in range(2):
                    weak[t, 2 * f + part] = w[part]
                    lost[t, 2 * f + part] = got[part]
    beyond = []
    for k in range(2 * F):
        tiles = [lost[t, k] for t in range(MERGED)]
        side = sides[k] - jnp.concatenate(apart(tiles), axis=0)
        middle = inner[k] - jnp.concatenate(tiles[:4], axis=0)
        forward[k] = middle[TOP : TOP + rows]
        for i in range(SHIFTS):
            moved[k * SHIFTS + i, 0:TOP] = jnp.zeros((TOP, LANES), f32)
            moved[k * SHIFTS + i, TOP + rows :] = jnp.zeros((TOP, LANES), f32)
        store_shifted(moved, k, middle[TOP : TOP + rows], side[TOP : TOP + rows])
        above_edge = range(TOP - 1, TOP - 1 - H, -1)
        below_edge = range(TOP + rows, TOP + rows + H)
        pairs = [pair_rows(row_list(part, above_edge), row_list(part, below_edge), True) for part in (middle, side)]
        beyond.append([shifted(*pairs, dy) for dy in range(-H, H + 1)])
    near = [jnp.zeros((2 * SUB, LANES), f32) for _ in range(2 * F)]
    for dy in range(-H, H + 1):
        add_near(near, [edge_green[4 * (dy + H) + k] for k in range(2 * F)], lambda k: beyond[k][dy + H])
    for k in range(2 * F):
        put_pairs(near[k], spill, k)
    near = [spill[k] for k in range(2 * F)]
    for code in range(OFFSETS):
        dx, dy = offset_of(code)
        add_near(
            near,
            [green[4 * code + k] for k in range(2 * F)],
            lambda k: moved[k * SHIFTS + dy + H, TOP + dx : TOP + dx + rows],
        )
    for f in range(F):
        rest = []
        for part in range(2):
            k = 2 * f + part
            w = jnp.concatenate([weak[1, k], weak[2, k]], axis=0)
            rest.append(fields[N_FIELDS + k] - near[k] - w)
        s = times((fields[2 * F + 1 + 2 * f], fields[2 * F + 2 + 2 * f]), rest)
        driven[2 * f] = s[0]
        driven[2 * f + 1] = s[1]
        base = [jnp.concatenate([back_plain[t, f, part] for t in range(2)], axis=0) for part in range(2)]
        add = conj_times(base, s)
        cs[2 * f] = add[0]
        cs[2 * f + 1] = add[1]

    def keep(f, row):
        common[f : f + 1] = row

    project(left_mat, right_mat, tables, 2, cs, rows, keep)
    pair = common[0:2]

    def fill(s):
        payload[s] = pair

    laps(n_r * n_c, fill, 8 * SUB)


def last_body(
    n_r, n_c, spread, recv, fed, new, driven, fields, weights, columns, first, second, carriers, below_gens,
    forward, currents, amps, kept,
):
    rows = fields.shape[1]
    d, c = place_of()
    forward[...] = new[...]
    below = below_gens[...]

    def feeds(k):
        j = n_r - 1 - k
        feed = fed[j * n_c]
        for i in range(1, n_c):
            feed = feed + fed[j * n_c + i]
        return [wide(feed[f : f + 1]) for f in range(F)]

    def share(k):
        return recv[(n_r - 1 - k) * n_c, SUB + 2 : SUB + 3]

    def maps(k, f):
        return toeplitz(gens_sum(recv, n_r - 1 - k, n_c, d, c, 1, below)[4 * f : 4 * f + 4], True)

    sweep(n_r, maps, feeds, share, weights, columns, spread, putter(amps, kept), True)
    at = n_r - 1 - d
    take_rows(amps, kept, at - (at & 1))
    tiles = tuple(range(rows // SUB))
    for f in range(F):
        for tile, w in zip(tiles, radiated(amps, at, f, first, second, carriers, tiles, 1), strict=True):
            rows_at = slice(SUB * tile, SUB * (tile + 1))
            lost = times((fields[2 * F + 1 + 2 * f, rows_at], fields[2 * F + 2 + 2 * f, rows_at]), w)
            currents[2 * f, rows_at] = driven[2 * f, rows_at] - lost[0]
            currents[2 * f + 1, rows_at] = driven[2 * f + 1, rows_at] - lost[1]


def swaps(n):
    first = [(i, i ^ 1) for i in range(n) if i ^ 1 < n]
    second = [(i, i + 1) for i in range(1, n - 1, 2)] + [(i + 1, i) for i in range(1, n - 1, 2)]
    return first, second


def swap(axis, n, a, b):
    first, second = swaps(n)
    b = lax.ppermute(b, axis, second)
    return lax.ppermute(a, axis, first), b


def stacked(arrays):
    rows, cols = arrays[0].shape[1:]
    total = sum(array.shape[0] for array in arrays)
    out, at = None, 0
    for array in arrays:
        count = array.shape[0]
        wide_array = jnp.pad(
            array, ((at, total - at - count), (0, rows - array.shape[1]), (0, cols - array.shape[2]))
        )
        out = wide_array if out is None else out + wide_array
        at += count
    return out


def per_device(n_r, n_c, incident, inverse_diag, previous, heights, neighbours, counts, transmit, angle_weights):
    rows, cols = heights.shape
    patches = rows * cols
    spread = 1.0 / math.sqrt(rows * cols * n_c)
    slots = n_r * n_c
    tall = rows + 2 * SUB
    fields = stacked([previous, heights[None], inverse_diag, incident, angle_weights, transmit])
    cols_b, cols_a = call(columns_body, [(rows, LANES)] * 2, [VMEM], flops=400_000_000)(fields)
    cols_a, cols_b = swap("xr", n_c, cols_a, cols_b)
    tables, gens = call(
        functools.partial(tables_body, n_r),
        [(6, rows, SUB, LANES), (2 * SUB, LANES)],
        [VMEM],
        [pltpu.VMEM((16 * SUB, patches), f32), pltpu.VMEM((4 * SUB, patches), f32)],
    )(fields)
    weights, share, columns = call(
        params_body, [(2 * F, LANES), (1, LANES), (2 * F, Q, LANES)], [VMEM], flops=400_000_000
    )(fields)
    gens, weights, share, columns = lax.optimization_barrier((gens, weights, share, columns))
    rows_b, rows_a = call(rows_body, [(ROWS_SENT, LANES)] * 2, [VMEM] * 4, flops=400_000_000)(fields, gens, cols_b, cols_a)
    rows_a, rows_b = swap("rng", n_r, rows_a, rows_b)
    green, inner_near, bits = call(
        inner_body,
        [
            (4 * OFFSETS, rows, LANES),
            (2 * F, rows, LANES),
            jax.ShapeDtypeStruct((2, rows, LANES), jnp.int32),
        ],
        [VMEM] * 5,
        [pltpu.VMEM(((2 * F + 1) * SHIFTS, tall, LANES), f32)],
        400_000_000,
    )(fields, neighbours, counts, cols_b, cols_a)
    edges = [pltpu.VMEM((tall, LANES), f32)] * 2
    payload, edge_green, source = call(
        functools.partial(near_body, n_r, n_c),
        [(slots, SLOT, LANES), (4 * SHIFTS, 2 * SUB, LANES), (2 * F, rows, LANES)],
        [VMEM] * 10,
        [
            pltpu.VMEM((2 * F, rows, LANES), f32),
            pltpu.VMEM((2 * F, rows, LANES), f32),
            pltpu.VMEM((4 * SUB, patches), f32),
            pltpu.VMEM((2 * SUB, patches), f32),
            pltpu.VMEM((3 * SUB, LANES), f32),
            pltpu.VMEM((2 * SUB, LANES), f32),
        ],
    )(fields, bits, inner_near, share, cols_b, cols_a, rows_b, rows_a, gens, tables)
    recv = lax.all_to_all(payload, BOTH, 0, 0)
    tile = (2, SUB, LANES)
    new, driven, payload, second, back_first, back_carriers, below_gens = call(
        functools.partial(new_body, n_r, n_c, spread),
        [
            (2 * F, rows, LANES),
            (2 * F, rows, LANES),
            (slots, 2, LANES),
            (MERGED, SUB // 2, *tile),
            (2, Q // SUB - 1, *tile),
            (2, F, *tile),
            (SUB, LANES),
        ],
        [VMEM] * 12,
        [
            pltpu.VMEM((MERGED, 2 * F, SUB, LANES), f32),
            pltpu.VMEM((MERGED, Q // SUB - 1, *tile), f32),
            pltpu.VMEM((MERGED, F, *tile), f32),
            pltpu.VMEM((2, F, *tile), f32),
            pltpu.VMEM((n_r, F, 2 * Q, LANES), f32),
            pltpu.VMEM(((n_r + 1) // 2, F, SUB, LANES), f32),
            pltpu.VMEM((2 * F + 1, tall, LANES), f32),
            pltpu.VMEM((2 * F, tall, LANES), f32),
            pltpu.VMEM((2 * F * (2 * H + 1), tall, LANES), f32),
            *edges,
            pltpu.VMEM((2 * F, rows, LANES), f32),
            pltpu.VMEM((2 * F, rows, LANES), f32),
            pltpu.VMEM((4 * SUB, patches), f32),
            pltpu.VMEM((2 * SUB, patches), f32),
            pltpu.VMEM((SUB, LANES), f32),
            pltpu.VMEM((2, 2 * SUB, LANES), f32),
        ],
    )(recv, green, edge_green, source, fields, cols_b, cols_a, rows_b, rows_a, tables, weights, columns)
    fed = lax.all_to_all(payload, BOTH, 0, 0)
    return call(
        functools.partial(last_body, n_r, n_c, spread),
        [(2 * F, rows, LANES), (2 * F, rows, LANES)],
        [VMEM] * 11,
        [pltpu.VMEM((n_r, F, 2 * Q, LANES), f32), pltpu.VMEM(((n_r + 1) // 2, F, SUB, LANES), f32)],
    )(recv, fed, new, driven, fields, weights, columns, back_first, second, back_carriers, below_gens)


def solution(mesh):
    body = functools.partial(per_device, mesh.shape["rng"], mesh.shape["xr"])
    field = P(None, "rng", "xr")
    return jax.shard_map(
        body,
        mesh=mesh,
        in_specs=(field, field, field, P("rng", "xr"), field, P("rng", "xr"), P("rng", None, None), P()),
        out_specs=(field, field),
        check_vma=False,
    )
```
